32 devices in a mesh: rows: 4 (over z), seq: 8 (over y, x, core).
Axes of the slice: x: 2, y: 2, z: 4, core: 2. Of those that a mesh axis runs over, the one named last changes fastest.
Arguments:
- tokens: bfloat16 [4, 2048, 512], P('rows', 'seq'), may hold values from -6 to 6
- norm_attn: bfloat16 [512], replicated, may hold values from 0.099609375 to 1.8984375
- query_weight: bfloat16 [512, 384], replicated, may hold values from -0.0625 to 0.0625
- key_weight: bfloat16 [512, 384], replicated, may hold values from -0.25 to 0.25
- value_weight: bfloat16 [512, 384], replicated, may hold values from -0.25 to 0.25
- out_weight: bfloat16 [384, 512], replicated, may hold values from -1.25 to 1.25
- bucket_bias_table: bfloat16 [32, 6], replicated, may hold values from -4 to 4
- norm_ffn: bfloat16 [512], replicated, may hold values from 0.099609375 to 1.8984375
- gate_weight: bfloat16 [512, 1024], replicated, may hold values from -0.25 to 0.25
- expansion_matrix: bfloat16 [512, 1024], replicated, may hold values from -0.25 to 0.25
- down_weight: bfloat16 [1024, 512], replicated, may hold values from -0.25 to 0.25
- lengths: int32 [4, 16], P('rows'), may hold values from 0 to 2048, as said below
- cotangent: bfloat16 [4, 2048, 512], P('rows', 'seq'), may hold values from -6 to 6
Outputs:
- output: bfloat16 [4, 2048, 512], P('rows', 'seq')
- grad_tokens: float32 [4, 2048, 512], P('rows', 'seq')
- grad_norm_attn: float32 [512], replicated
- grad_query_weight: float32 [512, 384], replicated
- key_weight_gradient: float32 [512, 384], replicated
- grad_value_weight: float32 [512, 384], replicated
- grad_out_weight: float32 [384, 512], replicated
- grad_bias_table: float32 [32, 6], replicated
- grad_norm_ffn: float32 [512], replicated
- grad_gate_weight: float32 [512, 1024], replicated
- grad_up_weight: float32 [512, 1024], replicated
- grad_down_weight: float32 [1024, 512], replicated
The draws below stay inside these ranges and needn't reach their ends.
Inputs may be any that keep to these rules, and one draw needn't show every extreme that they name: Each row's lengths sum to at most 2048; bytes past the sum are padding. In every draw some row is one segment of 2048 bytes.
All inputs are finite; a program needn't handle non-finite values.
Results may differ from the reference program's by a relative error of at most 0.03.
Values may be sent and summed in bfloat16 or wider, within the bound.
No kernel may reach another device: no remote copies, remote signals or barrier semaphores. Data moves between devices by JAX's collectives and lax.ppermute only.
A program may use at most 128 MiB of HBM per device.

```python
import math
import jax
import jax.numpy as jnp
from jax import lax

D = 512
FF = 1024
H = 6
DK = 64
BUCKETS = 32
MAXDIST = 128
SEGS = 16
BLOCK = 256
ROWS_DEV = 1
ROWS = 4
ROW_LEN = 2048
N_ROWS = 4


def split_region(region_key, region_len, slot_count, live_count):
    cut_points = jnp.sort(jax.random.randint(region_key, (slot_count - 1,), 0, region_len + 1))
    places = jnp.arange(1, slot_count, dtype=jnp.int32)
    cut_points = jnp.where(places >= live_count, region_len, cut_points)
    bounds = jnp.concatenate([jnp.zeros((1,), jnp.int32), cut_points.astype(jnp.int32), jnp.reshape(region_len, (1,)).astype(jnp.int32)])
    return bounds[1:] - bounds[:-1]


def draw_lengths(key, part):
    key = jax.random.fold_in(key, 7)
    main_keys = jax.random.split(key, 3)
    chosen = jax.random.randint(main_keys[0], (N_ROWS,), 0, ROWS_DEV)
    spanning = jnp.arange(ROWS) % ROWS_DEV == jnp.repeat(chosen, ROWS_DEV)

    def one_row(row_key):
        sub_keys = jax.random.split(row_key, 7)
        pad_len = jax.random.randint(sub_keys[0], (), 0, BLOCK // 4)
        used_len = ROW_LEN - pad_len
        live_ragged = jax.random.randint(sub_keys[1], (), 2, SEGS)
        uneven_lengths_flag = split_region(sub_keys[2], used_len, SEGS, live_ragged)
        head_len = jax.random.randint(sub_keys[3], (), 0, BLOCK // 2)
        tail_len = jax.random.randint(sub_keys[4], (), 0, BLOCK // 4)
        live_tail = jax.random.randint(sub_keys[5], (), 1, SEGS - 2)
        tail_parts = split_region(sub_keys[6], tail_len, SEGS - 2, live_tail)
        span_len = used_len - head_len - tail_len
        spanned = jnp.concatenate([jnp.stack([head_len, span_len]).astype(jnp.int32), tail_parts])
        return (uneven_lengths_flag, spanned)
    uneven_lengths_flag, spanned = jax.vmap(one_row)(jax.random.split(main_keys[1], ROWS))
    drawn = jnp.where(spanning[:, None], spanned, uneven_lengths_flag).astype(jnp.int32)
    full_index = jax.random.randint(main_keys[2], (), 0, ROWS)
    full_row = (jnp.arange(SEGS, dtype=jnp.int32) == 0).astype(jnp.int32) * ROW_LEN
    is_full = (jnp.arange(ROWS, dtype=jnp.int32) == full_index)[:, None]
    return jnp.where(is_full, full_row[None, :], drawn).astype(jnp.int32)


def level_of(own_key, extent, cuts, least, top_value):
    def one(dim, blocks):
        draws = jax.random.uniform(jax.random.fold_in(jax.random.fold_in(own_key, 6), dim), (blocks,), jnp.float32, least / len(cuts), top_value / len(cuts))
        return jnp.repeat(jnp.exp(draws), extent[dim] // blocks).reshape((-1,) + (1,) * (len(extent) - dim - 1))

    level = one(*cuts[0])
    for cut in cuts[1:]:
        level = level * one(*cut)
    return level


def normal_values(key, shape, width, limit, shards=(), kind=jnp.bfloat16):
    factor_of = level_of(key, shape, shards, -0.22, 0.18) if shards else 1.0
    entries = jax.random.normal(key, shape, jnp.float32) * width * factor_of
    return jnp.minimum(jnp.maximum(entries, -limit), limit).astype(kind)


def setup_inputs(seed: int = 0) -> dict:
    key_of = jax.random.split(jax.random.key(seed), 14)
    tokens = normal_values(key_of[0], (ROWS, ROW_LEN, D), 1.0, 6.0, ((0, 4), (1, 8)))
    norm_attn = jnp.clip(1.0 + 0.18 * jax.random.normal(key_of[1], (D,), jnp.float32), 0.099609375, 1.8984375).astype(jnp.bfloat16)
    query_weight = normal_values(key_of[2], (D, H * DK), (D * DK // 4) ** -0.5, 0.0625)
    key_weight = normal_values(key_of[3], (D, H * DK), D ** -0.5, 0.25)
    value_weight = normal_values(key_of[4], (D, H * DK), D ** -0.5, 0.25)
    out_weight = normal_values(key_of[5], (H * DK, D), (H * DK // 16) ** -0.5, 1.25)
    bucket_bias_table = normal_values(key_of[6], (BUCKETS, H), 1.0, 4.0)
    norm_ffn = jnp.clip(1.0 + 0.18 * jax.random.normal(key_of[7], (D,), jnp.float32), 0.099609375, 1.8984375).astype(jnp.bfloat16)
    gate_weight = normal_values(key_of[8], (D, FF), D ** -0.5, 0.25)
    expansion_matrix = normal_values(key_of[9], (D, FF), D ** -0.5, 0.25)
    down_weight = normal_values(key_of[10], (FF, D), (FF // 2) ** -0.5, 0.25)
    lengths = draw_lengths(jax.random.fold_in(key_of[13], 71), 0)
    cotangent = normal_values(key_of[12], (ROWS, ROW_LEN, D), 1.0, 6.0, ((0, 4), (1, 8)))
    return dict(tokens=tokens, norm_attn=norm_attn, query_weight=query_weight, key_weight=key_weight, value_weight=value_weight, out_weight=out_weight, bucket_bias_table=bucket_bias_table, norm_ffn=norm_ffn, gate_weight=gate_weight, expansion_matrix=expansion_matrix, down_weight=down_weight, lengths=lengths, cotangent=cotangent)


norm_epsilon = 1e-06
masked_score = -1000000000.0

@jax.custom_vjp
def low(v):
    return lax.optimization_barrier(v.astype(jnp.bfloat16)).astype(jnp.float32)

@jax.custom_vjp
def low_back(v):
    return v

def low_keep(v):
    return (low(v), None)

def low_pass(kept, grad):
    return (grad,)

def back_keep(v):
    return (v, None)

def backward_lowered(kept, grad):
    return (low(grad),)
low.defvjp(low_keep, low_pass)
low_back.defvjp(back_keep, backward_lowered)

def bucket_thresholds(bucket_count, max_distance):
    half_count = bucket_count // 2
    exact_count = half_count // 2
    log_range = half_count - exact_count
    thresholds = list(range(1, exact_count))
    for power_step in range(log_range):
        target = exact_count ** (log_range - power_step) * max_distance ** power_step
        candidate = exact_count
        while candidate ** log_range < target:
            candidate += 1
        thresholds.append(candidate)
    return thresholds

def relative_bucket(query_pos, key_pos):
    offsets = key_pos[None, :] - query_pos[:, None]
    distance = jnp.abs(offsets)
    bucket = (offsets > 0).astype(jnp.int32) * (BUCKETS // 2)
    for threshold in bucket_thresholds(BUCKETS, MAXDIST):
        bucket = bucket + (distance >= threshold).astype(jnp.int32)
    return bucket

def rms_norm(values, gain_vec):
    return values * lax.rsqrt(lax.optimization_barrier(jnp.mean(values * values, axis=-1, keepdims=True)) + norm_epsilon) * gain_vec

def project(left_side, right_side):
    return jnp.einsum('rtd,de->rte', left_side, right_side, precision=lax.Precision.HIGHEST)

def block_attention(query_block, query_pos, query_segment, key_heads, value_heads, bucket_bias_table, segment):
    positions = jnp.arange(ROW_LEN, dtype=jnp.int32)
    bucket = relative_bucket(query_pos, positions)
    position_bias_term = jnp.transpose(jnp.take(bucket_bias_table, bucket, axis=0), (2, 0, 1))
    scores = jnp.einsum('qhd,khd->hqk', query_block, key_heads, precision=lax.Precision.HIGHEST) + position_bias_term
    scores = low_back(scores)
    allowed = query_segment[:, None] == segment[None, :]
    scores = jnp.where(allowed[None], scores, masked_score)
    largest = lax.optimization_barrier(jnp.max(scores, axis=-1, keepdims=True))
    raised = jnp.exp(scores - largest)
    weights = low(raised / lax.optimization_barrier(jnp.sum(raised, axis=-1, keepdims=True)))
    return jnp.einsum('hqk,khd->qhd', weights, value_heads, precision=lax.Precision.HIGHEST)

def attend_row(query_low, key_low, value_low, bucket_bias_table, segment):
    positions = jnp.arange(ROW_LEN, dtype=jnp.int32)
    block_len = math.gcd(ROW_LEN, 512)
    block_count = ROW_LEN // block_len
    key_heads = key_low.reshape(ROW_LEN, H, DK)
    value_heads = value_low.reshape(ROW_LEN, H, DK)
    saved_block = jax.checkpoint(block_attention)

    def over_items(item_list):
        return saved_block(item_list[0], item_list[1], item_list[2], key_heads, value_heads, bucket_bias_table, segment)
    mixed_out = lax.map(over_items, (query_low.reshape(block_count, block_len, H, DK), positions.reshape(block_count, block_len), segment.reshape(block_count, block_len)))
    return mixed_out.reshape(ROW_LEN, H * DK)

def forward(tokens, norm_attn, query_weight, key_weight, value_weight, out_weight, bucket_bias_table, norm_ffn, gate_weight, expansion_matrix, down_weight, segments):
    normed_one = low(rms_norm(tokens, norm_attn))
    query_low = low(low_back(project(normed_one, query_weight)))
    key_low = low(low_back(project(normed_one, key_weight)))
    value_low = low(low_back(project(normed_one, value_weight)))

    def row_attention(item_list):
        return attend_row(item_list[0], item_list[1], item_list[2], bucket_bias_table, item_list[3])
    mixed_out = lax.map(row_attention, (query_low, key_low, value_low, segments))
    mixed_out = low(low_back(mixed_out))
    hidden = tokens + low_back(project(mixed_out, out_weight))
    normed_two = low(rms_norm(hidden, norm_ffn))
    gate_val = low_back(project(normed_two, gate_weight))
    up_val = low_back(project(normed_two, expansion_matrix))
    inner_low = low(low_back(jax.nn.gelu(gate_val, approximate=True) * up_val))
    return hidden + low_back(project(inner_low, down_weight))

def reference(tokens, norm_attn, query_weight, key_weight, value_weight, out_weight, bucket_bias_table, norm_ffn, gate_weight, expansion_matrix, down_weight, lengths, cotangent):
    segment_ends = jnp.cumsum(lengths, axis=1).astype(jnp.int32)
    positions = jnp.arange(ROW_LEN, dtype=jnp.int32)
    segments = lax.optimization_barrier(jnp.sum((positions[None, :, None] >= segment_ends[:, None, :]).astype(jnp.int32), axis=2)).astype(jnp.int32)
    valid_mask = (positions[None, :] < segment_ends[:, -1:]).astype(jnp.float32)
    floats = tuple((argument.astype(jnp.float32) for argument in (tokens, norm_attn, query_weight, key_weight, value_weight, out_weight, bucket_bias_table, norm_ffn, gate_weight, expansion_matrix, down_weight)))

    def closed(*params_list):
        return forward(*params_list, segments)
    output, pullback = jax.vjp(closed, *floats)
    gradients = pullback(cotangent.astype(jnp.float32) * valid_mask[:, :, None])
    return (output.astype(jnp.bfloat16), gradients[0], gradients[1], gradients[2], gradients[3], gradients[4], gradients[5], gradients[6], gradients[7], gradients[8], gradients[9], gradients[10])
```

```python
from functools import partial

import jax
import jax.numpy as jnp
from jax import lax
from jax.experimental import pallas as pl
from jax.experimental.pallas import tpu as pltpu
from jax.sharding import PartitionSpec as P

EPS = 1e-6
BIG = -(2.0**30)
LEFT, RIGHT, ONES = 17, 18, 19
SMALL = 16
VMEM = 56 * 1024 * 1024

f32, bf16, i32 = jnp.float32, jnp.bfloat16, jnp.int32


def thresholds(buckets, max_distance):
    half = buckets // 2
    exact = half // 2
    steps = half - exact
    out = list(range(1, exact))
    for j in range(steps):
        target = exact ** (steps - j) * max_distance**j
        m = exact
        while m**steps < target:
            m += 1
        out.append(m)
    return out


def bucket_of(offset, buckets):
    distance = jnp.abs(offset)
    bucket = (offset > 0).astype(i32) * (buckets // 2)
    for t in thresholds(buckets, 128):
        bucket = bucket + (distance >= t).astype(i32)
    return bucket


def nn(a, b):
    return lax.dot_general(a, b, (((1,), (0,)), ((), ())), preferred_element_type=f32)


def nt(a, b):
    return lax.dot_general(a, b, (((1,), (1,)), ((), ())), preferred_element_type=f32)


def tn(a, b):
    return lax.dot_general(a, b, (((0,), (0,)), ((), ())), preferred_element_type=f32)


def iota(shape, dim):
    return lax.broadcasted_iota(i32, shape, dim)


def rms(values, gain):
    scale = lax.rsqrt(jnp.mean(values * values, axis=-1, keepdims=True) + EPS)
    return values * scale * gain


def attention_kernel(n, ids, lens, table, gain, *refs):
    x = refs[:n]
    wq, wkv, n1, kv, e, p, o, q, s, bias, qe = refs[n:]
    step = pl.program_id(0)
    me = ids[0]
    t = x[0].shape[0]
    buckets = table.shape[0]

    @pl.when(step == 0)
    def _():
        lane = iota((1, 128), 1)
        low = jnp.full((1, 128), 2**30, i32)
        high = jnp.full((1, 128), -1, i32)
        low = jnp.where(lane == 0, -1, low)
        total = 0
        for k in range(lens.shape[0]):
            total = total + lens[k]
            high = jnp.where(lane == k, total, high)
            low = jnp.where(lane == k + 1, total, low)
        high = jnp.where(lane == lens.shape[0], 2**30, high)
        row = iota((t, 128), 0)
        lanes = iota((t, 128), 1)
        for j in range(n):
            n1[j] = rms(x[j][...].astype(f32), gain[...]).astype(bf16)
            pos = row + (me ^ j) * t
            away = (me ^ j) - me
            flag = jnp.where(away <= -2, LEFT, jnp.where(away >= 2, RIGHT, ONES))
            here = ((pos >= low) & (pos < high)) | (lanes == flag) | (lanes == ONES)
            e[j] = here.astype(f32).astype(bf16)
        other = (e[0][...].astype(f32) - 1.0) * -BIG
        qe[...] = jnp.where(lanes < LEFT, other, 0.0)

    q2 = nn(n1[0], wq[...]).astype(bf16)
    q[...] = q2
    for j in range(n):
        kv2 = nn(n1[j], wkv[...]).astype(bf16)
        kv[0, j] = kv2[:, :128]
        kv[1, j] = kv2[:, 128:]
    lanes = iota((t, 128), 1)
    for hh in range(2):
        h = 2 * step + hh
        far_left = table[buckets // 2 - 1, h]
        far_right = table[buckets - 1, h]
        ext = jnp.where(lanes == LEFT, far_left, jnp.where(lanes == RIGHT, far_right, qe[...]))
        qa = jnp.concatenate([q2[:, hh * 128 : hh * 128 + 128], ext.astype(bf16)], axis=1)
        for j in range(n):
            s[j] = nt(qa, jnp.concatenate([kv[hh, j], e[j]], axis=1))
        u = iota((1, 4 * t), 1)
        bucket = bucket_of(jnp.where(u < 3 * t, u - t, u - 5 * t), buckets)
        line = jnp.zeros((1, 4 * t), f32)
        for b in range(buckets):
            line = jnp.where(bucket == b, table[b, h], line)
        band = pltpu.roll(jnp.broadcast_to(line, (t, 4 * t)), 0, 1, stride=1, stride_axis=0)
        for r in range(3):
            bias[r] = band[:, r * t : (r + 1) * t]
        bias[3] = jnp.zeros((t, t), f32)
        for r in (-1, 0, 1):
            there = me + r
            inside = (there >= 0) & (there < n)
            slot = jnp.where(inside, me ^ there, 0)
            s[slot] = s[slot] + bias[jnp.where(inside, r + 1, 3)]
        top = jnp.maximum(s[0][:, :128], s[0][:, 128:])
        for j in range(1, n):
            top = jnp.maximum(top, jnp.maximum(s[j][:, :128], s[j][:, 128:]))
        top = jnp.max(top, axis=1, keepdims=True)
        acc = jnp.zeros((t, 256), f32)
        for j in range(n):
            raised = jnp.exp(s[j] - top).astype(bf16)
            p[hh, j] = raised
            acc = acc + nn(raised, jnp.concatenate([kv[hh, j], e[j]], axis=1))
        inverse = 1.0 / acc[:, 128 + ONES : 129 + ONES]
        o[:, hh * 128 : hh * 128 + 128] = jnp.where(lanes < 64, inverse, acc[:, :128] * inverse)


def attention_forward(ids, lens, table, gain, blocks, wq, wkv):
    n = len(blocks)
    t, d = blocks[0].shape
    heads = wq.shape[1] // 128
    smem = pl.BlockSpec(memory_space=pltpu.SMEM)
    const = lambda *shape: pl.BlockSpec(shape, lambda i: (0,) * len(shape), pipeline_mode=pl.Buffered(1))
    keep = lambda *shape: pl.BlockSpec(shape, lambda i: (0,) * len(shape))
    pair = lambda rows: pl.BlockSpec((rows, 256), lambda i: (0, i))
    by_head = lambda *shape: pl.BlockSpec((2, n, *shape), lambda i: (i, 0, 0, 0))
    shape = jax.ShapeDtypeStruct
    return pl.pallas_call(
        partial(attention_kernel, n),
        grid=(heads // 2,),
        in_specs=[smem, smem, smem, const(1, d)] + [const(t, d)] * n + [pair(d), pair(d)],
        out_specs=[keep(n, t, d), by_head(t, 128), keep(n, t, 128), by_head(t, t), pair(t), pair(t)],
        out_shape=[
            shape((n, t, d), bf16),
            shape((heads, n, t, 128), bf16),
            shape((n, t, 128), bf16),
            shape((heads, n, t, t), bf16),
            shape((t, heads * 128), f32),
            shape((t, heads * 128), bf16),
        ],
        scratch_shapes=[
            pltpu.VMEM((n, t, t), f32),
            pltpu.VMEM((4, t, t), f32),
            pltpu.VMEM((t, 128), f32),
        ],
        compiler_params=pltpu.CompilerParams(vmem_limit_bytes=VMEM),
        name="attention_forward",
    )(ids, lens, table, gain, *blocks, wq, wkv)


def feed_forward_kernel(ids, lens, gain, x, o, wo, wg, wu, wd, cot, out, dh, dop, delta, gwo, keep, send, gn, grads):
    t, d = x.shape
    ff = wg.shape[1]
    heads = o.shape[1] // 128
    mixed = o[...].astype(bf16)
    h1 = x[...].astype(f32) + nn(mixed, wo[...])
    g2 = gain[...]
    s2 = lax.rsqrt(jnp.mean(h1 * h1, axis=-1, keepdims=True) + EPS)
    hat = h1 * s2
    n2 = (hat * g2).astype(bf16)
    gate = nn(n2, wg[...])
    up = nn(n2, wu[...])
    c0 = 0.7978845608028654
    square = gate * gate
    th = jnp.tanh(c0 * gate * (1.0 + 0.044715 * square))
    half = 0.5 * (1.0 + th)
    act = gate * half
    dact = half + 0.5 * gate * (1.0 - th * th) * (c0 * (1.0 + 3 * 0.044715 * square))
    u = (act * up).astype(bf16)
    out[...] = (h1 + nn(u, wd[...])).astype(bf16)
    total = lens[0]
    for k in range(1, lens.shape[0]):
        total = total + lens[k]
    pos = ids[0] * t + iota((t, 1), 0)
    g = cot[...].astype(f32) * (pos < total).astype(f32)
    gb = g.astype(bf16)
    down = tn(u, gb).astype(bf16)
    grads[2 * d : 3 * d, :d] = down[:d]
    grads[2 * d : 3 * d, d:] = down[d:]
    du = nt(gb, wd[...]).astype(bf16).astype(f32)
    dgate = (du * up * dact).astype(bf16)
    dup = (du * act).astype(bf16)
    grads[0:d] = tn(n2, dgate).astype(bf16)
    grads[d : 2 * d] = tn(n2, dup).astype(bf16)
    rows = keep.shape[0]
    core = ids[0] % 2
    keep[...] = grads[pl.ds(pl.multiple_of(core * rows, 16), rows)]
    send[...] = grads[pl.ds(pl.multiple_of((1 - core) * rows, 16), rows)]
    dn2 = nt(dgate, wg[...]) + nt(dup, wu[...])
    gn[...] = jnp.sum(dn2 * hat, axis=0, keepdims=True)
    scaled = dn2 * g2
    dh1 = g + s2 * (scaled - hat * jnp.mean(hat * scaled, axis=-1, keepdims=True))
    dh[...] = dh1
    dhb = dh1.astype(bf16)
    full = tn(mixed, dhb)
    dmix = nt(dhb, wo[...]).astype(bf16).astype(f32)
    lanes = iota((t, 128), 1)
    deltas = jnp.zeros((t, 128), f32)
    for h in range(heads):
        gwo[h * 64 : h * 64 + 64] = full[h * 128 + 64 : h * 128 + 128].astype(bf16)
        inverse = o[:, h * 128 : h * 128 + 1]
        dm = dmix[:, h * 128 : h * 128 + 128] * inverse
        deltas = jnp.where(lanes == h, jnp.sum(dm * o[:, h * 128 : h * 128 + 128], axis=1, keepdims=True), deltas)
        dop[:, h * 128 : h * 128 + 128] = dm.astype(bf16)
    delta[...] = deltas


def feed_forward(ids, lens, gain, x, o, wo, wg, wu, wd, cot):
    t, d = x.shape
    ff = wg.shape[1]
    smem = pl.BlockSpec(memory_space=pltpu.SMEM)
    vmem = pl.BlockSpec(memory_space=pltpu.VMEM)
    shape = jax.ShapeDtypeStruct
    half = 3 * d // 2
    return pl.pallas_call(
        feed_forward_kernel,
        in_specs=[smem, smem] + [vmem] * 8,
        out_specs=[vmem] * 8,
        out_shape=[
            shape((t, d), bf16),
            shape((t, d), f32),
            shape((t, o.shape[1]), bf16),
            shape((t, 128), f32),
            shape((o.shape[1] // 2, d), bf16),
            shape((half, ff), bf16),
            shape((half, ff), bf16),
            shape((1, d), f32),
        ],
        scratch_shapes=[pltpu.VMEM((3 * d, ff), bf16)],
        compiler_params=pltpu.CompilerParams(vmem_limit_bytes=VMEM),
        name="feed_forward",
    )(ids, lens, gain, x, o, wo, wg, wu, wd, cot)


def attention_back_kernel(
    n, buckets, ids, gain, p, kv, e, n1, q, do, delta, wq, wkv, wqt, wkvt, gwo, gn,
    even, odd, dn1q, keep, send, ds, dkv, dq, grads, sums, line,
):
    h = pl.program_id(0)
    heads = pl.num_programs(0)
    me = ids[0]
    t = q.shape[0]
    width = gwo.shape[0]
    lanes = iota((t, 128), 1)
    lhs = jnp.concatenate([q[...].T, do[...].T], axis=1)
    shift = jnp.sum(jnp.where(lanes == h, delta[...], 0.0), axis=1, keepdims=True)
    acc = jnp.zeros((t, 256), f32)
    weight = jnp.zeros((128, n1.shape[2]), f32)
    for j in range(n):
        probs = p[0, j]
        keys = kv[0, j]
        d_score = (probs.astype(f32) * (nt(do[...], keys) - shift)).astype(bf16)
        ds[j] = d_score
        acc = acc + nn(d_score, jnp.concatenate([keys, e[j]], axis=1))
        both = nn(lhs, jnp.concatenate([d_score, probs], axis=0)).astype(bf16)
        dkv[j, pl.ds(pl.multiple_of(h * 128, 128), 128)] = both
        weight = weight + nn(both, n1[j])
    dqb = acc[:, :128].astype(bf16)
    dq[h] = dqb
    from_q = nn(dqb.T, n1[0])[:64]
    at = pl.multiple_of(h * 64, 64)
    grads[pl.ds(at, 64)] = from_q.astype(bf16)
    grads[pl.ds(pl.multiple_of(width + h * 64, 64), 64)] = weight[:64].astype(bf16)
    grads[pl.ds(pl.multiple_of(2 * width + h * 64, 64), 64)] = weight[64:].astype(bf16)
    gains = jnp.sum(from_q * wqt[...].astype(f32), axis=0, keepdims=True)
    gains = gains + jnp.sum(weight * wkvt[...].astype(f32), axis=0, keepdims=True)

    @pl.when(h == 0)
    def _():
        sums[...] = jnp.zeros_like(sums)
        line[...] = jnp.zeros_like(line)

    sums[0:1] = sums[0:1] + gains
    back = (iota((t, t), 0) + iota((t, t), 1) == t - 1).astype(f32).astype(bf16)
    parts = []
    for r in (-1, 0, 1):
        there = me + r
        inside = (there >= 0) & (there < n)
        slot = jnp.where(inside, me ^ there, 0)
        parts.append(nn(back, ds[slot]) * inside.astype(f32))
    parts.append(jnp.zeros((t, t), f32))
    band = pltpu.roll(jnp.concatenate(parts, axis=1), 0, 1, stride=1, stride_axis=0)
    line[...] = line[...] + jnp.where(iota(line.shape, 0) == h, jnp.sum(band, axis=0, keepdims=True), 0.0)
    ends = jnp.sum(acc[:, 128:], axis=0, keepdims=True)
    lane = iota((1, 128), 1)
    left = jnp.sum(jnp.where(lane == LEFT, ends, 0.0), axis=1, keepdims=True)
    right = jnp.sum(jnp.where(lane == RIGHT, ends, 0.0), axis=1, keepdims=True)
    far = jnp.where(lane == buckets // 2 - 1, left, jnp.where(lane == buckets - 1, right, 0.0))
    sums[:, :128] = sums[:, :128] + jnp.where(iota((SMALL, 128), 0) == 2 + h, far, 0.0)

    @pl.when(h == heads - 1)
    def _():
        for j in range(0, n, 2):
            even[j // 2] = nn(wkv[...], dkv[j]).astype(bf16)
            odd[j // 2] = nn(wkv[...], dkv[j + 1]).astype(bf16)
        total = jnp.zeros((t, n1.shape[2]), f32)
        for k in range(dq.shape[0]):
            total = total + nt(dq[k], wq[:, k * 128 : k * 128 + 128])
        dn1q[...] = total
        u = iota((4 * t, 128), 0)
        pick = (bucket_of(u - (2 * t - 1), buckets) == iota((4 * t, 128), 1)).astype(f32)
        near = lax.dot_general(line[...], pick, (((1,), (0,)), ((), ())), precision=lax.Precision.HIGHEST,
                               preferred_element_type=f32)
        sums[2:8, :128] = sums[2:8, :128] + near[:6]
        sums[0:1] = sums[0:1] / gain[...]
        sums[1:2] = gn[...]
        small = sums[...].astype(bf16)
        grads[pl.ds(3 * width, width)] = gwo[...]
        rows = 2 * width
        core = me % 2
        keep[:rows] = grads[pl.ds(pl.multiple_of(core * rows, 16), rows)]
        send[:rows] = grads[pl.ds(pl.multiple_of((1 - core) * rows, 16), rows)]
        keep[rows:] = small
        send[rows:] = small


def attention_back(ids, gain, buckets, p, kv, e, n1, q, do, delta, wq, wkv, wqt, wkvt, gwo, gn):
    heads, n, t, _ = p.shape
    d = n1.shape[2]
    smem = pl.BlockSpec(memory_space=pltpu.SMEM)
    const = lambda *shape: pl.BlockSpec(shape, lambda i: (0,) * len(shape), pipeline_mode=pl.Buffered(1))
    keep = lambda *shape: pl.BlockSpec(shape, lambda i: (0,) * len(shape))
    by_head = lambda *shape: pl.BlockSpec((1, n, *shape), lambda i: (i, 0, 0, 0))
    column = pl.BlockSpec((t, 128), lambda i: (0, i))
    shape = jax.ShapeDtypeStruct
    half = 2 * gwo.shape[0] + SMALL
    return pl.pallas_call(
        partial(attention_back_kernel, n, buckets),
        grid=(heads,),
        in_specs=[
            smem, const(1, d), by_head(t, t), by_head(t, 128), const(n, t, 128), const(n, t, d),
            column, column, const(t, 128), const(*wq.shape), const(*wkv.shape),
            pl.BlockSpec((64, d), lambda i: (i, 0)), pl.BlockSpec((128, d), lambda i: (i, 0)),
            const(*gwo.shape), const(1, d),
        ],
        out_specs=[keep(n // 2, d, t), keep(n // 2, d, t), keep(t, d), keep(half, d), keep(half, d)],
        out_shape=[
            shape((n // 2, d, t), bf16),
            shape((n // 2, d, t), bf16),
            shape((t, d), f32),
            shape((half, d), bf16),
            shape((half, d), bf16),
        ],
        scratch_shapes=[
            pltpu.VMEM((n, t, t), bf16),
            pltpu.VMEM((n, heads * 128, t), bf16),
            pltpu.VMEM((heads, t, 128), bf16),
            pltpu.VMEM((4 * gwo.shape[0], d), bf16),
            pltpu.VMEM((SMALL, d), f32),
            pltpu.VMEM((8, 4 * t), f32),
        ],
        compiler_params=pltpu.CompilerParams(vmem_limit_bytes=VMEM),
        name="attention_back",
    )(ids, gain, p, kv, e, n1, q, do, delta, wq, wkv, wqt, wkvt, gwo, gn)


def whole_call(kernel, name, out_shape, *args, scratch=()):
    smem = pl.BlockSpec(memory_space=pltpu.SMEM)
    vmem = pl.BlockSpec(memory_space=pltpu.VMEM)
    return pl.pallas_call(
        kernel,
        in_specs=[smem] + [vmem] * (len(args) - 1),
        out_specs=jax.tree.map(lambda _: vmem, out_shape),
        out_shape=out_shape,
        scratch_shapes=list(scratch),
        compiler_params=pltpu.CompilerParams(vmem_limit_bytes=VMEM),
        name=name,
    )(*args)


def split_kernel(which, count, extra, ids, *refs):
    inputs, outs = refs[:-count], refs[-count:]
    rows = (inputs[0].shape[0] - extra) // count
    own = ids[which]
    for j in range(count):
        at = pl.ds(pl.multiple_of((own ^ j) * rows, 16), rows)
        total = inputs[0][at].astype(f32)
        for ref in inputs[1:]:
            total = total + ref[at].astype(f32)
        outs[j][:rows] = total.astype(bf16)
    if extra:
        at = pl.ds(rows * count, extra)
        total = inputs[0][at].astype(f32)
        for ref in inputs[1:]:
            total = total + ref[at].astype(f32)
        for j in range(count):
            outs[j][rows:] = total.astype(bf16)


def add_and_split(which, count, extra, ids, *arrays):
    rows = (arrays[0].shape[0] - extra) // count + extra
    out = jax.ShapeDtypeStruct((rows, arrays[0].shape[1]), bf16)
    return whole_call(partial(split_kernel, which, count, extra), "add_parts", [out] * count, ids, *arrays)


def swap(array, axis, j):
    size = lax.axis_size(axis)
    return lax.ppermute(array, axis, [(i, i ^ j) for i in range(size)])


def reduce_halves(ids, keep, send, extra):
    chips, rows = lax.axis_size("seq") // 2, lax.axis_size("rows")
    recv = swap(send, "seq", 1)
    size = keep.shape[0] - extra
    if size % (16 * chips * rows):
        both = add_and_split(0, 1, extra, ids * 0, keep, recv)[0].astype(f32)
        placed = jnp.zeros((2 * size, keep.shape[1]), f32)
        placed = lax.dynamic_update_slice_in_dim(placed, both[:size], ids[1] * size, 0)
        full, tail = lax.psum((placed, both[size:] * 0.5), ("rows", "seq"))
        mine = lax.dynamic_slice_in_dim(full, ids[1] * size, size, 0)
        other = lax.dynamic_slice_in_dim(full, (1 - ids[1]) * size, size, 0)
        return mine.astype(bf16), other.astype(bf16), tail.astype(bf16)
    parts = add_and_split(2, chips, extra, ids, keep, recv)
    parts = [parts[0]] + [swap(parts[j], "seq", 2 * j) for j in range(1, chips)]
    parts = add_and_split(3, rows, extra, ids, *parts)
    parts = [parts[0]] + [swap(parts[j], "rows", j) for j in range(1, rows)]
    done = add_and_split(3, 1, extra, ids * 0, *parts)[0]
    least = size // (chips * rows)
    chunk = done[:least]
    line = jnp.concatenate([chunk] + [swap(chunk, "rows", j) for j in range(1, rows)], axis=0)
    half = jnp.concatenate([line] + [swap(line, "seq", 2 * j) for j in range(1, chips)], axis=0)
    return half, swap(half, "seq", 1), done[least:]


def place_halves(ids, mine, other, full, chips, rows):
    size = mine.shape[0]
    least = size // (chips * rows)
    for c, ref in ((ids[1], mine), (1 - ids[1], other)):
        if chips * rows == 1:
            full[pl.ds(pl.multiple_of(c * size, 16), size)] = ref[...]
            continue
        for a in range(chips):
            for b in range(rows):
                at = c * size + ((ids[2] ^ a) * rows + (ids[3] ^ b)) * least
                full[pl.ds(pl.multiple_of(at, 16), least)] = ref[pl.ds((a * rows + b) * least, least)]


def unpack_ffn_kernel(chips, rows, ids, mine, other, gate, up, down, full):
    place_halves(ids, mine, other, full, chips, rows)
    d = gate.shape[0]
    gate[...] = full[:d].astype(f32)
    up[...] = full[d : 2 * d].astype(f32)
    down[:d] = full[2 * d :, :d].astype(f32)
    down[d:] = full[2 * d :, d:].astype(f32)


def unpack_attention_kernel(chips, rows, heads, ids, mine, other, tail, gq, gk, gv, go, g1, g2, gb, full):
    place_halves(ids, mine, other, full, chips, rows)
    w = gq.shape[1]
    for k, ref in enumerate((gq, gk, gv)):
        ref[...] = full[k * w : (k + 1) * w].astype(f32).T
    go[...] = full[3 * w :].astype(f32)
    small = tail[...].astype(f32)
    g1[...] = small[0:1]
    g2[...] = small[1:2]
    gb[...] = small[0:8, :128].T[: gb.shape[0], 2 : 2 + heads]


def input_grad_kernel(ids, *refs):
    *parts, dn1q, x, dh, gain, out = refs
    total = parts[0][...].astype(f32)
    for ref in parts[1:]:
        total = total + ref[...].astype(f32)
    dn1 = total.T + dn1q[...]
    value = x[...].astype(f32)
    s1 = lax.rsqrt(jnp.mean(value * value, axis=-1, keepdims=True) + EPS)
    hat = value * s1
    scaled = dn1 * gain[...]
    out[...] = dh[...] + s1 * (scaled - hat * jnp.mean(hat * scaled, axis=-1, keepdims=True))


def slots_kernel(count, ids, mine, other, *outs):
    for j in range(count):
        outs[j][...] = (mine[j].astype(f32) + other[j].astype(f32)).astype(bf16)


def shards(
    tokens, norm_attn, query_weight, key_weight, value_weight, out_weight, bucket_bias_table, norm_ffn,
    gate_weight, expansion_matrix, down_weight, lengths, cotangent,
):
    _, t, d = tokens.shape
    n = lax.axis_size("seq")
    buckets, heads = bucket_bias_table.shape
    width = query_weight.shape[1]
    dk = width // heads
    seq = lax.axis_index("seq")
    ids = jnp.stack([seq, seq % 2, seq // 2, lax.axis_index("rows")]).astype(i32)
    x = tokens.reshape(t, d)
    cot = cotangent.reshape(t, d)
    lens = lengths.reshape(-1)

    blocks = [None] * n
    blocks[0] = x
    for j in range(n - 2, 0, -2):
        blocks[j] = swap(x, "seq", j)
    for j in range(0, n, 2):
        blocks[j + 1] = swap(blocks[j], "seq", 1)

    by_head = lambda w: w.reshape(d, heads, dk)
    wq = jnp.pad(by_head(query_weight), ((0, 0), (0, 0), (0, 128 - dk))).reshape(d, heads * 128)
    wkv = jnp.concatenate([by_head(key_weight), by_head(value_weight)], axis=2).reshape(d, heads * 128)
    wo = jnp.pad(out_weight.reshape(heads, dk, d), ((0, 0), (128 - dk, 0), (0, 0))).reshape(heads * 128, d)
    table = bucket_bias_table.astype(f32)
    gain1 = norm_attn.astype(f32).reshape(1, d)
    gain2 = norm_ffn.astype(f32).reshape(1, d)

    n1, kv, e, p, o, q = attention_forward(ids, lens, table, gain1, blocks, wq, wkv)
    output, dh, do, delta, gwo, keep, send, gn = feed_forward(
        ids, lens, gain2, x, o, wo, gate_weight, expansion_matrix, down_weight, cot
    )
    ffn = reduce_halves(ids, keep, send, 0)
    even, odd, dn1q, keep, send = attention_back(
        ids, gain1, buckets, p, kv, e, n1, q, do, delta, wq, wkv, query_weight.T, wkv.T, gwo, gn
    )
    mine, other, tail = reduce_halves(ids, keep, send, SMALL)
    recv = swap(odd, "seq", 1)
    half = n // 2
    parts = whole_call(partial(slots_kernel, half), "add_slots",
                       [jax.ShapeDtypeStruct((d, t), bf16)] * half, ids, even, recv)
    parts = [parts[0]] + [swap(parts[j], "seq", 2 * j) for j in range(1, half)]
    grad_tokens = whole_call(input_grad_kernel, "input_grad", jax.ShapeDtypeStruct((t, d), f32),
                             ids, *parts, dn1q, x, dh, gain1)

    rows = lax.axis_size("rows")
    chips = n // 2
    if keep.shape[0] - SMALL and (keep.shape[0] - SMALL) % (16 * chips * rows):
        chips = rows = 1
    ff = gate_weight.shape[1]
    shape = jax.ShapeDtypeStruct
    gate, up, down = whole_call(
        partial(unpack_ffn_kernel, chips, rows), "unpack_ffn",
        [shape((d, ff), f32), shape((d, ff), f32), shape((ff, d), f32)],
        ids, ffn[0], ffn[1], scratch=[pltpu.VMEM((3 * d, ff), bf16)],
    )
    gq, gk, gv, go, g1, g2, gb = whole_call(
        partial(unpack_attention_kernel, chips, rows, heads), "unpack_attention",
        [shape((d, width), f32)] * 3 + [shape((width, d), f32)] + [shape((1, d), f32)] * 2
        + [shape((buckets, heads), f32)],
        ids, mine, other, tail, scratch=[pltpu.VMEM((4 * width, d), bf16)],
    )
    return (
        output.reshape(tokens.shape), grad_tokens.reshape(tokens.shape), g1.reshape(d), gq, gk, gv, go, gb,
        g2.reshape(d), gate, up, down,
    )


def solution(mesh):
    split = P("rows", "seq", None)
    in_specs = (split,) + (P(),) * 10 + (P("rows", None), split)
    out_specs = (split, split) + (P(),) * 10
    return jax.shard_map(shards, mesh=mesh, in_specs=in_specs, out_specs=out_specs, check_vma=False)
```

```python
from functools import partial

import jax
import jax.numpy as jnp
from jax import lax
from jax.experimental import pallas as pl
from jax.experimental.pallas import tpu as pltpu
from jax.sharding import PartitionSpec as P

EPS = 1e-6
BIG = -(2.0**30)
LEFT, RIGHT, ONES = 17, 18, 19
SMALL = 16
VMEM = 24 * 1024 * 1024
MUCH = 56 * 1024 * 1024

f32, bf16, i32 = jnp.float32, jnp.bfloat16, jnp.int32


def thresholds(buckets, max_distance):
    half = buckets // 2
    exact = half // 2
    steps = half - exact
    out = list(range(1, exact))
    for j in range(steps):
        target = exact ** (steps - j) * max_distance**j
        m = exact
        while m**steps < target:
            m += 1
        out.append(m)
    return out


def bucket_of(offset, buckets):
    distance = jnp.abs(offset)
    bucket = (offset > 0).astype(i32) * (buckets // 2)
    for t in thresholds(buckets, 128):
        bucket = bucket + (distance >= t).astype(i32)
    return bucket


def nn(a, b):
    return lax.dot_general(a, b, (((1,), (0,)), ((), ())), preferred_element_type=f32)


def nt(a, b):
    return lax.dot_general(a, b, (((1,), (1,)), ((), ())), preferred_element_type=f32)


def tn(a, b):
    return lax.dot_general(a, b, (((0,), (0,)), ((), ())), preferred_element_type=f32)


def iota(shape, dim):
    return lax.broadcasted_iota(i32, shape, dim)


def rms(values, gain):
    scale = lax.rsqrt(jnp.mean(values * values, axis=-1, keepdims=True) + EPS)
    return values * scale * gain


def call(kernel, name, us, out_shape, smem_args, args, scratch=(), much=False):
    smem = pl.BlockSpec(memory_space=pltpu.SMEM)
    vmem = pl.BlockSpec(memory_space=pltpu.VMEM)
    return pl.pallas_call(
        kernel,
        in_specs=[smem] * len(smem_args) + [vmem] * len(args),
        out_specs=jax.tree.map(lambda _: vmem, out_shape),
        out_shape=out_shape,
        scratch_shapes=list(scratch),
        compiler_params=pltpu.CompilerParams(vmem_limit_bytes=MUCH if much else VMEM),
        cost_estimate=pl.CostEstimate(flops=int(us * 1e9), bytes_accessed=int(us * 2e6), transcendentals=0),
        name=name,
    )(*smem_args, *args)


def shape(*dims, dtype=bf16):
    return jax.ShapeDtypeStruct(dims, dtype)


def low_half(t):
    return iota((t, 128), 1) < 64


def turn(pair):
    return pltpu.roll(pair, 64, 1)


def prepare_kernel(ids, lens, x, gain, table, wq, wk, wv, q, ext, bands, wt, line):
    t = x.shape[0]
    buckets, heads = table.shape
    n1 = rms(x[...].astype(f32), gain[...].astype(f32)).astype(bf16)
    q[...] = nn(n1, wq[...]).astype(bf16)
    low, high = segment_bounds(lens)
    lanes = iota((t, 128), 1)
    pos = iota((t, 128), 0) + ids[0] * t
    other = jnp.where((pos >= low) & (pos < high), 0.0, BIG)
    ext[...] = jnp.where(lanes < LEFT, other, 0.0)
    u = iota((buckets, 4 * t), 1)
    bucket = bucket_of(jnp.where(u < 3 * t, u - t, u - 5 * t), buckets)
    pick = (bucket == iota((buckets, 4 * t), 0)).astype(f32).astype(bf16)
    line[...] = jnp.zeros_like(line)
    line[:heads] = tn(table[...], pick)
    for h in range(heads):
        band = pltpu.roll(jnp.broadcast_to(line[h : h + 1], (t, 4 * t)), 0, 1, stride=1, stride_axis=0)
        for r in range(3):
            bands[h, r] = band[:, r * t : (r + 1) * t].astype(bf16)
        bands[h, 3] = jnp.zeros((t, t), bf16)
    w = wq.shape[1]
    for k, ref in enumerate((wq, wk, wv)):
        wt[k * w : (k + 1) * w] = ref[...].astype(f32).T.astype(bf16)


def prepare(ids, lens, x, gain, table, wq, wk, wv):
    t, d = x.shape
    heads, w = table.shape[1], wq.shape[1]
    return call(
        prepare_kernel, "prepare", 4,
        [shape(t, w), shape(t, 128, dtype=f32), shape(heads, 4, t, t), shape(3 * w, d), shape(8, 4 * t, dtype=f32)],
        (ids, lens), (x, gain, table, wq, wk, wv),
    )


def segment_bounds(lens):
    lane = iota((1, 128), 1)
    low = jnp.where(lane == 0, -1, 2**30)
    high = jnp.full((1, 128), -1, i32)
    total = 0
    for k in range(lens.shape[0]):
        total = total + lens[k]
        high = jnp.where(lane == k, total, high)
        low = jnp.where(lane == k + 1, total, low)
    return low, jnp.where(lane == lens.shape[0], 2**30, high)


def attend_kernel(n, first, count, ids, lens, *refs):
    x = refs[:count]
    gain, wk, wv, q, ext, bands, line, n1, e, acc, stat = refs[count : count + 11]
    pairs = q.shape[1] // 128
    kv, p = refs[count + 11 : count + 11 + pairs], refs[count + 11 + pairs : -1]
    s = refs[-1]
    me = ids[0]
    t = x[0].shape[0]
    low, high = segment_bounds(lens)
    row = iota((t, 128), 0)
    lanes = iota((t, 128), 1)
    for i in range(count):
        at = slice(i * t, (i + 1) * t)
        n1[at] = rms(x[i][...].astype(f32), gain[...].astype(f32)).astype(bf16)
        block = me ^ (first + i)
        pos = row + block * t
        away = block - me
        flag = jnp.where(away <= -2, LEFT, jnp.where(away >= 2, RIGHT, ONES))
        here = ((pos >= low) & (pos < high)) | (lanes == flag) | (lanes == ONES)
        e[at] = here.astype(f32).astype(bf16)
    upper = iota((count * t, 128), 1) >= 64
    stats = jnp.zeros((t, 128), f32)
    for g in range(pairs):
        at = slice(g * 128, g * 128 + 128)
        both = nn(n1[...], jnp.concatenate([wk[:, at], wv[:, at]], axis=1))
        keys, values = both[:, :128], turn(both[:, 128:])
        kv[g][0] = jnp.where(upper, values, keys).astype(bf16)
        kv[g][1] = jnp.where(upper, keys, values).astype(bf16)
        q2 = q[:, at].astype(f32)
        sums = []
        for k in range(2):
            h = 2 * g + k
            lane_ext = jnp.where(lanes == LEFT, line[h : h + 1, 0:1],
                                 jnp.where(lanes == RIGHT, line[h : h + 1, 3 * t - 1 : 3 * t], ext[...]))
            qh = jnp.where(low_half(t) == (k == 0), q2, 0.0)
            qa = jnp.concatenate([qh, lane_ext], axis=1).astype(bf16)
            right = jnp.concatenate([kv[g][k], e[...]], axis=1)
            s[...] = nt(qa, right)
            for r in (-1, 0, 1):
                there = me + r
                slot = (me ^ there) - first
                inside = (there >= 0) & (there < n) & (slot >= 0) & (slot < count)
                if r == 0 and first > 0:
                    continue
                where = pl.ds(pl.multiple_of(jnp.where(inside, slot, 0) * t, t), t)
                s[:, where] = s[:, where] + bands[h, jnp.where(inside, r + 1, 3)].astype(f32)
            top = s[:, :128]
            for i in range(1, count * t // 128):
                top = jnp.maximum(top, s[:, i * 128 : (i + 1) * 128])
            top = jnp.max(top, axis=1, keepdims=True)
            raised = jnp.exp(s[...] - top).astype(bf16)
            p[g][k] = raised
            out = nn(raised, right)
            sums.append(out[:, :128])
            stats = jnp.where(lanes == h, top, stats)
            stats = jnp.where(lanes == 8 + h, out[:, 128 + ONES : 129 + ONES], stats)
        acc[:, at] = turn(jnp.where(low_half(t), sums[1], sums[0]))
    stat[...] = stats


def attend(n, first, ids, lens, blocks, gain, wk, wv, q, ext, bands, line):
    count = len(blocks)
    t, d = blocks[0].shape
    pairs = wk.shape[1] // 128
    c = count * t
    out = call(
        partial(attend_kernel, n, first, count), "attend", 2 * count,
        [shape(c, d), shape(c, 128), shape(t, wk.shape[1], dtype=f32), shape(t, 128, dtype=f32)]
        + [shape(2, c, 128)] * pairs + [shape(2, t, c)] * pairs,
        (ids, lens), (*blocks, gain, wk, wv, q, ext, bands, line), scratch=[pltpu.VMEM((t, c), f32)], much=n > 8,
    )
    return dict(n1=out[0], e=out[1], acc=out[2], stat=out[3], kv=out[4 : 4 + pairs], p=out[4 + pairs :])


def feed_forward_kernel(phases, ids, lens, gain, x, wo, wg, wu, wd, cot, *refs):
    accs, stats = refs[:phases], refs[phases : 2 * phases]
    out, dh, do, scale, gwo, keep, send, gn, o, grads = refs[2 * phases :]
    t, d = x.shape
    pairs = wo.shape[0] // 128
    lanes = iota((t, 128), 1)
    scales = jnp.zeros((t, 128), f32)
    for g in range(pairs):
        at = slice(g * 128, g * 128 + 128)
        factors = []
        for h in (2 * g, 2 * g + 1):
            tops = [ref[:, h : h + 1] for ref in stats]
            top = tops[0]
            for other in tops[1:]:
                top = jnp.maximum(top, other)
            weights = [jnp.exp(v - top) for v in tops]
            total = weights[0] * stats[0][:, 8 + h : 9 + h]
            for w, ref in zip(weights[1:], stats[1:], strict=True):
                total = total + w * ref[:, 8 + h : 9 + h]
            weights = [w / total for w in weights]
            for i, w in enumerate(weights):
                scales = jnp.where(lanes == 8 * i + h, w, scales)
            factors.append(weights)
        value = jnp.zeros((t, 128), f32)
        for i in range(phases):
            value = value + accs[i][:, at] * jnp.where(lanes < 64, factors[0][i], factors[1][i])
        o[:, at] = value
    mixed = o[...].astype(bf16)
    h1 = x[...].astype(f32) + nn(mixed, wo[...])
    g2 = gain[...].astype(f32)
    s2 = lax.rsqrt(jnp.mean(h1 * h1, axis=-1, keepdims=True) + EPS)
    hat = h1 * s2
    n2 = (hat * g2).astype(bf16)
    gate = nn(n2, wg[...])
    up = nn(n2, wu[...])
    c0 = 0.7978845608028654
    square = gate * gate
    th = jnp.tanh(c0 * gate * (1.0 + 0.044715 * square))
    half = 0.5 * (1.0 + th)
    act = gate * half
    dact = half + 0.5 * gate * (1.0 - th * th) * (c0 * (1.0 + 3 * 0.044715 * square))
    u = (act * up).astype(bf16)
    out[...] = (h1 + nn(u, wd[...])).astype(bf16)
    total = lens[0]
    for k in range(1, lens.shape[0]):
        total = total + lens[k]
    pos = ids[0] * t + iota((t, 1), 0)
    g = cot[...].astype(f32) * (pos < total).astype(f32)
    gb = g.astype(bf16)
    down = tn(u, gb).astype(bf16)
    grads[2 * d : 3 * d, :d] = down[:d]
    grads[2 * d : 3 * d, d:] = down[d:]
    du = nt(gb, wd[...]).astype(bf16).astype(f32)
    dgate = (du * up * dact).astype(bf16)
    dup = (du * act).astype(bf16)
    grads[0:d] = tn(n2, dgate).astype(bf16)
    grads[d : 2 * d] = tn(n2, dup).astype(bf16)
    rows = keep.shape[0]
    core = ids[1]
    keep[...] = grads[pl.ds(pl.multiple_of(core * rows, 16), rows)]
    send[...] = grads[pl.ds(pl.multiple_of((1 - core) * rows, 16), rows)]
    dn2 = nt(dgate, wg[...]) + nt(dup, wu[...])
    gn[...] = jnp.sum(dn2 * hat, axis=0, keepdims=True)
    scaled = dn2 * g2
    dh1 = g + s2 * (scaled - hat * jnp.mean(hat * scaled, axis=-1, keepdims=True))
    dh[...] = dh1
    dhb = dh1.astype(bf16)
    gwo[...] = tn(mixed, dhb).astype(bf16)
    dmix = nt(dhb, wo[...]).astype(bf16)
    do[...] = dmix
    product = dmix.astype(f32) * o[...]
    for h in range(2 * pairs):
        part = product[:, h // 2 * 128 : h // 2 * 128 + 128]
        delta = jnp.sum(jnp.where(low_half(t) == (h % 2 == 0), part, 0.0), axis=1, keepdims=True)
        scales = jnp.where(lanes == 64 + h, delta, scales)
    scale[...] = scales


def feed_forward(ids, lens, gain, x, wo, wg, wu, wd, cot, parts):
    t, d = x.shape
    ff, w = wg.shape[1], wo.shape[0]
    half = 3 * d // 2
    return call(
        partial(feed_forward_kernel, len(parts)), "feed_forward", 8,
        [shape(t, d), shape(t, d, dtype=f32), shape(t, w), shape(t, 128, dtype=f32), shape(w, d),
         shape(half, ff), shape(half, ff), shape(1, d, dtype=f32)],
        (ids, lens), (gain, x, wo, wg, wu, wd, cot, *[v["acc"] for v in parts], *[v["stat"] for v in parts]),
        scratch=[pltpu.VMEM((t, w), f32), pltpu.VMEM((3 * d, ff), bf16)],
    )


def attend_back_kernel(n, g, counts, ids, q, do, scale, *refs):
    phases = len(counts)
    p, kv, e = (refs[k * phases : (k + 1) * phases] for k in range(3))
    dk, dv = (refs[k * phases : (k + 1) * phases] for k in (3, 4))
    dq, line, ds, stack = refs[5 * phases :]
    me = ids[0]
    t = q.shape[0]
    lower = low_half(t)
    at = slice(g * 128, g * 128 + 128)
    q2 = q[:, at].astype(f32)
    do2 = turn(do[:, at].astype(f32))
    back = (iota((t, t), 0) + iota((t, t), 1) == t - 1).astype(f32).astype(bf16)
    lane = iota((1, 128), 1)
    line[...] = jnp.zeros_like(line)
    sums = []
    for k in range(2):
        h = 2 * g + k
        qh = jnp.where(lower == (k == 0), q2, 0.0)
        doh = jnp.where(lower == (k == 1), do2, 0.0)
        acc = jnp.zeros((t, 256), f32)
        start = 0
        for i, count in enumerate(counts):
            c = count * t
            cols = slice(start, start + c)
            factor = scale[:, 8 * i + h : 8 * i + h + 1]
            scaled = doh * factor
            low = scaled.astype(bf16)
            keys = kv[i][k]
            probs = p[i][k]
            d_score = (probs.astype(f32) * (nt(low, keys) - scale[:, 64 + h : 65 + h] * factor)).astype(bf16)
            ds[:, cols] = d_score
            stack[:t, :c] = d_score
            stack[t:, :c] = probs
            acc = acc + nn(d_score, jnp.concatenate([keys, e[i][...]], axis=1))
            lhs = jnp.concatenate([qh.T, scaled.T], axis=1).astype(bf16)
            both = nn(lhs, stack[:, :c]).astype(bf16)
            mine, other = (both[:64], both[64:]) if k == 0 else (both[64:], both[:64])
            dk[i][k * 64 : k * 64 + 64] = mine
            dv[i][k * 64 : k * 64 + 64] = other
            start += c
        sums.append(acc[:, :128])
        parts = []
        for r in (-1, 0, 1):
            there = me + r
            inside = (there >= 0) & (there < n)
            slot = jnp.where(inside, me ^ there, 0)
            block = ds[:, pl.ds(pl.multiple_of(slot * t, t), t)]
            parts.append(nn(back, block) * inside.astype(f32))
        parts.append(jnp.zeros((t, t), f32))
        band = pltpu.roll(jnp.concatenate(parts, axis=1), 0, 1, stride=1, stride_axis=0)
        line[k : k + 1, : 4 * t] = jnp.sum(band, axis=0, keepdims=True)
        ends = jnp.sum(acc[:, 128:], axis=0, keepdims=True)
        line[k : k + 1, 4 * t :] = jnp.where((lane == LEFT) | (lane == RIGHT), ends, 0.0)
    dq[...] = jnp.where(lower, sums[0], sums[1]).astype(bf16)


def attend_back(n, g, ids, q, do, scale, parts):
    t = q.shape[0]
    widths = [v["e"].shape[0] for v in parts]
    s = sum(widths)
    phases = len(parts)
    out = call(
        partial(attend_back_kernel, n, g, [w // t for w in widths]), "attend_back", 4,
        [shape(128, w) for w in widths] * 2 + [shape(t, 128), shape(8, 4 * t + 128, dtype=f32)],
        (ids,), (q, do, scale, *[v["p"][g] for v in parts], *[v["kv"][g] for v in parts], *[v["e"] for v in parts]),
        scratch=[pltpu.VMEM((t, s), bf16), pltpu.VMEM((2 * t, max(widths)), bf16)], much=n > 8,
    )
    return dict(dk=out[:phases], dv=out[phases : 2 * phases], dq=out[-2], line=out[-1])


def gather_back_kernel(n, buckets, counts, pairs, ids, gain, gn, gwo, wq, wk, wv, wt, *refs):
    phases = len(counts)
    n1 = refs[:phases]
    dk = [refs[phases + 2 * i * pairs :][:pairs] for i in range(phases)]
    dv = [refs[phases + (2 * i + 1) * pairs :][:pairs] for i in range(phases)]
    refs = refs[phases + 2 * phases * pairs :]
    dq, lines = refs[:pairs], refs[pairs : 2 * pairs]
    even, odd, dn1q, keep, send, grads, sums, diagonal = refs[2 * pairs :]
    d, w = wq.shape
    t = dn1q.shape[0]
    weights = jnp.concatenate([wk[...], wv[...]], axis=1)
    total = jnp.zeros((2 * w, d), f32)
    slot = 0
    for i, count in enumerate(counts):
        both = jnp.concatenate([ref[...] for ref in (*dk[i], *dv[i])], axis=0)
        total = total + nn(both, n1[i][...])
        back = nn(weights, both).astype(bf16)
        for _ in range(count):
            ref = odd if slot % 2 else even
            ref[slot // 2] = back[:, (slot * t - sum(counts[:i]) * t) :][:, :t]
            slot += 1
    dq_all = jnp.concatenate([ref[...] for ref in dq], axis=1)
    from_q = tn(dq_all, n1[0][:t])
    dn1q[...] = nt(dq_all, wq[...])
    grads[:w] = from_q.astype(bf16)
    grads[w : 3 * w] = total.astype(bf16)
    grads[3 * w :] = gwo[...]
    gains = jnp.sum(from_q * wt[:w].astype(f32), axis=0, keepdims=True)
    gains = gains + jnp.sum(total * wt[w:].astype(f32), axis=0, keepdims=True)
    sums[...] = jnp.zeros_like(sums)
    sums[0:1] = gains / gain[...].astype(f32)
    sums[1:2] = gn[...]
    diagonal[...] = jnp.zeros_like(diagonal)
    for g in range(pairs):
        diagonal[2 * g : 2 * g + 2] = lines[g][:2]
    width = diagonal.shape[1]
    u = iota((width, 128), 0)
    bucket = bucket_of(u - (2 * t - 1), buckets)
    bucket = jnp.where(u == 4 * t + LEFT, buckets // 2 - 1, jnp.where(u == 4 * t + RIGHT, buckets - 1, bucket))
    pick = (bucket == iota((width, 128), 1)).astype(f32)
    sums[8:16, :128] = lax.dot_general(diagonal[...], pick, (((1,), (0,)), ((), ())),
                                       precision=lax.Precision.HIGHEST, preferred_element_type=f32)
    small = sums[...].astype(bf16)
    rows = 2 * w
    keep[:rows] = grads[pl.ds(pl.multiple_of(ids[1] * rows, 16), rows)]
    send[:rows] = grads[pl.ds(pl.multiple_of((1 - ids[1]) * rows, 16), rows)]
    keep[rows:] = small
    send[rows:] = small


def gather_back(n, buckets, ids, gain, gn, gwo, wq, wk, wv, wt, parts, backs):
    d, w = wq.shape
    t = backs[0]["dq"].shape[0]
    pairs = w // 128
    counts = [v["e"].shape[0] // t for v in parts]
    pieces = []
    for i in range(len(parts)):
        pieces += [v["dk"][i] for v in backs] + [v["dv"][i] for v in backs]
    half = 2 * w + SMALL
    return call(
        partial(gather_back_kernel, n, buckets, counts, pairs), "gather_back", 6,
        [shape(n // 2, d, t), shape(n // 2, d, t), shape(t, d, dtype=f32), shape(half, d), shape(half, d)],
        (ids,), (gain, gn, gwo, wq, wk, wv, wt, *[v["n1"] for v in parts], *pieces, *[v["dq"] for v in backs],
                 *[v["line"] for v in backs]),
        scratch=[pltpu.VMEM((4 * w, d), bf16), pltpu.VMEM((SMALL, d), f32), pltpu.VMEM((8, 4 * t + 128), f32)], much=n > 8,
    )


def split_kernel(which, count, extra, ids, *refs):
    inputs, outs = refs[:-count], refs[-count:]
    rows = (inputs[0].shape[0] - extra) // count
    own = ids[which]
    for j in range(count):
        at = pl.ds(pl.multiple_of((own ^ j) * rows, 16), rows)
        total = inputs[0][at].astype(f32)
        for ref in inputs[1:]:
            total = total + ref[at].astype(f32)
        outs[j][:rows] = total.astype(bf16)
    if extra:
        at = pl.ds(rows * count, extra)
        total = inputs[0][at].astype(f32)
        for ref in inputs[1:]:
            total = total + ref[at].astype(f32)
        for j in range(count):
            outs[j][rows:] = total.astype(bf16)


def add_and_split(which, count, extra, ids, *arrays):
    rows = (arrays[0].shape[0] - extra) // count + extra
    out = shape(rows, arrays[0].shape[1])
    return call(partial(split_kernel, which, count, extra), "add_parts", 1, [out] * count, (ids,), arrays)


def swap(array, axis, j):
    size = lax.axis_size(axis)
    return lax.ppermute(array, axis, [(i, i ^ j) for i in range(size)])


def reduce_start(ids, keep, send, extra):
    chips, rows = lax.axis_size("seq") // 2, lax.axis_size("rows")
    recv = swap(send, "seq", 1)
    if (keep.shape[0] - extra) % (64 * chips) or rows != 4:
        return add_and_split(0, 1, extra, ids * 0, keep, recv)
    return add_and_split(2, chips, extra, ids, keep, recv)


def reduce_finish(ids, parts, extra):
    chips, rows = lax.axis_size("seq") // 2, lax.axis_size("rows")
    if len(parts) == 1:
        both = parts[0].astype(f32)
        size = both.shape[0] - extra
        placed = jnp.zeros((2 * size, both.shape[1]), f32)
        placed = lax.dynamic_update_slice_in_dim(placed, both[:size], ids[1] * size, 0)
        full, tail = lax.psum((placed, both[size:] * 0.5), ("rows", "seq"))
        mine = lax.dynamic_slice_in_dim(full, ids[1] * size, size, 0)
        other = lax.dynamic_slice_in_dim(full, (1 - ids[1]) * size, size, 0)
        return [mine.astype(bf16)], [other.astype(bf16)], tail.astype(bf16)
    parts = [parts[0]] + [swap(parts[j], "seq", 2 * j) for j in range(1, chips)]
    near = ids[3:4] % 2
    mine, other = add_and_split(0, 2, extra, near, *parts)
    mine = add_and_split(0, 1, extra, near * 0, mine, swap(other, "rows", 1))[0]
    mine = add_and_split(0, 1, extra, near * 0, mine, swap(mine, "rows", 2))[0]
    size = mine.shape[0] - extra
    line = jnp.concatenate([mine[:size], swap(mine[:size], "rows", 1)], axis=0)
    own = [line] + [swap(line, "seq", 2 * j) for j in range(1, chips)]
    return own, [swap(v, "seq", 1) for v in own], mine[size:]


def place_halves(ids, mine, other, full):
    size = full.shape[0] // 2
    if len(mine) == 1:
        full[pl.ds(pl.multiple_of(ids[1] * size, 16), size)] = mine[0][...]
        full[pl.ds(pl.multiple_of((1 - ids[1]) * size, 16), size)] = other[0][...]
        return
    piece = size // len(mine)
    for c, refs in ((ids[1], mine), (1 - ids[1], other)):
        for a, ref in enumerate(refs):
            at = c * size + (ids[2] ^ a) * piece
            for b in range(2):
                where = at + ((ids[3] % 2) ^ b) * (piece // 2)
                full[pl.ds(pl.multiple_of(where, 16), piece // 2)] = ref[b * (piece // 2) : (b + 1) * (piece // 2)]


def unpack_ffn_kernel(pieces, ids, *refs):
    gate, up, down, full = refs[2 * pieces :]
    place_halves(ids, refs[:pieces], refs[pieces : 2 * pieces], full)
    d = gate.shape[0]
    gate[...] = full[:d].astype(f32)
    up[...] = full[d : 2 * d].astype(f32)
    down[:d] = full[2 * d :, :d].astype(f32)
    down[d:] = full[2 * d :, d:].astype(f32)


def unpack_attention_kernel(pieces, heads, ids, tail, *refs):
    gq, gk, gv, go, g1, g2, gb, full = refs[2 * pieces :]
    place_halves(ids, refs[:pieces], refs[pieces : 2 * pieces], full)
    w = gq.shape[1]
    for k, ref in enumerate((gq, gk, gv)):
        ref[...] = full[k * w : (k + 1) * w].astype(f32).T
    go[...] = full[3 * w :].astype(f32)
    small = tail[...].astype(f32)
    g1[...] = small[0:1]
    g2[...] = small[1:2]
    gb[...] = small[8:16, :128].T[: gb.shape[0], :heads]


def input_grad_kernel(ids, *refs):
    *parts, dn1q, x, dh, gain, out = refs
    total = parts[0][...].astype(f32)
    for ref in parts[1:]:
        total = total + ref[...].astype(f32)
    dn1 = total.T + dn1q[...]
    value = x[...].astype(f32)
    s1 = lax.rsqrt(jnp.mean(value * value, axis=-1, keepdims=True) + EPS)
    hat = value * s1
    scaled = dn1 * gain[...].astype(f32)
    out[...] = dh[...] + s1 * (scaled - hat * jnp.mean(hat * scaled, axis=-1, keepdims=True))


def slots_kernel(count, ids, mine, other, *outs):
    for j in range(count):
        outs[j][...] = (mine[j].astype(f32) + other[j].astype(f32)).astype(bf16)


def shards(
    tokens, norm_attn, query_weight, key_weight, value_weight, out_weight, bucket_bias_table, norm_ffn,
    gate_weight, expansion_matrix, down_weight, lengths, cotangent,
):
    _, t, d = tokens.shape
    n = lax.axis_size("seq")
    buckets, heads = bucket_bias_table.shape
    width = query_weight.shape[1]
    ff = gate_weight.shape[1]
    seq = lax.axis_index("seq")
    ids = jnp.stack([seq, seq % 2, seq // 2, lax.axis_index("rows")]).astype(i32)
    x = tokens.reshape(t, d)
    cot = cotangent.reshape(t, d)
    lens = lengths.reshape(-1)
    gain1 = norm_attn.reshape(1, d)
    gain2 = norm_ffn.reshape(1, d)

    blocks = [None] * n
    blocks[0] = x
    for j in range(n - 2, 0, -2):
        blocks[j] = swap(x, "seq", j)
    for j in range(0, n, 2):
        blocks[j + 1] = swap(blocks[j], "seq", 1)

    q, ext, bands, wt, line = prepare(ids, lens, x, gain1, bucket_bias_table, query_weight, key_weight, value_weight)
    cuts = [0, 2, 6, 8] if n == 8 else [0, 2, *range(8, n, 8), n]
    parts = [
        attend(n, a, ids, lens, blocks[a:b], gain1, key_weight, value_weight, q, ext, bands, line)
        for a, b in zip(cuts[:-1], cuts[1:], strict=True)
    ]
    output, dh, do, scale, gwo, keep, send, gn = feed_forward(
        ids, lens, gain2, x, out_weight, gate_weight, expansion_matrix, down_weight, cot, parts
    )
    ffn = reduce_start(ids, keep, send, 0)
    backs = [attend_back(n, 0, ids, q, do, scale, parts)]
    (*ffn, do, scale) = lax.optimization_barrier((*ffn, do, scale))
    backs += [attend_back(n, g, ids, q, do, scale, parts) for g in range(1, width // 128)]
    even, odd, dn1q, keep, send = gather_back(
        n, buckets, ids, gain1, gn, gwo, query_weight, key_weight, value_weight, wt, parts, backs
    )
    attention = reduce_start(ids, keep, send, SMALL)
    recv = swap(odd, "seq", 1)
    half = n // 2
    slots = call(partial(slots_kernel, half), "add_slots", 1, [shape(d, t)] * half, (ids,), (even, recv))
    slots = [slots[0]] + [swap(slots[j], "seq", 2 * j) for j in range(1, half)]
    grad_tokens = call(input_grad_kernel, "input_grad", 2, shape(t, d, dtype=f32), (ids,),
                       (*slots, dn1q, x, dh, gain1))

    mine, other, _ = reduce_finish(ids, ffn, 0)
    gate, up, down = call(
        partial(unpack_ffn_kernel, len(mine)), "unpack_ffn", 4,
        [shape(d, ff, dtype=f32), shape(d, ff, dtype=f32), shape(ff, d, dtype=f32)],
        (ids,), (*mine, *other), scratch=[pltpu.VMEM((3 * d, ff), bf16)],
    )
    mine, other, tail = reduce_finish(ids, attention, SMALL)
    gq, gk, gv, go, g1, g2, gb = call(
        partial(unpack_attention_kernel, len(mine), heads), "unpack_attention", 3,
        [shape(d, width, dtype=f32)] * 3 + [shape(width, d, dtype=f32)] + [shape(1, d, dtype=f32)] * 2
        + [shape(buckets, heads, dtype=f32)],
        (ids,), (tail, *mine, *other), scratch=[pltpu.VMEM((4 * width, d), bf16)],
    )
    return (
        output.reshape(tokens.shape), grad_tokens.reshape(tokens.shape), g1.reshape(d), gq, gk, gv, go, gb,
        g2.reshape(d), gate, up, down,
    )


def solution(mesh):
    split = P("rows", "seq", None)
    in_specs = (split,) + (P(),) * 10 + (P("rows", None), split)
    out_specs = (split, split) + (P(),) * 10
    return jax.shard_map(shards, mesh=mesh, in_specs=in_specs, out_specs=out_specs, check_vma=False)
```

```python
from functools import partial

import jax
import jax.numpy as jnp
from jax import lax
from jax.experimental import pallas as pl
from jax.experimental.pallas import tpu as pltpu
from jax.sharding import PartitionSpec as P

EPS = 1e-6
BIG = -(2.0**30)
LEFT, RIGHT, ONES = 17, 18, 19
FFN_CHUNKS = 1
SMALL = 16
VMEM = 24 * 1024 * 1024
MUCH = 56 * 1024 * 1024

f32, bf16, i32 = jnp.float32, jnp.bfloat16, jnp.int32


def thresholds(buckets, max_distance):
    half = buckets // 2
    exact = half // 2
    steps = half - exact
    out = list(range(1, exact))
    for j in range(steps):
        target = exact ** (steps - j) * max_distance**j
        m = exact
        while m**steps < target:
            m += 1
        out.append(m)
    return out


def bucket_of(offset, buckets):
    distance = jnp.abs(offset)
    bucket = (offset > 0).astype(i32) * (buckets // 2)
    for t in thresholds(buckets, 128):
        bucket = bucket + (distance >= t).astype(i32)
    return bucket


def nn(a, b):
    return lax.dot_general(a, b, (((1,), (0,)), ((), ())), preferred_element_type=f32)


def nt(a, b):
    return lax.dot_general(a, b, (((1,), (1,)), ((), ())), preferred_element_type=f32)


def tn(a, b):
    return lax.dot_general(a, b, (((0,), (0,)), ((), ())), preferred_element_type=f32)


def iota(shape, dim):
    return lax.broadcasted_iota(i32, shape, dim)


def rms(values, gain):
    scale = lax.rsqrt(jnp.mean(values * values, axis=-1, keepdims=True) + EPS)
    return values * scale * gain


def call(kernel, name, us, out_shape, smem_args, args, scratch=(), much=False, anywhere=0):
    smem = pl.BlockSpec(memory_space=pltpu.SMEM)
    vmem = pl.BlockSpec(memory_space=pltpu.VMEM)
    return pl.pallas_call(
        kernel,
        in_specs=[smem] * len(smem_args) + [vmem] * (len(args) - anywhere) + [pl.BlockSpec(memory_space=pltpu.HBM)] * anywhere,
        out_specs=jax.tree.map(lambda _: vmem, out_shape),
        out_shape=out_shape,
        scratch_shapes=list(scratch),
        compiler_params=pltpu.CompilerParams(vmem_limit_bytes=MUCH if much else VMEM),
        cost_estimate=pl.CostEstimate(flops=int(us * 1e6), bytes_accessed=int(us * 2e3), transcendentals=0),
        name=name,
    )(*smem_args, *args)


def shape(*dims, dtype=bf16):
    return jax.ShapeDtypeStruct(dims, dtype)


def low_half(t):
    return iota((t, 128), 1) < 64


def turn(pair):
    return pltpu.roll(pair, 64, 1)


def prepare_kernel(ids, lens, gain, table, x, wq, wk, wv, q, ext, bands, wt, line, x_here, wq_here, wk_here, wv_here, sems):
    pairs = ((x, x_here), (wq, wq_here), (wk, wk_here), (wv, wv_here))
    copies = [pltpu.make_async_copy(a, b, sems.at[i]) for i, (a, b) in enumerate(pairs)]
    for copy in copies:
        copy.start()
    t = x.shape[0]
    heads, buckets = table.shape
    low, high = segment_bounds(lens)
    lanes = iota((t, 128), 1)
    pos = iota((t, 128), 0) + ids[0] * t
    other = jnp.where((pos >= low) & (pos < high), 0.0, BIG)
    ext[...] = jnp.where(lanes < LEFT, other, 0.0)
    u = iota((buckets, 4 * t), 1)
    bucket = bucket_of(jnp.where(u < 3 * t, u - t, u - 5 * t), buckets)
    pick = (bucket == iota((buckets, 4 * t), 0)).astype(f32).astype(bf16)
    line[...] = jnp.zeros_like(line)
    line[:heads] = nn(table[...], pick)
    for h in range(heads):
        band = pltpu.roll(jnp.broadcast_to(line[h : h + 1], (t, 4 * t)), 0, 1, stride=1, stride_axis=0)
        for r in range(3):
            bands[h, r] = band[:, r * t : (r + 1) * t].astype(bf16)
        bands[h, 3] = jnp.zeros((t, t), bf16)
    for copy in copies:
        copy.wait()
    n1 = rms(x_here[...].astype(f32), gain[...].astype(f32)).astype(bf16)
    q[...] = nn(n1, wq_here[...]).astype(bf16)
    w = wq.shape[1]
    for k, ref in enumerate((wq_here, wk_here, wv_here)):
        wt[k * w : (k + 1) * w] = ref[...].astype(f32).T.astype(bf16)


def prepare(ids, lens, x, gain, table, wq, wk, wv):
    t, d = x.shape
    heads, w = table.shape[0], wq.shape[1]
    return call(
        prepare_kernel, "prepare", 4,
        [shape(t, w), shape(t, 128, dtype=f32), shape(heads, 4, t, t), shape(3 * w, d), shape(8, 4 * t, dtype=f32),
         shape(t, d), shape(d, w), shape(d, w), shape(d, w)],
        (ids, lens), (gain, table, x, wq, wk, wv), anywhere=4, scratch=[pltpu.SemaphoreType.DMA((4,))],
    )


def segment_bounds(lens):
    lane = iota((1, 128), 1)
    low = jnp.where(lane == 0, -1, 2**30)
    high = jnp.full((1, 128), -1, i32)
    total = 0
    for k in range(lens.shape[0]):
        total = total + lens[k]
        high = jnp.where(lane == k, total, high)
        low = jnp.where(lane == k + 1, total, low)
    return low, jnp.where(lane == lens.shape[0], 2**30, high)


def attend_kernel(n, first, count, ids, lens, *refs):
    x = refs[:count]
    gain, wk, wv, q, ext, bands, line, n1, e, acc, stat = refs[count : count + 11]
    pairs = q.shape[1] // 128
    kv, p = refs[count + 11 : count + 11 + pairs], refs[count + 11 + pairs : -1]
    s = refs[-1]
    me = ids[0]
    t = x[0].shape[0]
    low, high = segment_bounds(lens)
    row = iota((t, 128), 0)
    lanes = iota((t, 128), 1)
    for i in range(count):
        at = slice(i * t, (i + 1) * t)
        n1[at] = rms(x[i][...].astype(f32), gain[...].astype(f32)).astype(bf16)
        block = me ^ (first + i)
        pos = row + block * t
        away = block - me
        flag = jnp.where(away <= -2, LEFT, jnp.where(away >= 2, RIGHT, ONES))
        here = ((pos >= low) & (pos < high)) | (lanes == flag) | (lanes == ONES)
        e[at] = here.astype(f32).astype(bf16)
    upper = iota((t, 128), 1) >= 64
    near = [i for i in range(count) if (first + i) & (first + i + 1) == 0]

    def project(g, i):
        rows, at = slice(i * t, (i + 1) * t), slice(g * 128, g * 128 + 128)
        both = nn(n1[rows], jnp.concatenate([wk[:, at], wv[:, at]], axis=1))
        keys, values = both[:, :128], turn(both[:, 128:])
        kv[g][0, rows] = jnp.where(upper, values, keys).astype(bf16)
        kv[g][1, rows] = jnp.where(upper, keys, values).astype(bf16)

    def query(h):
        lane_ext = jnp.where(lanes == LEFT, line[h : h + 1, 0:1],
                             jnp.where(lanes == RIGHT, line[h : h + 1, 3 * t - 1 : 3 * t], ext[...]))
        q2 = q[:, h // 2 * 128 : h // 2 * 128 + 128].astype(f32)
        return jnp.concatenate([jnp.where(upper == (h % 2 == 1), q2, 0.0), lane_ext], axis=1).astype(bf16)

    def keys_of(h, i):
        rows = slice(i * t, (i + 1) * t)
        return jnp.concatenate([kv[h // 2][h % 2, rows], e[rows]], axis=1)

    def score(h, i, qa, top):
        block = nt(qa, keys_of(h, i))
        if i in near:
            away = (me ^ (first + i)) - me
            block = block + bands[h, jnp.where(jnp.abs(away) <= 1, away + 1, 3)].astype(f32)
        s[h % 2, :, i * t : (i + 1) * t] = block
        here = block[:, :128]
        for c in range(1, t // 128):
            here = jnp.maximum(here, block[:, c * 128 : (c + 1) * 128])
        return here if top is None else jnp.maximum(top, here)

    def mix(h, i, top, out):
        raised = jnp.exp(s[h % 2, :, i * t : (i + 1) * t] - top).astype(bf16)
        p[h // 2][h % 2, :, i * t : (i + 1) * t] = raised
        more = nn(raised, keys_of(h, i))
        return more if out is None else out + more

    for i in range(count):
        project(0, i)
    stats = jnp.zeros((t, 128), f32)
    last = None
    sums = []
    for h in range(2 * pairs + 1):
        qa = query(h) if h < 2 * pairs else None
        top = out = None
        for i in range(count):
            if h < 2 * pairs:
                top = score(h, i, qa, top)
            if h > 0:
                out = mix(h - 1, i, last, out)
            if h % 2 == 1 and h // 2 + 1 < pairs:
                project(h // 2 + 1, i)
        if h > 0:
            stats = jnp.where(lanes == h - 1, last, stats)
            stats = jnp.where(lanes == 7 + h, out[:, 128 + ONES : 129 + ONES], stats)
            sums.append(out[:, :128])
        if h < 2 * pairs:
            last = jnp.max(top, axis=1, keepdims=True)
    for g in range(pairs):
        acc[:, g * 128 : g * 128 + 128] = turn(jnp.where(upper, sums[2 * g], sums[2 * g + 1]))
    stat[...] = stats


def attend(n, first, ids, lens, blocks, gain, wk, wv, q, ext, bands, line):
    count = len(blocks)
    t, d = blocks[0].shape
    pairs = wk.shape[1] // 128
    c = count * t
    out = call(
        partial(attend_kernel, n, first, count), "attend", 2 * count,
        [shape(c, d), shape(c, 128), shape(t, wk.shape[1], dtype=f32), shape(t, 128, dtype=f32)]
        + [shape(2, c, 128)] * pairs + [shape(2, t, c)] * pairs,
        (ids, lens), (*blocks, gain, wk, wv, q, ext, bands, line), scratch=[pltpu.VMEM((2, t, c), f32)], much=n > 8,
    )
    return dict(n1=out[0], e=out[1], acc=out[2], stat=out[3], kv=out[4 : 4 + pairs], p=out[4 + pairs :])


def feed_forward_kernel(phases, ids, lens, gain, x, wo, wg, wu, wd, cot, *refs):
    accs, stats = refs[:phases], refs[phases : 2 * phases]
    out, dh, do, scale, gwo, keep, send, gn, grads, mixed_all, n2_all, u_all, gb_all, dg_all, du_all, dh_all = refs[2 * phases :]
    t, d = x.shape
    pairs = wo.shape[0] // 128
    chunk = t // FFN_CHUNKS
    lanes = iota((chunk, 128), 1)
    g2 = gain[...].astype(f32)
    last = lens[0]
    for k in range(1, lens.shape[0]):
        last = last + lens[k]
    work = [dict(rows=slice(c * chunk, (c + 1) * chunk)) for c in range(FFN_CHUNKS)]

    def weigh(v):
        rows = v["rows"]
        tops = [ref[rows] for ref in stats]
        top = tops[0]
        for other in tops[1:]:
            top = jnp.maximum(top, other)
        weights = [jnp.exp(a - top) for a in tops]
        total = jnp.where(lanes < 2 * pairs, 0.0, 1.0)
        for w, ref in zip(weights, stats, strict=True):
            total = total + w * pltpu.roll(ref[rows], 120, 1)
        weights = [jnp.where(lanes < 2 * pairs, w / total, 0.0) for w in weights]
        v["scales"] = weights[0]
        for i, w in enumerate(weights[1:], 1):
            v["scales"] = v["scales"] + pltpu.roll(w, 8 * i, 1)
        v["o"] = []
        for g in range(pairs):
            at = slice(g * 128, g * 128 + 128)
            value = jnp.zeros((chunk, 128), f32)
            for i, w in enumerate(weights):
                value = value + accs[i][rows, at] * jnp.where(lanes < 64, w[:, 2 * g : 2 * g + 1], w[:, 2 * g + 1 : 2 * g + 2])
            v["o"].append(value)
            mixed_all[rows, at] = value.astype(bf16)
        pos = ids[0] * t + rows.start + iota((chunk, 1), 0)
        v["g"] = cot[rows].astype(f32) * (pos < last).astype(f32)
        gb_all[rows] = v["g"].astype(bf16)

    def norm(v):
        rows = v["rows"]
        v["h1"] = x[rows].astype(f32) + nn(mixed_all[rows], wo[...])
        v["s2"] = lax.rsqrt(jnp.mean(v["h1"] * v["h1"], axis=-1, keepdims=True) + EPS)
        v["hat"] = v["h1"] * v["s2"]
        n2_all[rows] = (v["hat"] * g2).astype(bf16)

    def project(v):
        rows = v["rows"]
        v["gate"], v["up"] = nn(n2_all[rows], wg[...]), nn(n2_all[rows], wu[...])
        v["du"] = nt(gb_all[rows], wd[...]).astype(bf16).astype(f32)

    def activate(v):
        rows, gate, up = v["rows"], v["gate"], v["up"]
        c0 = 0.7978845608028654
        square = gate * gate
        th = jnp.tanh(c0 * gate * (1.0 + 0.044715 * square))
        half = 0.5 * (1.0 + th)
        act = gate * half
        dact = half + 0.5 * gate * (1.0 - th * th) * (c0 * (1.0 + 3 * 0.044715 * square))
        u_all[rows] = (act * up).astype(bf16)
        dg_all[rows] = (v["du"] * up * dact).astype(bf16)
        du_all[rows] = (v["du"] * act).astype(bf16)

    def down(v):
        rows = v["rows"]
        out[rows] = (v["h1"] + nn(u_all[rows], wd[...])).astype(bf16)
        v["dn2"] = nt(dg_all[rows], wg[...]) + nt(du_all[rows], wu[...])

    def norm_back(v):
        rows, dn2, hat, s2 = v["rows"], v["dn2"], v["hat"], v["s2"]
        v["gn"] = jnp.sum(dn2 * hat, axis=0, keepdims=True)
        scaled = dn2 * g2
        dh1 = v["g"] + s2 * (scaled - hat * jnp.mean(hat * scaled, axis=-1, keepdims=True))
        dh[rows] = dh1
        dh_all[rows] = dh1.astype(bf16)

    def mix_back(v):
        rows = v["rows"]
        dmix = nt(dh_all[rows], wo[...]).astype(bf16)
        do[rows] = dmix
        scales = v["scales"]
        for h in range(2 * pairs):
            at = slice(h // 2 * 128, h // 2 * 128 + 128)
            product = dmix[:, at].astype(f32) * v["o"][h // 2]
            own = jnp.where((lanes < 64) == (h % 2 == 0), product, 0.0)
            scales = jnp.where(lanes == 64 + h, jnp.sum(own, axis=1, keepdims=True), scales)
        scale[rows] = scales

    def weights_kernel():
        low = tn(u_all[...], gb_all[...]).astype(bf16)
        grads[2 * d : 3 * d, :d] = low[:d]
        grads[2 * d : 3 * d, d:] = low[d:]
        grads[0:d] = tn(n2_all[...], dg_all[...]).astype(bf16)
        grads[d : 2 * d] = tn(n2_all[...], du_all[...]).astype(bf16)

    stages = [weigh, norm, project, activate, down, norm_back, mix_back]
    for step in range(len(stages) + FFN_CHUNKS - 1):
        for c, v in enumerate(work):
            if 0 <= step - c < len(stages):
                stages[step - c](v)
        if step == 3 + FFN_CHUNKS - 1:
            weights_kernel()
    gn[...] = sum(v["gn"] for v in work)
    gwo[...] = tn(mixed_all[...], dh_all[...]).astype(bf16)
    rows = keep.shape[0]
    keep[...] = grads[pl.ds(pl.multiple_of(ids[1] * rows, 16), rows)]
    send[...] = grads[pl.ds(pl.multiple_of((1 - ids[1]) * rows, 16), rows)]


def feed_forward(ids, lens, gain, x, wo, wg, wu, wd, cot, parts):
    t, d = x.shape
    ff, w = wg.shape[1], wo.shape[0]
    half = 3 * d // 2
    return call(
        partial(feed_forward_kernel, len(parts)), "feed_forward", 8,
        [shape(t, d), shape(t, d, dtype=f32), shape(t, w), shape(t, 128, dtype=f32), shape(w, d),
         shape(half, ff), shape(half, ff), shape(1, d, dtype=f32)],
        (ids, lens), (gain, x, wo, wg, wu, wd, cot, *[v["acc"] for v in parts], *[v["stat"] for v in parts]),
        scratch=[pltpu.VMEM((3 * d, ff), bf16)]
        + [pltpu.VMEM((t, k), bf16) for k in (w, d, ff, d, ff, ff, d)],
    )


def attend_back_kernel(n, pairs, counts, ids, q, do, scale, *refs):
    phases, size = len(counts), len(pairs)
    p = [refs[i * size : (i + 1) * size] for i in range(phases)]
    refs = refs[phases * size :]
    kv = [refs[i * size : (i + 1) * size] for i in range(phases)]
    e, refs = refs[phases * size : phases * size + phases], refs[phases * size + phases :]
    dk, dv, refs = refs[:size], refs[size : 2 * size], refs[2 * size :]
    dq, line, ds = refs
    me = ids[0]
    t = q.shape[0]
    lower = low_half(t)
    back = (iota((t, t), 0) + iota((t, t), 1) == t - 1).astype(f32).astype(bf16)
    lane = iota((1, 128), 1)
    line[...] = jnp.zeros_like(line)
    slots = [(i, j) for i, count in enumerate(counts) for j in range(count)]

    def operands(k):
        h = 2 * pairs[k // 2] + k % 2
        at = slice(h // 2 * 128, h // 2 * 128 + 128)
        qt = jnp.where(lower == (k % 2 == 0), q[:, at].astype(f32), 0.0).T
        doh = jnp.where(lower == (k % 2 == 1), turn(do[:, at].astype(f32)), 0.0)
        out = []
        for i in range(phases):
            factor = scale[:, 8 * i + h : 8 * i + h + 1]
            scaled = doh * factor
            shift = scale[:, 64 + h : 65 + h] * factor
            out.append((scaled.astype(bf16), shift, jnp.concatenate([qt, scaled.T], axis=1).astype(bf16)))
        return out

    def start(k, s, ops):
        i, j = slots[s]
        return nt(ops[i][0], kv[i][k // 2][k % 2, j * t : (j + 1) * t])

    def finish(k, s, ops, d_prob, acc):
        i, j = slots[s]
        rows = slice(j * t, (j + 1) * t)
        probs = p[i][k // 2][k % 2, :, rows]
        d_score = (probs.astype(f32) * (d_prob - ops[i][1])).astype(bf16)
        ds[k % 2, :, s * t : (s + 1) * t] = d_score
        more = nn(d_score, jnp.concatenate([kv[i][k // 2][k % 2, rows], e[i][rows]], axis=1))
        both = nn(ops[i][2], jnp.concatenate([d_score, probs], axis=0)).astype(bf16)
        mine, other = (both[:64], both[64:]) if k % 2 == 0 else (both[64:], both[:64])
        dk[k // 2][k % 2 * 64 : k % 2 * 64 + 64, s * t : (s + 1) * t] = mine
        dv[k // 2][k % 2 * 64 : k % 2 * 64 + 64, s * t : (s + 1) * t] = other
        return more if acc is None else acc + more

    def bias(k, acc):
        parts = []
        for r in (-1, 0, 1):
            there = me + r
            inside = (there >= 0) & (there < n)
            slot = jnp.where(inside, me ^ there, 0)
            block = ds[k % 2, :, pl.ds(pl.multiple_of(slot * t, t), t)]
            parts.append(nn(back, block) * inside.astype(f32))
        parts.append(jnp.zeros((t, t), f32))
        band = pltpu.roll(jnp.concatenate(parts, axis=1), 0, 1, stride=1, stride_axis=0)
        line[k : k + 1, : 4 * t] = jnp.sum(band, axis=0, keepdims=True)
        ends = jnp.sum(acc[:, 128:], axis=0, keepdims=True)
        line[k : k + 1, 4 * t :] = jnp.where((lane == LEFT) | (lane == RIGHT), ends, 0.0)

    tasks = [(k, s) for k in range(2 * size) for s in range(len(slots))]
    ops = [operands(0)]
    d_prob = start(0, 0, ops[0])
    accs = [None] * (2 * size)
    for index, (k, s) in enumerate(tasks):
        if s == 0 and k + 1 < 2 * size:
            ops.append(operands(k + 1))
        later = None
        if index + 1 < len(tasks):
            k2, s2 = tasks[index + 1]
            later = start(k2, s2, ops[k2])
        accs[k] = finish(k, s, ops[k], d_prob, accs[k])
        d_prob = later
        if s == len(slots) - 1:
            bias(k, accs[k])
    for g in range(size):
        dq[:, g * 128 : g * 128 + 128] = jnp.where(lower, accs[2 * g][:, :128], accs[2 * g + 1][:, :128]).astype(bf16)


def attend_back(n, pairs, ids, q, do, scale, parts):
    t = q.shape[0]
    widths = [v["e"].shape[0] for v in parts]
    s = sum(widths)
    size = len(pairs)
    out = call(
        partial(attend_back_kernel, n, pairs, [w // t for w in widths]), "attend_back", 4 * size,
        [shape(128, s)] * (2 * size) + [shape(t, 128 * size), shape(8, 4 * t + 128, dtype=f32)],
        (ids,), (q, do, scale, *[v["p"][g] for v in parts for g in pairs],
                 *[v["kv"][g] for v in parts for g in pairs], *[v["e"] for v in parts]),
        scratch=[pltpu.VMEM((2, t, s), bf16)], much=n > 8,
    )
    return dict(dk=out[:size], dv=out[size : 2 * size], dq=out[-2], line=out[-1], pairs=size)


def gather_back_kernel(n, buckets, counts, pairs, ids, gain, gn, gwo, wq, wk, wv, wt, *refs):
    phases = len(counts)
    n1, refs = refs[:phases], refs[phases:]
    total_pairs = sum(pairs)
    dkv, refs = refs[: 2 * total_pairs], refs[2 * total_pairs :]
    dq, lines = refs[: len(pairs)], refs[len(pairs) : 2 * len(pairs)]
    even, odd, dn1q, keep, send, grads, sums, diagonal = refs[2 * len(pairs) :]
    d, w = wq.shape
    t = dn1q.shape[0]
    weights = jnp.concatenate([wk[...], wv[...]], axis=1)
    total = jnp.zeros((2 * w, d), f32)
    slot = 0
    for i, count in enumerate(counts):
        begin = sum(counts[:i]) * t
        both = jnp.concatenate([ref[:, begin : begin + count * t] for ref in dkv], axis=0)
        total = total + nn(both, n1[i][...])
        back = nn(weights, both).astype(bf16)
        for _ in range(count):
            ref = odd if slot % 2 else even
            ref[slot // 2] = back[:, slot * t - begin : slot * t - begin + t]
            slot += 1
    dq_all = jnp.concatenate([ref[...] for ref in dq], axis=1)
    from_q = tn(dq_all, n1[0][:t])
    dn1q[...] = nt(dq_all, wq[...])
    grads[:w] = from_q.astype(bf16)
    grads[w : 3 * w] = total.astype(bf16)
    grads[3 * w :] = gwo[...]
    gains = jnp.sum(from_q * wt[:w].astype(f32), axis=0, keepdims=True)
    gains = gains + jnp.sum(total * wt[w:].astype(f32), axis=0, keepdims=True)
    sums[...] = jnp.zeros_like(sums)
    sums[0:1] = gains / gain[...].astype(f32)
    sums[1:2] = gn[...]
    diagonal[...] = jnp.zeros_like(diagonal)
    begin = 0
    for ref, count in zip(lines, pairs, strict=True):
        diagonal[begin : begin + 2 * count] = ref[: 2 * count]
        begin += 2 * count
    width = diagonal.shape[1]
    u = iota((width, 128), 0)
    bucket = bucket_of(u - (2 * t - 1), buckets)
    bucket = jnp.where(u == 4 * t + LEFT, buckets // 2 - 1, jnp.where(u == 4 * t + RIGHT, buckets - 1, bucket))
    pick = (bucket == iota((width, 128), 1)).astype(f32)
    sums[8:16, :128] = lax.dot_general(diagonal[...], pick, (((1,), (0,)), ((), ())),
                                       precision=lax.Precision.HIGHEST, preferred_element_type=f32)
    small = sums[...].astype(bf16)
    rows = 2 * w
    keep[:rows] = grads[pl.ds(pl.multiple_of(ids[1] * rows, 16), rows)]
    send[:rows] = grads[pl.ds(pl.multiple_of((1 - ids[1]) * rows, 16), rows)]
    keep[rows:] = small
    send[rows:] = small


def gather_back(n, buckets, ids, gain, gn, gwo, wq, wk, wv, wt, parts, backs):
    d, w = wq.shape
    t = backs[0]["dq"].shape[0]
    pairs = [v["pairs"] for v in backs]
    counts = [v["e"].shape[0] // t for v in parts]
    pieces = [ref for v in backs for ref in v["dk"]] + [ref for v in backs for ref in v["dv"]]
    half = 2 * w + SMALL
    return call(
        partial(gather_back_kernel, n, buckets, counts, pairs), "gather_back", 6,
        [shape(n // 2, d, t), shape(n // 2, d, t), shape(t, d, dtype=f32), shape(half, d), shape(half, d)],
        (ids,), (gain, gn, gwo, wq, wk, wv, wt, *[v["n1"] for v in parts], *pieces, *[v["dq"] for v in backs],
                 *[v["line"] for v in backs]),
        scratch=[pltpu.VMEM((4 * w, d), bf16), pltpu.VMEM((SMALL, d), f32), pltpu.VMEM((8, 4 * t + 128), f32)], much=n > 8,
    )


def split_kernel(which, count, extra, ids, *refs):
    inputs, outs = refs[:-count], refs[-count:]
    rows = (inputs[0].shape[0] - extra) // count
    own = ids[which]
    for j in range(count):
        at = pl.ds(pl.multiple_of((own ^ j) * rows, 16), rows)
        total = inputs[0][at].astype(f32)
        for ref in inputs[1:]:
            total = total + ref[at].astype(f32)
        outs[j][:rows] = total.astype(bf16)
    if extra:
        at = pl.ds(rows * count, extra)
        total = inputs[0][at].astype(f32)
        for ref in inputs[1:]:
            total = total + ref[at].astype(f32)
        for j in range(count):
            outs[j][rows:] = total.astype(bf16)


def add_and_split(which, count, extra, ids, *arrays):
    rows = (arrays[0].shape[0] - extra) // count + extra
    out = shape(rows, arrays[0].shape[1])
    return call(partial(split_kernel, which, count, extra), "add_parts", 1, [out] * count, (ids,), arrays)


def by_chip_kernel(ids, keep, recv, *outs):
    rows = keep.shape[0] // 4
    for half, own in ((0, ids[2] % 2), (1, ids[2] // 2)):
        for j in range(2):
            at = pl.ds(pl.multiple_of((2 * half + (own ^ j)) * rows, 16), rows)
            outs[2 * half + j][...] = (keep[at].astype(f32) + recv[at].astype(f32)).astype(bf16)


def by_next_chip_kernel(ids, keep_x, recv_x, keep_y, recv_y, *outs):
    rows = keep_x.shape[0] // 2
    for half, own, a, b in ((0, ids[2] // 2, keep_x, recv_x), (1, ids[2] % 2, keep_y, recv_y)):
        for j in range(2):
            at = pl.ds(pl.multiple_of((own ^ j) * rows, 16), rows)
            outs[2 * half + j][...] = (a[at].astype(f32) + b[at].astype(f32)).astype(bf16)


def by_row_kernel(ids, keep_x, recv_x, keep_y, recv_y, mine, other):
    first = keep_x[...].astype(f32) + recv_x[...].astype(f32)
    second = keep_y[...].astype(f32) + recv_y[...].astype(f32)
    even = ids[3] % 2 == 0
    mine[...] = jnp.where(even, first, second).astype(bf16)
    other[...] = jnp.where(even, second, first).astype(bf16)


def pick_kernel(ids, mine, other, first, second):
    even = ids[3] % 2 == 0
    a, b = mine[...].astype(f32), other[...].astype(f32)
    first[...] = jnp.where(even, a, b).astype(bf16)
    second[...] = jnp.where(even, b, a).astype(bf16)


def join_kernel(ids, a, b, c, d, first, second):
    rows = a.shape[0]
    first[:rows], first[rows:] = a[...], b[...]
    second[:rows], second[rows:] = c[...], d[...]


def swap(array, axis, j):
    size = lax.axis_size(axis)
    return lax.ppermute(array, axis, [(i, i ^ j) for i in range(size)])


def order(first, *values):
    first, values = lax.optimization_barrier((first, values))
    return values if len(values) > 1 else values[0]


def sum_all(ids, keep, recv, extra):
    both = add_and_split(0, 1, extra, ids * 0, keep, recv)[0].astype(f32)
    size = both.shape[0] - extra
    placed = jnp.zeros((2 * size, both.shape[1]), f32)
    placed = lax.dynamic_update_slice_in_dim(placed, both[:size], ids[1] * size, 0)
    full, tail = lax.psum((placed, both[size:] * 0.5), ("rows", "seq"))
    mine = lax.dynamic_slice_in_dim(full, ids[1] * size, size, 0)
    other = lax.dynamic_slice_in_dim(full, (1 - ids[1]) * size, size, 0)
    return [mine.astype(bf16)], [other.astype(bf16)], tail.astype(bf16)


def to_chips(parts):
    return [parts[0]] + [swap(parts[j], "seq", 2 * j) for j in range(1, len(parts))]


def place_halves(ids, mine, other, full):
    size = full.shape[0] // 2
    if len(mine) == 1:
        full[pl.ds(pl.multiple_of(ids[1] * size, 16), size)] = mine[0][...]
        full[pl.ds(pl.multiple_of((1 - ids[1]) * size, 16), size)] = other[0][...]
        return
    piece = size // len(mine)
    for c, refs in ((ids[1], mine), (1 - ids[1], other)):
        for a, ref in enumerate(refs):
            at = c * size + (ids[2] ^ a) * piece
            for b in range(2):
                where = at + ((ids[3] % 2) ^ b) * (piece // 2)
                full[pl.ds(pl.multiple_of(where, 16), piece // 2)] = ref[b * (piece // 2) : (b + 1) * (piece // 2)]


def unpack_ffn_kernel(pieces, ids, *refs):
    gate, up, down, full = refs[2 * pieces :]
    size = full.shape[0] // 2
    x, y = ids[2] % 2, ids[2] // 2
    for c, parts in ((ids[1], refs[:pieces]), (1 - ids[1], refs[pieces : 2 * pieces])):
        if pieces == 1:
            full[pl.ds(pl.multiple_of(c * size, 16), size)] = parts[0][...]
            continue
        rows = size // 8
        for half, first, second in ((0, x, y), (1, y, x)):
            for a in range(2):
                for b in range(2):
                    where = c * size + (4 * half + 2 * (first ^ a) + (second ^ b)) * rows
                    piece = parts[2 * half + a][b * rows : (b + 1) * rows]
                    full[pl.ds(pl.multiple_of(where, 16), rows)] = piece
    d = gate.shape[0]
    gate[...] = full[:d].astype(f32)
    up[...] = full[d : 2 * d].astype(f32)
    down[:d] = full[2 * d :, :d].astype(f32)
    down[d:] = full[2 * d :, d:].astype(f32)


def unpack_attention_kernel(pieces, ids, *refs):
    gq, gk, gv, go, full = refs[2 * pieces :]
    place_halves(ids, refs[:pieces], refs[pieces : 2 * pieces], full)
    w = gq.shape[1]
    for k, ref in enumerate((gq, gk, gv)):
        ref[...] = full[k * w : (k + 1) * w].astype(f32).T
    go[...] = full[3 * w :].astype(f32)


def unpack_small_kernel(ids, tail, g1, g2, gb):
    small = tail[...].astype(f32)
    g1[...] = small[0:1]
    g2[...] = small[1:2]
    gb[...] = small[8 : 8 + gb.shape[0], : gb.shape[1]]


def input_grad_kernel(ids, *refs):
    *parts, dn1q, x, dh, gain, out = refs
    total = parts[0][...].astype(f32)
    for ref in parts[1:]:
        total = total + ref[...].astype(f32)
    dn1 = total.T + dn1q[...]
    value = x[...].astype(f32)
    s1 = lax.rsqrt(jnp.mean(value * value, axis=-1, keepdims=True) + EPS)
    hat = value * s1
    scaled = dn1 * gain[...].astype(f32)
    out[...] = dh[...] + s1 * (scaled - hat * jnp.mean(hat * scaled, axis=-1, keepdims=True))


def slots_kernel(count, ids, mine, other, *outs):
    for j in range(count):
        outs[j][...] = (mine[j].astype(f32) + other[j].astype(f32)).astype(bf16)


def shards(
    tokens, norm_attn, query_weight, key_weight, value_weight, out_weight, bucket_bias_table, norm_ffn,
    gate_weight, expansion_matrix, down_weight, lengths, cotangent,
):
    _, t, d = tokens.shape
    n = lax.axis_size("seq")
    buckets, heads = bucket_bias_table.shape
    width = query_weight.shape[1]
    ff = gate_weight.shape[1]
    seq = lax.axis_index("seq")
    ids = jnp.stack([seq, seq % 2, seq // 2, lax.axis_index("rows")]).astype(i32)
    x = tokens.reshape(t, d)
    cot = cotangent.reshape(t, d)
    lens = lengths.reshape(-1)
    gain1 = norm_attn.reshape(1, d)
    gain2 = norm_ffn.reshape(1, d)

    blocks = [None] * n
    blocks[0], blocks[1] = x, swap(x, "seq", 1)
    for j in range(2, n, 2):
        blocks[j] = swap(x, "seq", j)
    q, ext, bands, wt, line, x, wq, wk, wv = prepare(
        ids, lens, x, gain1, bucket_bias_table.T, query_weight, key_weight, value_weight
    )
    blocks[0] = x
    cuts = [0, 2, *range(8, n, 8), n]

    def phase(a, b):
        return attend(n, a, ids, lens, blocks[a:b], gain1, wk, wv, q, ext, bands, line)

    parts = [phase(0, 2)]
    for j in range(2, n, 2):
        blocks[j] = order(parts[0]["acc"], blocks[j])
        blocks[j + 1] = swap(blocks[j], "seq", 1)
    parts += [phase(a, b) for a, b in zip(cuts[1:-1], cuts[2:], strict=True)]
    output, dh, do, scale, gwo, keep, send, gn = feed_forward(
        ids, lens, gain2, x, out_weight, gate_weight, expansion_matrix, down_weight, cot, parts
    )
    half = n // 2
    pairs = width // 128
    whole = n != 8 or lax.axis_size("rows") != 4
    zero, near = ids * 0, ids[3:4] % 2

    def unpack_ffn(mine, other):
        return call(
            partial(unpack_ffn_kernel, len(mine)), "unpack_ffn", 4,
            [shape(d, ff, dtype=f32), shape(d, ff, dtype=f32), shape(ff, d, dtype=f32)],
            (ids,), (*mine, *other), scratch=[pltpu.VMEM((3 * d, ff), bf16)],
        )

    def unpack_attention(mine, other):
        return call(
            partial(unpack_attention_kernel, len(mine)), "unpack_attention", 3,
            [shape(d, width, dtype=f32)] * 3 + [shape(width, d, dtype=f32)],
            (ids,), (*mine, *other), scratch=[pltpu.VMEM((4 * width, d), bf16)],
        )

    def unpack_small(tail):
        return call(unpack_small_kernel, "unpack_small", 1,
                    [shape(1, d, dtype=f32)] * 2 + [shape(heads, buckets, dtype=f32)], (ids,), (tail,))

    def input_grad(slots):
        return call(input_grad_kernel, "input_grad", 2, shape(t, d, dtype=f32), (ids,), (*slots, dn1q, x, dh, gain1))

    def add_slots(recv):
        return call(partial(slots_kernel, half), "add_slots", 1, [shape(d, t)] * half, (ids,), (even, recv))

    f_core = swap(send, "seq", 1)
    backs = [attend_back(n, [0], ids, q, do, scale, parts)]
    f_keep = keep
    part = lambda rows: shape(f_keep.shape[0] // rows, ff)
    if not whole:
        f_core = order(backs[0]["dq"], f_core)
        f_x, f_x2, f_y, f_y2 = call(by_chip_kernel, "add_parts", 1, [part(4)] * 4, (ids,), (keep, f_core))
        do = order(f_x, do)
        f_x2, f_y2 = swap(f_x2, "seq", 2), swap(f_y2, "seq", 4)
    backs.append(attend_back(n, list(range(1, pairs)), ids, q, do, scale, parts))
    even, odd, dn1q, keep, send = gather_back(
        n, buckets, ids, gain1, gn, gwo, wq, wk, wv, wt, parts, backs
    )
    if not whole:
        send, odd = order((f_x2, f_y2), send, odd)
    a_core, d_core = swap(send, "seq", 1), swap(odd, "seq", 1)
    if whole:
        mine, other, _ = sum_all(ids, f_keep, f_core, 0)
        gate, up, down = unpack_ffn(mine, other)
        grad_tokens = input_grad(to_chips(add_slots(d_core)))
        mine, other, tail = sum_all(ids, keep, a_core, SMALL)
        gq, gk, gv, go = unpack_attention(mine, other)
        g1, g2, gb = unpack_small(tail)
    else:
        f_x, f_x2, f_y, f_y2 = call(
            by_next_chip_kernel, "add_parts", 1, [part(8)] * 4, (ids,), (f_x, f_x2, f_y, f_y2)
        )
        f_x2, f_y2 = swap(f_x2, "seq", 4), swap(f_y2, "seq", 2)
        a_core = order(f_x, a_core)
        a_parts = to_chips(add_and_split(2, half, SMALL, ids, keep, a_core))
        f_x2, f_y2 = order(a_parts[0], f_x2, f_y2)
        f_mine, f_other = call(by_row_kernel, "add_parts", 1, [part(8)] * 2, (ids,), (f_x, f_x2, f_y, f_y2))
        f_other = swap(f_other, "rows", 1)
        d_core = order(f_mine, d_core)
        d_parts = add_slots(d_core)
        f_other = order(d_parts, f_other)
        f_mine = add_and_split(0, 1, 0, zero, f_mine, f_other)[0]
        f_other = swap(f_mine, "rows", 2)
        d_parts = to_chips(order(f_mine, d_parts))
        a_parts = order(f_mine, a_parts)
        a_mine, a_other = add_and_split(0, 2, SMALL, near, *a_parts)
        a_other = swap(a_other, "rows", 1)
        f_other = order(a_mine, f_other)
        f_mine = add_and_split(0, 1, 0, zero, f_mine, f_other)[0]
        f_other = swap(f_mine, "rows", 1)
        a_other = order(f_mine, a_other)
        a_mine = add_and_split(0, 1, SMALL, zero, a_mine, a_other)[0]
        a_other = swap(a_mine, "rows", 2)
        f_other = order(a_mine, f_other)
        f_x, f_y = call(pick_kernel, "pick", 1, [part(8)] * 2, (ids,), (f_mine, f_other))
        f_x2, f_y2 = swap(f_x, "seq", 4), swap(f_y, "seq", 2)
        a_other = order(f_x, a_other)
        a_mine = add_and_split(0, 1, SMALL, zero, a_mine, a_other)[0]
        size = a_mine.shape[0] - SMALL
        a_other = swap(a_mine[:size], "rows", 1)
        d_parts = order(a_mine, d_parts)
        a_other = order(d_parts, a_other)
        a_line = jnp.concatenate([a_mine[:size], a_other], axis=0)
        a_own = [a_line] + [swap(a_line, "seq", 2 * j) for j in range(1, half)]
        grad_tokens = input_grad(order(a_line, d_parts))
        f_x2, f_y2, grad_tokens = order(grad_tokens, f_x2, f_y2, grad_tokens)
        f_x, f_y = call(join_kernel, "join", 1, [part(4)] * 2, (ids,), (f_x, f_x2, f_y, f_y2))
        f_own = [f_x, swap(f_x, "seq", 2), f_y, swap(f_y, "seq", 4)]
        g1, g2, gb = unpack_small(order(f_x, a_mine[size:]))
        a_own, g1 = order(g1, a_own, g1)
        f_own = order(a_own, f_own)
        gate, up, down = unpack_ffn(f_own, [swap(v, "seq", 1) for v in f_own])
        gq, gk, gv, go = unpack_attention(a_own, [swap(v, "seq", 1) for v in a_own])
    return (
        output.reshape(tokens.shape), grad_tokens.reshape(tokens.shape), g1.reshape(d), gq, gk, gv, go, gb.T,
        g2.reshape(d), gate, up, down,
    )


def solution(mesh):
    split = P("rows", "seq", None)
    in_specs = (split,) + (P(),) * 10 + (P("rows", None), split)
    out_specs = (split, split) + (P(),) * 10
    return jax.shard_map(shards, mesh=mesh, in_specs=in_specs, out_specs=out_specs, check_vma=False)
```

```python
from functools import partial

import jax
import jax.numpy as jnp
from jax import lax
from jax.experimental import pallas as pl
from jax.experimental.pallas import tpu as pltpu
from jax.sharding import PartitionSpec as P

EPS = 1e-6
BIG = -(2.0**30)
LEFT, RIGHT, ONES = 17, 18, 19
PIECE = 32
FFN_CHUNKS = 1
STEPS = """
    a_chips f_rows f_z0 a_rows d_slots f_z1 f_pick a_z0 d:3 d_out a_z1 f_join a_stack f_near small a_swap f_swap last
"""
SMALL = 16
VMEM = 24 * 1024 * 1024
MUCH = 56 * 1024 * 1024

f32, bf16, i32 = jnp.float32, jnp.bfloat16, jnp.int32


def thresholds(buckets, max_distance):
    half = buckets // 2
    exact = half // 2
    steps = half - exact
    out = list(range(1, exact))
    for j in range(steps):
        target = exact ** (steps - j) * max_distance**j
        m = exact
        while m**steps < target:
            m += 1
        out.append(m)
    return out


def bucket_of(offset, buckets):
    distance = jnp.abs(offset)
    bucket = (offset > 0).astype(i32) * (buckets // 2)
    for t in thresholds(buckets, 128):
        bucket = bucket + (distance >= t).astype(i32)
    return bucket


def nn(a, b):
    return lax.dot_general(a, b, (((1,), (0,)), ((), ())), preferred_element_type=f32)


def nt(a, b):
    return lax.dot_general(a, b, (((1,), (1,)), ((), ())), preferred_element_type=f32)


def tn(a, b):
    return lax.dot_general(a, b, (((0,), (0,)), ((), ())), preferred_element_type=f32)


def iota(shape, dim):
    return lax.broadcasted_iota(i32, shape, dim)


def rms(values, gain):
    scale = lax.rsqrt(jnp.mean(values * values, axis=-1, keepdims=True) + EPS)
    return values * scale * gain


def call(kernel, name, us, out_shape, smem_args, args, scratch=(), much=False, anywhere=0):
    smem = pl.BlockSpec(memory_space=pltpu.SMEM)
    vmem = pl.BlockSpec(memory_space=pltpu.VMEM)
    return pl.pallas_call(
        kernel,
        in_specs=[smem] * len(smem_args) + [vmem] * (len(args) - anywhere) + [pl.BlockSpec(memory_space=pltpu.HBM)] * anywhere,
        out_specs=jax.tree.map(lambda _: vmem, out_shape),
        out_shape=out_shape,
        scratch_shapes=list(scratch),
        compiler_params=pltpu.CompilerParams(vmem_limit_bytes=MUCH if much else VMEM),
        cost_estimate=pl.CostEstimate(flops=int(us * 1e6), bytes_accessed=int(us * 2e3), transcendentals=0),
        name=name,
    )(*smem_args, *args)


def shape(*dims, dtype=bf16):
    return jax.ShapeDtypeStruct(dims, dtype)


def low_half(t):
    return iota((t, 128), 1) < 64


def turn(pair):
    return pltpu.roll(pair, 64, 1)


def prepare_kernel(ids, lens, gain, table, x, wq, wk, wv, q, ext, bands, wt, line, x_here, wq_here, wk_here, wv_here, sems):
    pairs = ((x, x_here), (wq, wq_here), (wk, wk_here), (wv, wv_here))
    copies = [pltpu.make_async_copy(a, b, sems.at[i]) for i, (a, b) in enumerate(pairs)]
    for copy in copies:
        copy.start()
    t = x.shape[0]
    heads, buckets = table.shape
    low, high = segment_bounds(lens)
    lanes = iota((t, 128), 1)
    pos = iota((t, 128), 0) + ids[0] * t
    other = jnp.where((pos >= low) & (pos < high), 0.0, BIG)
    ext[...] = jnp.where(lanes < LEFT, other, 0.0)
    u = iota((buckets, 4 * t), 1)
    bucket = bucket_of(jnp.where(u < 3 * t, u - t, u - 5 * t), buckets)
    pick = (bucket == iota((buckets, 4 * t), 0)).astype(f32).astype(bf16)
    line[...] = jnp.zeros_like(line)
    line[:heads] = nn(table[...], pick)
    for h in range(heads):
        band = pltpu.roll(jnp.broadcast_to(line[h : h + 1], (t, 4 * t)), 0, 1, stride=1, stride_axis=0)
        for r in range(3):
            bands[h, r] = band[:, r * t : (r + 1) * t].astype(bf16)
        bands[h, 3] = jnp.zeros((t, t), bf16)
    for copy in copies:
        copy.wait()
    n1 = rms(x_here[...].astype(f32), gain[...].astype(f32)).astype(bf16)
    q[...] = nn(n1, wq_here[...]).astype(bf16)
    w = wq.shape[1]
    for k, ref in enumerate((wq_here, wk_here, wv_here)):
        wt[k * w : (k + 1) * w] = ref[...].astype(f32).T.astype(bf16)


def prepare(ids, lens, x, gain, table, wq, wk, wv):
    t, d = x.shape
    heads, w = table.shape[0], wq.shape[1]
    return call(
        prepare_kernel, "prepare", 4,
        [shape(t, w), shape(t, 128, dtype=f32), shape(heads, 4, t, t), shape(3 * w, d), shape(8, 4 * t, dtype=f32),
         shape(t, d), shape(d, w), shape(d, w), shape(d, w)],
        (ids, lens), (gain, table, x, wq, wk, wv), anywhere=4, scratch=[pltpu.SemaphoreType.DMA((4,))],
    )


def segment_bounds(lens):
    lane = iota((1, 128), 1)
    low = jnp.where(lane == 0, -1, 2**30)
    high = jnp.full((1, 128), -1, i32)
    total = 0
    for k in range(lens.shape[0]):
        total = total + lens[k]
        high = jnp.where(lane == k, total, high)
        low = jnp.where(lane == k + 1, total, low)
    return low, jnp.where(lane == lens.shape[0], 2**30, high)


def attend_kernel(n, first, count, ids, lens, *refs):
    x = refs[:count]
    gain, wk, wv, q, ext, bands, line, n1, e, acc, stat = refs[count : count + 11]
    pairs = q.shape[1] // 128
    kv, p = refs[count + 11 : count + 11 + pairs], refs[count + 11 + pairs : -1]
    s = refs[-1]
    me = ids[0]
    t = x[0].shape[0]
    low, high = segment_bounds(lens)
    row = iota((t, 128), 0)
    lanes = iota((t, 128), 1)
    for i in range(count):
        at = slice(i * t, (i + 1) * t)
        n1[at] = rms(x[i][...].astype(f32), gain[...].astype(f32)).astype(bf16)
        block = me ^ (first + i)
        pos = row + block * t
        away = block - me
        flag = jnp.where(away <= -2, LEFT, jnp.where(away >= 2, RIGHT, ONES))
        here = ((pos >= low) & (pos < high)) | (lanes == flag) | (lanes == ONES)
        e[at] = here.astype(f32).astype(bf16)
    upper = iota((t, 128), 1) >= 64
    near = [i for i in range(count) if (first + i) & (first + i + 1) == 0]

    def project(g, i):
        rows, at = slice(i * t, (i + 1) * t), slice(g * 128, g * 128 + 128)
        both = nn(n1[rows], jnp.concatenate([wk[:, at], wv[:, at]], axis=1))
        keys, values = both[:, :128], turn(both[:, 128:])
        kv[g][0, rows] = jnp.where(upper, values, keys).astype(bf16)
        kv[g][1, rows] = jnp.where(upper, keys, values).astype(bf16)

    def query(h):
        lane_ext = jnp.where(lanes == LEFT, line[h : h + 1, 0:1],
                             jnp.where(lanes == RIGHT, line[h : h + 1, 3 * t - 1 : 3 * t], ext[...]))
        q2 = q[:, h // 2 * 128 : h // 2 * 128 + 128].astype(f32)
        return jnp.concatenate([jnp.where(upper == (h % 2 == 1), q2, 0.0), lane_ext], axis=1).astype(bf16)

    def keys_of(h, i):
        rows = slice(i * t, (i + 1) * t)
        return jnp.concatenate([kv[h // 2][h % 2, rows], e[rows]], axis=1)

    def score(h, i, qa, top):
        block = nt(qa, keys_of(h, i))
        if i in near:
            away = (me ^ (first + i)) - me
            block = block + bands[h, jnp.where(jnp.abs(away) <= 1, away + 1, 3)].astype(f32)
        s[h % 2, :, i * t : (i + 1) * t] = block
        here = block[:, :128]
        for c in range(1, t // 128):
            here = jnp.maximum(here, block[:, c * 128 : (c + 1) * 128])
        return here if top is None else jnp.maximum(top, here)

    def mix(h, i, top, out):
        raised = jnp.exp(s[h % 2, :, i * t : (i + 1) * t] - top).astype(bf16)
        p[h // 2][h % 2, :, i * t : (i + 1) * t] = raised
        more = nn(raised, keys_of(h, i))
        return more if out is None else out + more

    for i in range(count):
        project(0, i)
    stats = jnp.zeros((t, 128), f32)
    last = None
    sums = []
    for h in range(2 * pairs + 1):
        qa = query(h) if h < 2 * pairs else None
        top = out = None
        for i in range(count):
            if h < 2 * pairs:
                top = score(h, i, qa, top)
            if h > 0:
                out = mix(h - 1, i, last, out)
            if h % 2 == 1 and h // 2 + 1 < pairs:
                project(h // 2 + 1, i)
        if h > 0:
            stats = jnp.where(lanes == h - 1, last, stats)
            stats = jnp.where(lanes == 7 + h, out[:, 128 + ONES : 129 + ONES], stats)
            sums.append(out[:, :128])
        if h < 2 * pairs:
            last = jnp.max(top, axis=1, keepdims=True)
    for g in range(pairs):
        acc[:, g * 128 : g * 128 + 128] = turn(jnp.where(upper, sums[2 * g], sums[2 * g + 1]))
    stat[...] = stats


def attend(n, first, ids, lens, blocks, gain, wk, wv, q, ext, bands, line):
    count = len(blocks)
    t, d = blocks[0].shape
    pairs = wk.shape[1] // 128
    c = count * t
    out = call(
        partial(attend_kernel, n, first, count), "attend", 2 * count,
        [shape(c, d), shape(c, 128), shape(t, wk.shape[1], dtype=f32), shape(t, 128, dtype=f32)]
        + [shape(2, c, 128)] * pairs + [shape(2, t, c)] * pairs,
        (ids, lens), (*blocks, gain, wk, wv, q, ext, bands, line), scratch=[pltpu.VMEM((2, t, c), f32)], much=n > 8,
    )
    return dict(n1=out[0], e=out[1], acc=out[2], stat=out[3], kv=out[4 : 4 + pairs], p=out[4 + pairs :])


def feed_forward_kernel(phases, ids, lens, gain, x, wo, wg, wu, wd, cot, *refs):
    accs, stats = refs[:phases], refs[phases : 2 * phases]
    out, dh, do, scale, gwo, keep, send, gn, grads, mixed_all, n2_all, u_all, gb_all, dg_all, du_all, dh_all = refs[2 * phases :]
    t, d = x.shape
    pairs = wo.shape[0] // 128
    chunk = t // FFN_CHUNKS
    lanes = iota((chunk, 128), 1)
    g2 = gain[...].astype(f32)
    last = lens[0]
    for k in range(1, lens.shape[0]):
        last = last + lens[k]
    work = [dict(rows=slice(c * chunk, (c + 1) * chunk)) for c in range(FFN_CHUNKS)]

    def weigh(v):
        rows = v["rows"]
        tops = [ref[rows] for ref in stats]
        top = tops[0]
        for other in tops[1:]:
            top = jnp.maximum(top, other)
        weights = [jnp.exp(a - top) for a in tops]
        total = jnp.where(lanes < 2 * pairs, 0.0, 1.0)
        for w, ref in zip(weights, stats, strict=True):
            total = total + w * pltpu.roll(ref[rows], 120, 1)
        weights = [jnp.where(lanes < 2 * pairs, w / total, 0.0) for w in weights]
        v["scales"] = weights[0]
        for i, w in enumerate(weights[1:], 1):
            v["scales"] = v["scales"] + pltpu.roll(w, 8 * i, 1)
        v["o"] = []
        for g in range(pairs):
            at = slice(g * 128, g * 128 + 128)
            value = jnp.zeros((chunk, 128), f32)
            for i, w in enumerate(weights):
                value = value + accs[i][rows, at] * jnp.where(lanes < 64, w[:, 2 * g : 2 * g + 1], w[:, 2 * g + 1 : 2 * g + 2])
            v["o"].append(value)
            mixed_all[rows, at] = value.astype(bf16)
        pos = ids[0] * t + rows.start + iota((chunk, 1), 0)
        v["g"] = cot[rows].astype(f32) * (pos < last).astype(f32)
        gb_all[rows] = v["g"].astype(bf16)

    def norm(v):
        rows = v["rows"]
        v["h1"] = x[rows].astype(f32) + nn(mixed_all[rows], wo[...])
        v["s2"] = lax.rsqrt(jnp.mean(v["h1"] * v["h1"], axis=-1, keepdims=True) + EPS)
        v["hat"] = v["h1"] * v["s2"]
        n2_all[rows] = (v["hat"] * g2).astype(bf16)

    def project(v):
        rows = v["rows"]
        v["gate"], v["up"] = nn(n2_all[rows], wg[...]), nn(n2_all[rows], wu[...])
        v["du"] = nt(gb_all[rows], wd[...]).astype(bf16).astype(f32)

    def activate(v):
        rows, gate, up = v["rows"], v["gate"], v["up"]
        c0 = 0.7978845608028654
        square = gate * gate
        th = jnp.tanh(c0 * gate * (1.0 + 0.044715 * square))
        half = 0.5 * (1.0 + th)
        act = gate * half
        dact = half + 0.5 * gate * (1.0 - th * th) * (c0 * (1.0 + 3 * 0.044715 * square))
        u_all[rows] = (act * up).astype(bf16)
        dg_all[rows] = (v["du"] * up * dact).astype(bf16)
        du_all[rows] = (v["du"] * act).astype(bf16)

    def down(v):
        rows = v["rows"]
        out[rows] = (v["h1"] + nn(u_all[rows], wd[...])).astype(bf16)
        v["dn2"] = nt(dg_all[rows], wg[...]) + nt(du_all[rows], wu[...])

    def norm_back(v):
        rows, dn2, hat, s2 = v["rows"], v["dn2"], v["hat"], v["s2"]
        v["gn"] = jnp.sum(dn2 * hat, axis=0, keepdims=True)
        scaled = dn2 * g2
        dh1 = v["g"] + s2 * (scaled - hat * jnp.mean(hat * scaled, axis=-1, keepdims=True))
        dh[rows] = dh1
        dh_all[rows] = dh1.astype(bf16)

    def mix_back(v):
        rows = v["rows"]
        dmix = nt(dh_all[rows], wo[...]).astype(bf16)
        do[rows] = dmix
        scales = v["scales"]
        for h in range(2 * pairs):
            at = slice(h // 2 * 128, h // 2 * 128 + 128)
            product = dmix[:, at].astype(f32) * v["o"][h // 2]
            own = jnp.where((lanes < 64) == (h % 2 == 0), product, 0.0)
            scales = jnp.where(lanes == 64 + h, jnp.sum(own, axis=1, keepdims=True), scales)
        scale[rows] = scales

    def weights_kernel():
        low = tn(u_all[...], gb_all[...]).astype(bf16)
        for k, value in enumerate((tn(n2_all[...], dg_all[...]).astype(bf16), tn(n2_all[...], du_all[...]).astype(bf16))):
            for i in range(d // PIECE):
                grads[(3 * i + k) * PIECE : (3 * i + k + 1) * PIECE] = value[i * PIECE : (i + 1) * PIECE]
        for i in range(d // PIECE):
            at = slice((3 * i + 2) * PIECE, (3 * i + 3) * PIECE)
            grads[at, :d] = low[i * PIECE : (i + 1) * PIECE]
            grads[at, d:] = low[d + i * PIECE : d + (i + 1) * PIECE]

    stages = [weigh, norm, project, activate, down, norm_back, mix_back]
    for step in range(len(stages) + FFN_CHUNKS - 1):
        for c, v in enumerate(work):
            if 0 <= step - c < len(stages):
                stages[step - c](v)
        if step == 3 + FFN_CHUNKS - 1:
            weights_kernel()
    gn[...] = sum(v["gn"] for v in work)
    gwo[...] = tn(mixed_all[...], dh_all[...]).astype(bf16)
    rows = keep.shape[0]
    keep[...] = grads[pl.ds(pl.multiple_of(ids[1] * rows, 16), rows)]
    send[...] = grads[pl.ds(pl.multiple_of((1 - ids[1]) * rows, 16), rows)]


def feed_forward(ids, lens, gain, x, wo, wg, wu, wd, cot, parts):
    t, d = x.shape
    ff, w = wg.shape[1], wo.shape[0]
    half = 3 * d // 2
    return call(
        partial(feed_forward_kernel, len(parts)), "feed_forward", 8,
        [shape(t, d), shape(t, d, dtype=f32), shape(t, w), shape(t, 128, dtype=f32), shape(w, d),
         shape(half, ff), shape(half, ff), shape(1, d, dtype=f32)],
        (ids, lens), (gain, x, wo, wg, wu, wd, cot, *[v["acc"] for v in parts], *[v["stat"] for v in parts]),
        scratch=[pltpu.VMEM((3 * d, ff), bf16)]
        + [pltpu.VMEM((t, k), bf16) for k in (w, d, ff, d, ff, ff, d)],
    )


def attend_back_kernel(n, pairs, counts, ids, q, do, scale, *refs):
    phases, size = len(counts), len(pairs)
    p = [refs[i * size : (i + 1) * size] for i in range(phases)]
    refs = refs[phases * size :]
    kv = [refs[i * size : (i + 1) * size] for i in range(phases)]
    e, refs = refs[phases * size : phases * size + phases], refs[phases * size + phases :]
    dk, dv, refs = refs[:size], refs[size : 2 * size], refs[2 * size :]
    dq, line, ds = refs
    me = ids[0]
    t = q.shape[0]
    lower = low_half(t)
    back = (iota((t, t), 0) + iota((t, t), 1) == t - 1).astype(f32).astype(bf16)
    lane = iota((1, 128), 1)
    line[...] = jnp.zeros_like(line)
    slots = [(i, j) for i, count in enumerate(counts) for j in range(count)]

    def operands(k):
        h = 2 * pairs[k // 2] + k % 2
        at = slice(h // 2 * 128, h // 2 * 128 + 128)
        qt = jnp.where(lower == (k % 2 == 0), q[:, at].astype(f32), 0.0).T
        doh = jnp.where(lower == (k % 2 == 1), turn(do[:, at].astype(f32)), 0.0)
        out = []
        for i in range(phases):
            factor = scale[:, 8 * i + h : 8 * i + h + 1]
            scaled = doh * factor
            shift = scale[:, 64 + h : 65 + h] * factor
            out.append((scaled.astype(bf16), shift, jnp.concatenate([qt, scaled.T], axis=1).astype(bf16)))
        return out

    def start(k, s, ops):
        i, j = slots[s]
        return nt(ops[i][0], kv[i][k // 2][k % 2, j * t : (j + 1) * t])

    def finish(k, s, ops, d_prob, acc):
        i, j = slots[s]
        rows = slice(j * t, (j + 1) * t)
        probs = p[i][k // 2][k % 2, :, rows]
        d_score = (probs.astype(f32) * (d_prob - ops[i][1])).astype(bf16)
        ds[k % 2, :, s * t : (s + 1) * t] = d_score
        more = nn(d_score, jnp.concatenate([kv[i][k // 2][k % 2, rows], e[i][rows]], axis=1))
        both = nn(ops[i][2], jnp.concatenate([d_score, probs], axis=0)).astype(bf16)
        mine, other = (both[:64], both[64:]) if k % 2 == 0 else (both[64:], both[:64])
        dk[k // 2][k % 2 * 64 : k % 2 * 64 + 64, s * t : (s + 1) * t] = mine
        dv[k // 2][k % 2 * 64 : k % 2 * 64 + 64, s * t : (s + 1) * t] = other
        return more if acc is None else acc + more

    def bias(k, acc):
        parts = []
        for r in (-1, 0, 1):
            there = me + r
            inside = (there >= 0) & (there < n)
            slot = jnp.where(inside, me ^ there, 0)
            block = ds[k % 2, :, pl.ds(pl.multiple_of(slot * t, t), t)]
            parts.append(nn(back, block) * inside.astype(f32))
        parts.append(jnp.zeros((t, t), f32))
        band = pltpu.roll(jnp.concatenate(parts, axis=1), 0, 1, stride=1, stride_axis=0)
        line[k : k + 1, : 4 * t] = jnp.sum(band, axis=0, keepdims=True)
        ends = jnp.sum(acc[:, 128:], axis=0, keepdims=True)
        line[k : k + 1, 4 * t :] = jnp.where((lane == LEFT) | (lane == RIGHT), ends, 0.0)

    tasks = [(k, s) for k in range(2 * size) for s in range(len(slots))]
    ops = [operands(0)]
    d_prob = start(0, 0, ops[0])
    accs = [None] * (2 * size)
    for index, (k, s) in enumerate(tasks):
        if s == 0 and k + 1 < 2 * size:
            ops.append(operands(k + 1))
        later = None
        if index + 1 < len(tasks):
            k2, s2 = tasks[index + 1]
            later = start(k2, s2, ops[k2])
        accs[k] = finish(k, s, ops[k], d_prob, accs[k])
        d_prob = later
        if s == len(slots) - 1:
            bias(k, accs[k])
    for g in range(size):
        dq[:, g * 128 : g * 128 + 128] = jnp.where(lower, accs[2 * g][:, :128], accs[2 * g + 1][:, :128]).astype(bf16)


def attend_back(n, pairs, ids, q, do, scale, parts):
    t = q.shape[0]
    widths = [v["e"].shape[0] for v in parts]
    s = sum(widths)
    size = len(pairs)
    out = call(
        partial(attend_back_kernel, n, pairs, [w // t for w in widths]), "attend_back", 4 * size,
        [shape(128, s)] * (2 * size) + [shape(t, 128 * size), shape(8, 4 * t + 128, dtype=f32)],
        (ids,), (q, do, scale, *[v["p"][g] for v in parts for g in pairs],
                 *[v["kv"][g] for v in parts for g in pairs], *[v["e"] for v in parts]),
        scratch=[pltpu.VMEM((2, t, s), bf16)], much=n > 8,
    )
    return dict(dk=out[:size], dv=out[size : 2 * size], dq=out[-2], line=out[-1], pairs=size)


def gather_back_kernel(n, buckets, counts, pairs, ids, gain, gn, gwo, wq, wk, wv, wt, *refs):
    phases = len(counts)
    n1, refs = refs[:phases], refs[phases:]
    total_pairs = sum(pairs)
    dkv, refs = refs[: 2 * total_pairs], refs[2 * total_pairs :]
    dq, lines = refs[: len(pairs)], refs[len(pairs) : 2 * len(pairs)]
    even, odd, dn1q, keep, send, grads, sums, diagonal = refs[2 * len(pairs) :]
    d, w = wq.shape
    t = dn1q.shape[0]
    weights = jnp.concatenate([wk[...], wv[...]], axis=1)
    total = jnp.zeros((2 * w, d), f32)
    slot = 0
    for i, count in enumerate(counts):
        begin = sum(counts[:i]) * t
        both = jnp.concatenate([ref[:, begin : begin + count * t] for ref in dkv], axis=0)
        total = total + nn(both, n1[i][...])
        back = nn(weights, both).astype(bf16)
        for _ in range(count):
            ref = odd if slot % 2 else even
            ref[slot // 2] = back[:, slot * t - begin : slot * t - begin + t]
            slot += 1
    dq_all = jnp.concatenate([ref[...] for ref in dq], axis=1)
    from_q = tn(dq_all, n1[0][:t])
    dn1q[...] = nt(dq_all, wq[...])
    grads[:w] = from_q.astype(bf16)
    grads[w : 3 * w] = total.astype(bf16)
    grads[3 * w :] = gwo[...]
    gains = jnp.sum(from_q * wt[:w].astype(f32), axis=0, keepdims=True)
    gains = gains + jnp.sum(total * wt[w:].astype(f32), axis=0, keepdims=True)
    sums[...] = jnp.zeros_like(sums)
    sums[0:1] = gains / gain[...].astype(f32)
    sums[1:2] = gn[...]
    diagonal[...] = jnp.zeros_like(diagonal)
    begin = 0
    for ref, count in zip(lines, pairs, strict=True):
        diagonal[begin : begin + 2 * count] = ref[: 2 * count]
        begin += 2 * count
    width = diagonal.shape[1]
    u = iota((width, 128), 0)
    bucket = bucket_of(u - (2 * t - 1), buckets)
    bucket = jnp.where(u == 4 * t + LEFT, buckets // 2 - 1, jnp.where(u == 4 * t + RIGHT, buckets - 1, bucket))
    pick = (bucket == iota((width, 128), 1)).astype(f32)
    sums[8:16, :128] = lax.dot_general(diagonal[...], pick, (((1,), (0,)), ((), ())),
                                       precision=lax.Precision.HIGHEST, preferred_element_type=f32)
    small = sums[...].astype(bf16)
    rows = 2 * w
    keep[:rows] = grads[pl.ds(pl.multiple_of(ids[1] * rows, 16), rows)]
    send[:rows] = grads[pl.ds(pl.multiple_of((1 - ids[1]) * rows, 16), rows)]
    keep[rows:] = small
    send[rows:] = small


def gather_back(n, buckets, ids, gain, gn, gwo, wq, wk, wv, wt, parts, backs):
    d, w = wq.shape
    t = backs[0]["dq"].shape[0]
    pairs = [v["pairs"] for v in backs]
    counts = [v["e"].shape[0] // t for v in parts]
    pieces = [ref for v in backs for ref in v["dk"]] + [ref for v in backs for ref in v["dv"]]
    half = 2 * w + SMALL
    return call(
        partial(gather_back_kernel, n, buckets, counts, pairs), "gather_back", 6,
        [shape(n // 2, d, t), shape(n // 2, d, t), shape(t, d, dtype=f32), shape(half, d), shape(half, d)],
        (ids,), (gain, gn, gwo, wq, wk, wv, wt, *[v["n1"] for v in parts], *pieces, *[v["dq"] for v in backs],
                 *[v["line"] for v in backs]),
        scratch=[pltpu.VMEM((4 * w, d), bf16), pltpu.VMEM((SMALL, d), f32), pltpu.VMEM((8, 4 * t + 128), f32)], much=n > 8,
    )


def rest_back_kernel(n, buckets, pairs, counts, sizes, ids, *refs):
    first, second, outs, inner = (refs[a:b] for a, b in zip(sizes[:-1], sizes[1:], strict=True))
    size = len(pairs)
    dkv, (dq, line), ds = inner[: 2 * size], inner[2 * size : 2 * size + 2], inner[2 * size + 2]
    attend_back_kernel(n, pairs, counts, ids, *first, *dkv, dq, line, ds)
    head, (dk0, dv0, dq0, line0) = second[: 7 + len(counts)], second[7 + len(counts) :]
    gather_back_kernel(n, buckets, counts, [1, size], ids, *head, dk0, *dkv[:size], dv0, *dkv[size:], dq0, dq, line0, line,
                       *outs, *inner[2 * size + 3 :])


def rest_back(n, buckets, pairs, ids, q, do, scale, gain, gn, gwo, wq, wk, wv, wt, parts, back):
    d, w = wq.shape
    t = q.shape[0]
    widths = [v["e"].shape[0] for v in parts]
    s, size, half = sum(widths), len(pairs), 2 * w + SMALL
    first = (q, do, scale, *[v["p"][g] for v in parts for g in pairs], *[v["kv"][g] for v in parts for g in pairs],
             *[v["e"] for v in parts])
    second = (gain, gn, gwo, wq, wk, wv, wt, *[v["n1"] for v in parts], back["dk"][0], back["dv"][0], back["dq"], back["line"])
    cuts = [0, len(first), len(first) + len(second), len(first) + len(second) + 5]
    inner = [pltpu.VMEM((128, s), bf16)] * (2 * size) + [pltpu.VMEM((t, 128 * size), bf16), pltpu.VMEM((8, 4 * t + 128), f32),
             pltpu.VMEM((2, t, s), bf16), pltpu.VMEM((4 * w, d), bf16), pltpu.VMEM((SMALL, d), f32),
             pltpu.VMEM((8, 4 * t + 128), f32)]
    return call(
        partial(rest_back_kernel, n, buckets, pairs, [v // t for v in widths], [*cuts, cuts[-1] + len(inner)]), "rest_back", 10,
        [shape(n // 2, d, t), shape(n // 2, d, t), shape(t, d, dtype=f32), shape(half, d), shape(half, d)],
        (ids,), (*first, *second), scratch=inner,
    )


def split_kernel(which, count, extra, ids, *refs):
    inputs, outs = refs[:-count], refs[-count:]
    rows = (inputs[0].shape[0] - extra) // count
    own = ids[which]
    for j in range(count):
        at = pl.ds(pl.multiple_of((own ^ j) * rows, 16), rows)
        total = inputs[0][at].astype(f32)
        for ref in inputs[1:]:
            total = total + ref[at].astype(f32)
        outs[j][:rows] = total.astype(bf16)
    if extra:
        at = pl.ds(rows * count, extra)
        total = inputs[0][at].astype(f32)
        for ref in inputs[1:]:
            total = total + ref[at].astype(f32)
        for j in range(count):
            outs[j][rows:] = total.astype(bf16)


def add_and_split(which, count, extra, ids, *arrays):
    rows = (arrays[0].shape[0] - extra) // count + extra
    out = shape(rows, arrays[0].shape[1])
    return call(partial(split_kernel, which, count, extra), "add_parts", 1, [out] * count, (ids,), arrays)


def by_chip_kernel(ids, keep, recv, *outs):
    rows = keep.shape[0] // 4
    for half, own in ((0, ids[2] % 2), (1, ids[2] // 2)):
        for j in range(2):
            at = pl.ds(pl.multiple_of((2 * half + (own ^ j)) * rows, 16), rows)
            outs[2 * half + j][...] = (keep[at].astype(f32) + recv[at].astype(f32)).astype(bf16)


def by_next_chip_kernel(ids, keep_x, recv_x, keep_y, recv_y, *outs):
    rows = keep_x.shape[0] // 2
    for half, own, a, b in ((0, ids[2] // 2, keep_x, recv_x), (1, ids[2] % 2, keep_y, recv_y)):
        for j in range(2):
            at = pl.ds(pl.multiple_of((own ^ j) * rows, 16), rows)
            outs[2 * half + j][...] = (a[at].astype(f32) + b[at].astype(f32)).astype(bf16)


def by_row_kernel(ids, keep_x, recv_x, keep_y, recv_y, mine, other):
    first = keep_x[...].astype(f32) + recv_x[...].astype(f32)
    second = keep_y[...].astype(f32) + recv_y[...].astype(f32)
    even = ids[3] % 2 == 0
    mine[...] = jnp.where(even, first, second).astype(bf16)
    other[...] = jnp.where(even, second, first).astype(bf16)


def pick_kernel(ids, mine, other, first, second):
    even = ids[3] % 2 == 0
    a, b = mine[...].astype(f32), other[...].astype(f32)
    first[...] = jnp.where(even, a, b).astype(bf16)
    second[...] = jnp.where(even, b, a).astype(bf16)


def stack_kernel(ids, *refs):
    *parts, out = refs
    rows = parts[0].shape[0]
    for i, ref in enumerate(parts):
        out[i * rows : (i + 1) * rows] = ref[...]


def join_kernel(ids, a, b, c, d, first, second):
    rows = a.shape[0]
    first[:rows], first[rows:] = a[...], b[...]
    second[:rows], second[rows:] = c[...], d[...]


def swap(array, axis, j):
    size = lax.axis_size(axis)
    return lax.ppermute(array, axis, [(i, i ^ j) for i in range(size)])


def order(first, *values):
    first, values = lax.optimization_barrier((first, values))
    return values if len(values) > 1 else values[0]


def sum_all(ids, keep, recv, extra):
    both = add_and_split(0, 1, extra, ids * 0, keep, recv)[0].astype(f32)
    size = both.shape[0] - extra
    placed = jnp.zeros((2 * size, both.shape[1]), f32)
    placed = lax.dynamic_update_slice_in_dim(placed, both[:size], ids[1] * size, 0)
    full, tail = lax.psum((placed, both[size:] * 0.5), ("rows", "seq"))
    mine = lax.dynamic_slice_in_dim(full, ids[1] * size, size, 0)
    other = lax.dynamic_slice_in_dim(full, (1 - ids[1]) * size, size, 0)
    return [mine.astype(bf16)], [other.astype(bf16)], tail.astype(bf16)


def to_chips(parts):
    return [parts[0]] + [swap(parts[j], "seq", 2 * j) for j in range(1, len(parts))]


def place_halves(ids, mine, other, full):
    size = full.shape[0] // 2
    if len(mine) == 1:
        full[pl.ds(pl.multiple_of(ids[1] * size, 16), size)] = mine[0][...]
        full[pl.ds(pl.multiple_of((1 - ids[1]) * size, 16), size)] = other[0][...]
        return
    piece = size // len(mine)
    for c, refs in ((ids[1], mine), (1 - ids[1], other)):
        for a, ref in enumerate(refs):
            at = c * size + (ids[2] ^ a) * piece
            for b in range(2):
                where = at + ((ids[3] % 2) ^ b) * (piece // 2)
                full[pl.ds(pl.multiple_of(where, 16), piece // 2)] = ref[b * (piece // 2) : (b + 1) * (piece // 2)]


def send_out(copies, source, target, sem):
    copies.append(pltpu.make_async_copy(source, target, sem))
    copies[-1].start()


def write_ffn(far, ids, parts, gate, up, down, full, sems):
    d = gate.shape[0]
    x, y = ids[2] % 2, ids[2] // 2
    rows = 3 * PIECE
    copies = []
    for c, pair in ((ids[1], parts[:2]), (1 - ids[1], parts[2:])):
        for half, first, second in ((0, x, y), (1, y, x)):
            for b in range(2):
                k = len(copies) // 4
                piece = 8 * c + 4 * half + 2 * (first ^ far) + (second ^ b)
                full[k] = pair[half][b * rows : (b + 1) * rows].astype(f32)
                at = pl.multiple_of(piece * PIECE, PIECE)
                send_out(copies, full.at[k, :PIECE], gate.at[pl.ds(at, PIECE)], sems.at[4 * k])
                send_out(copies, full.at[k, PIECE : 2 * PIECE], up.at[pl.ds(at, PIECE)], sems.at[4 * k + 1])
                send_out(copies, full.at[k, 2 * PIECE :, :d], down.at[pl.ds(at, PIECE)], sems.at[4 * k + 2])
                send_out(copies, full.at[k, 2 * PIECE :, d:], down.at[pl.ds(d + at, PIECE)], sems.at[4 * k + 3])
    return copies


def unpack_near_kernel(ids, *refs):
    for copy in write_ffn(0, ids, refs[:4], *refs[4:]):
        copy.wait()


def unpack_far_kernel(pieces, ids, *refs):
    parts, stacks = refs[:4], refs[4:8]
    gate, up, down, *attention, full, sems, both, wide, tall, sem2 = refs[8 + 3 :]
    copies = write_ffn(1, ids, parts, gate, up, down, full, sems)
    size = both.shape[0] // 2
    rows = stacks[0].shape[0] // pieces
    for k, stack in enumerate(stacks):
        for a in range(pieces):
            where = (ids[1] ^ (k // 2)) * size + ((ids[2] ^ a) * 2 + ((ids[3] % 2) ^ (k % 2))) * rows
            both[pl.ds(pl.multiple_of(where, 16), rows)] = stack[a * rows : (a + 1) * rows]
    w = wide.shape[2]
    tall[...] = both[3 * w :].astype(f32)
    send_out(copies, tall, attention[3], sem2.at[3])
    for k in range(3):
        wide[k] = both[k * w : (k + 1) * w].astype(f32).T
        send_out(copies, wide.at[k], attention[k], sem2.at[k])
    for copy in copies:
        copy.wait()


def unpack(kernel, ids, vmem_args, filled, out_shape, scratch):
    vmem, hbm = pl.BlockSpec(memory_space=pltpu.VMEM), pl.BlockSpec(memory_space=pl.ANY)
    return pl.pallas_call(
        kernel,
        in_specs=[pl.BlockSpec(memory_space=pltpu.SMEM)] + [vmem] * len(vmem_args) + [hbm] * len(filled),
        out_specs=[hbm] * len(out_shape),
        out_shape=out_shape,
        scratch_shapes=scratch,
        input_output_aliases={1 + len(vmem_args) + i: i for i in range(len(filled))},
        compiler_params=pltpu.CompilerParams(vmem_limit_bytes=VMEM),
        cost_estimate=pl.CostEstimate(flops=1000, bytes_accessed=1000, transcendentals=0),
        name="unpack",
    )(ids, *vmem_args, *filled)


def unpack_ffn_halves(ids, mine, other, d, ff):
    full = jnp.where(ids[1] == 0, jnp.concatenate([mine, other]), jnp.concatenate([other, mine])).astype(f32)
    full = full.reshape(d // PIECE, 3, PIECE, ff)
    low = full[:, 2].reshape(d, ff)
    return full[:, 0].reshape(d, ff), full[:, 1].reshape(d, ff), jnp.concatenate([low[:, :d], low[:, d:]])


def unpack_attention_kernel(pieces, ids, *refs):
    gq, gk, gv, go, full = refs[2 * pieces :]
    place_halves(ids, refs[:pieces], refs[pieces : 2 * pieces], full)
    w = gq.shape[1]
    for k, ref in enumerate((gq, gk, gv)):
        ref[...] = full[k * w : (k + 1) * w].astype(f32).T
    go[...] = full[3 * w :].astype(f32)


def unpack_small_kernel(ids, tail, g1, g2, gb):
    small = tail[...].astype(f32)
    g1[...] = small[0:1]
    g2[...] = small[1:2]
    gb[...] = small[8 : 8 + gb.shape[0], : gb.shape[1]]


def input_grad_kernel(ids, *refs):
    *parts, dn1q, x, dh, gain, out = refs
    total = parts[0][...].astype(f32)
    for ref in parts[1:]:
        total = total + ref[...].astype(f32)
    dn1 = total.T + dn1q[...]
    value = x[...].astype(f32)
    s1 = lax.rsqrt(jnp.mean(value * value, axis=-1, keepdims=True) + EPS)
    hat = value * s1
    scaled = dn1 * gain[...].astype(f32)
    out[...] = dh[...] + s1 * (scaled - hat * jnp.mean(hat * scaled, axis=-1, keepdims=True))


def slots_kernel(count, ids, mine, other, *outs):
    for j in range(count):
        outs[j][...] = (mine[j].astype(f32) + other[j].astype(f32)).astype(bf16)


def shards(
    tokens, norm_attn, query_weight, key_weight, value_weight, out_weight, bucket_bias_table, norm_ffn,
    gate_weight, expansion_matrix, down_weight, lengths, cotangent,
):
    _, t, d = tokens.shape
    n = lax.axis_size("seq")
    buckets, heads = bucket_bias_table.shape
    width = query_weight.shape[1]
    ff = gate_weight.shape[1]
    seq = lax.axis_index("seq")
    ids = jnp.stack([seq, seq % 2, seq // 2, lax.axis_index("rows")]).astype(i32)
    x = tokens.reshape(t, d)
    cot = cotangent.reshape(t, d)
    lens = lengths.reshape(-1)
    gain1 = norm_attn.reshape(1, d)
    gain2 = norm_ffn.reshape(1, d)

    blocks = [None] * n
    blocks[0], blocks[1] = x, swap(x, "seq", 1)
    for j in range(2, n, 2):
        blocks[j] = swap(x, "seq", j)
    q, ext, bands, wt, line, x, wq, wk, wv = prepare(
        ids, lens, x, gain1, bucket_bias_table.T, query_weight, key_weight, value_weight
    )
    blocks[0] = x
    cuts = [0, 2, *range(8, n, 8), n]

    def phase(a, b):
        return attend(n, a, ids, lens, blocks[a:b], gain1, wk, wv, q, ext, bands, line)

    parts = [phase(0, 2)]
    for j in range(2, n, 2):
        blocks[j] = order(parts[0]["acc"], blocks[j])
        blocks[j + 1] = swap(blocks[j], "seq", 1)
    parts += [phase(a, b) for a, b in zip(cuts[1:-1], cuts[2:], strict=True)]
    output, dh, do, scale, gwo, keep, send, gn = feed_forward(
        ids, lens, gain2, x, out_weight, gate_weight, expansion_matrix, down_weight, cot, parts
    )
    half = n // 2
    pairs = width // 128
    whole = n != 8 or lax.axis_size("rows") != 4
    zero, near = ids * 0, ids[3:4] % 2

    def unpack_attention(mine, other):
        return call(
            partial(unpack_attention_kernel, len(mine)), "unpack_attention", 3,
            [shape(d, width, dtype=f32)] * 3 + [shape(width, d, dtype=f32)],
            (ids,), (*mine, *other), scratch=[pltpu.VMEM((4 * width, d), bf16)],
        )

    def unpack_small(tail):
        return call(unpack_small_kernel, "unpack_small", 1,
                    [shape(1, d, dtype=f32)] * 2 + [shape(heads, buckets, dtype=f32)], (ids,), (tail,))

    def input_grad(slots):
        return call(input_grad_kernel, "input_grad", 2, shape(t, d, dtype=f32), (ids,), (*slots, dn1q, x, dh, gain1))

    def add_slots(recv):
        return call(partial(slots_kernel, half), "add_slots", 1, [shape(d, t)] * half, (ids,), (even, recv))

    f_core = swap(send, "seq", 1)
    back = attend_back(n, [0], ids, q, do, scale, parts)
    f_keep = keep
    if whole:
        backs = [back, attend_back(n, list(range(1, pairs)), ids, q, do, scale, parts)]
        even, odd, dn1q, keep, send = gather_back(n, buckets, ids, gain1, gn, gwo, wq, wk, wv, wt, parts, backs)
        a_core, d_core = swap(send, "seq", 1), swap(odd, "seq", 1)
        mine, other, _ = sum_all(ids, f_keep, f_core, 0)
        gate, up, down = unpack_ffn_halves(ids, mine[0], other[0], d, ff)
        grad_tokens = input_grad(to_chips(add_slots(d_core)))
        mine, other, tail = sum_all(ids, keep, a_core, SMALL)
        gq, gk, gv, go = unpack_attention(mine, other)
        g1, g2, gb = unpack_small(tail)
    else:
        part = lambda rows: shape(f_keep.shape[0] // rows, ff)
        f_core = order(back["dq"], f_core)
        f_x, f_x2, f_y, f_y2 = call(by_chip_kernel, "add_parts", 1, [part(4)] * 4, (ids,), (keep, f_core))
        do = order(f_x, do)
        f_x2, f_y2 = swap(f_x2, "seq", 2), swap(f_y2, "seq", 4)
        even, odd, dn1q, keep, send = rest_back(
            n, buckets, list(range(1, pairs)), ids, q, do, scale, gain1, gn, gwo, wq, wk, wv, wt, parts, back
        )
        send, odd = order((f_x2, f_y2), send, odd)
        live = dict(a=swap(send, "seq", 1), d=swap(odd, "seq", 1))
        f_x, f_x2, f_y, f_y2 = call(
            by_next_chip_kernel, "add_parts", 1, [part(8)] * 4, (ids,), (f_x, f_x2, f_y, f_y2)
        )
        live["f"] = [swap(f_x2, "seq", 4), swap(f_y2, "seq", 2)]
        size = (keep.shape[0] - SMALL) // 8
        ffn_out = [shape(d, ff, dtype=f32), shape(d, ff, dtype=f32), shape(ff, d, dtype=f32)]
        ffn_scratch = [pltpu.VMEM((8, 3 * PIECE, ff), f32), pltpu.SemaphoreType.DMA((32,))]
        kept = dict(f=(f_x, f_y))

        def f_rows():
            (f_x, f_y), (f_x2, f_y2) = kept["f"], live["f"]
            mine, other = call(by_row_kernel, "add_parts", 1, [part(8)] * 2, (ids,), (f_x, f_x2, f_y, f_y2))
            kept["f"], live["f"] = mine, swap(other, "rows", 1)
            return mine

        def f_add(j):
            mine = add_and_split(0, 1, 0, zero, kept["f"], live["f"])[0]
            kept["f"], live["f"] = mine, swap(mine, "rows", j)
            return mine

        def f_pick():
            x, y = call(pick_kernel, "pick", 1, [part(8)] * 2, (ids,), (kept["f"], live["f"]))
            kept["f"], live["f"] = (x, y), [swap(x, "seq", 4), swap(y, "seq", 2)]
            return x

        def f_join():
            (x, y), (x2, y2) = kept["f"], live["f"]
            x, y = call(join_kernel, "join", 1, [part(4)] * 2, (ids,), (x, x2, y, y2))
            kept["f"], live["f"] = (x, y), [swap(x, "seq", 2), swap(y, "seq", 4)]
            live["near"] = [swap(v, "seq", 1) for v in (x, y)]
            return x

        def f_near():
            kept["near"] = unpack(unpack_near_kernel, ids, (*kept["f"], *live["near"]), (), ffn_out, ffn_scratch)
            return kept["near"][0]

        def f_swap():
            live["far"] = [swap(v, "seq", 1) for v in live["f"]]
            return None

        def a_chips():
            kept["a"] = add_and_split(2, half, SMALL, ids, keep, live["a"])
            live["a"] = to_chips(kept["a"])
            return kept["a"][0]

        def a_rows():
            kept["a"], other = add_and_split(0, 2, SMALL, near, *live["a"])
            live["a"] = swap(other, "rows", 1)
            return kept["a"]

        def a_add(j):
            kept["a"] = add_and_split(0, 1, SMALL, zero, kept["a"], live["a"])[0]
            live["a"] = swap(kept["a"], "rows", 2) if j == 2 else to_chips([kept["a"][:size]] * half)
            return kept["a"]

        def a_stack():
            kept["stack"] = call(stack_kernel, "stack", 1, shape(half * size, d), (ids,), live["a"])
            live["a"] = swap(kept["stack"], "rows", 1)
            live["anear"] = swap(kept["stack"], "seq", 1)
            return kept["stack"]

        def a_swap():
            live["afar"] = swap(live["a"], "seq", 1)
            return None

        def last():
            kept["out"] = unpack(
                partial(unpack_far_kernel, half), ids,
                (*live["f"], *live["far"], kept["stack"], live["a"], live["anear"], live["afar"]), kept["near"],
                ffn_out + [shape(d, width, dtype=f32)] * 3 + [shape(width, d, dtype=f32)],
                [*ffn_scratch, pltpu.VMEM((4 * width, d), bf16), pltpu.VMEM((3, d, width), f32),
                 pltpu.VMEM((width, d), f32), pltpu.SemaphoreType.DMA((4,))],
            )
            return kept["out"][0]

        def d_slots():
            kept["d"] = add_slots(live["d"])
            live["d"] = to_chips(kept["d"])
            return kept["d"][0]

        def d_out():
            kept["tokens"] = input_grad(live["d"])
            return kept["tokens"]

        def small():
            kept["small"] = unpack_small(kept["a"][size:])
            return kept["small"][0]

        steps = dict(
            f_rows=(f_rows, "f"), f_z0=(partial(f_add, 2), "f"), f_z1=(partial(f_add, 1), "f"), f_pick=(f_pick, "f"),
            f_join=(f_join, "f"), f_near=(f_near, "near"), f_swap=(f_swap, "f"), last=(last, "far"),
            a_chips=(a_chips, "a"), a_rows=(a_rows, "a"), a_z0=(partial(a_add, 2), "a"), a_z1=(partial(a_add, 1), "a"),
            a_stack=(a_stack, "a"), a_swap=(a_swap, "a"),
            d_slots=(d_slots, "d"), d_out=(d_out, "d"), small=(small, None),
        )
        token = f_x
        for name in STEPS.split():
            if ":" in name:
                stream, j = name.split(":")
                live[stream][int(j)] = token = order(token, live[stream][int(j)])
                continue
            step, stream = steps[name]
            if stream is not None:
                live[stream] = order(token, live[stream])
            elif name == "small":
                kept["a"] = order(token, kept["a"])
            done = step()
            token = live[stream] if done is None else done
        gate, up, down, gq, gk, gv, go = kept["out"]
        g1, g2, gb = kept["small"]
        grad_tokens = kept["tokens"]
    return (
        output.reshape(tokens.shape), grad_tokens.reshape(tokens.shape), g1.reshape(d), gq, gk, gv, go, gb.T,
        g2.reshape(d), gate, up, down,
    )


def solution(mesh):
    split = P("rows", "seq", None)
    in_specs = (split,) + (P(),) * 10 + (P("rows", None), split)
    out_specs = (split, split) + (P(),) * 10
    return jax.shard_map(shards, mesh=mesh, in_specs=in_specs, out_specs=out_specs, check_vma=False)
```

```python
from functools import partial

import jax
import jax.numpy as jnp
from jax import lax
from jax.experimental import pallas as pl
from jax.experimental.pallas import tpu as pltpu
from jax.sharding import PartitionSpec as P

EPS = 1e-6
BIG = -(2.0**30)
LEFT, RIGHT, ONES = 17, 18, 19
PIECE = 32
FFN_CHUNKS = 1
STEPS = (
    "a_chips", "f_rows", "f_z0", "a_rows", "d_slots", "f_z1", "f_pick", "a_z0", "d:3", "d_out", "a_z1",
    "f_join", "a_stack", "f_near", "small", "a_swap", "f_swap", "own", "last",
)
SMALL = 16
VMEM = 24 * 1024 * 1024
MUCH = 56 * 1024 * 1024

f32, bf16, i32 = jnp.float32, jnp.bfloat16, jnp.int32


def thresholds(buckets, max_distance):
    half = buckets // 2
    exact = half // 2
    steps = half - exact
    out = list(range(1, exact))
    for j in range(steps):
        target = exact ** (steps - j) * max_distance**j
        m = exact
        while m**steps < target:
            m += 1
        out.append(m)
    return out


def bucket_of(offset, buckets):
    distance = jnp.abs(offset)
    bucket = (offset > 0).astype(i32) * (buckets // 2)
    for t in thresholds(buckets, 128):
        bucket = bucket + (distance >= t).astype(i32)
    return bucket


def nn(a, b):
    return lax.dot_general(a, b, (((1,), (0,)), ((), ())), preferred_element_type=f32)


def nt(a, b):
    return lax.dot_general(a, b, (((1,), (1,)), ((), ())), preferred_element_type=f32)


def tn(a, b):
    return lax.dot_general(a, b, (((0,), (0,)), ((), ())), preferred_element_type=f32)


def iota(shape, dim):
    return lax.broadcasted_iota(i32, shape, dim)


def rms(values, gain):
    scale = lax.rsqrt(jnp.mean(values * values, axis=-1, keepdims=True) + EPS)
    return values * scale * gain


def call(kernel, name, us, out_shape, smem_args, args, scratch=(), much=False, anywhere=0):
    smem = pl.BlockSpec(memory_space=pltpu.SMEM)
    vmem = pl.BlockSpec(memory_space=pltpu.VMEM)
    return pl.pallas_call(
        kernel,
        in_specs=[smem] * len(smem_args) + [vmem] * (len(args) - anywhere) + [pl.BlockSpec(memory_space=pltpu.HBM)] * anywhere,
        out_specs=jax.tree.map(lambda _: vmem, out_shape),
        out_shape=out_shape,
        scratch_shapes=list(scratch),
        compiler_params=pltpu.CompilerParams(vmem_limit_bytes=MUCH if much else VMEM),
        cost_estimate=pl.CostEstimate(flops=int(us * 1e6), bytes_accessed=int(us * 2e3), transcendentals=0),
        name=name,
    )(*smem_args, *args)


def shape(*dims, dtype=bf16):
    return jax.ShapeDtypeStruct(dims, dtype)


def low_half(t):
    return iota((t, 128), 1) < 64


def turn(pair):
    return pltpu.roll(pair, 64, 1)


def prepare_kernel(ids, lens, gain, table, x, w3, q, ext, bands, wt, line, x_here, wq, wk, wv):
    w = wq.shape[1]
    for k, ref in enumerate((wq, wk, wv)):
        ref[...] = w3[:, k * w : (k + 1) * w]
        wt[k * w : (k + 1) * w] = ref[...].astype(f32).T.astype(bf16)
    x_here[...] = x[...]
    t = x.shape[0]
    heads, buckets = table.shape
    low, high = segment_bounds(lens)
    lanes = iota((t, 128), 1)
    pos = iota((t, 128), 0) + ids[0] * t
    other = jnp.where((pos >= low) & (pos < high), 0.0, BIG)
    ext[...] = jnp.where(lanes < LEFT, other, 0.0)
    u = iota((buckets, 4 * t), 1)
    bucket = bucket_of(jnp.where(u < 3 * t, u - t, u - 5 * t), buckets)
    pick = (bucket == iota((buckets, 4 * t), 0)).astype(f32).astype(bf16)
    line[...] = jnp.zeros_like(line)
    line[:heads] = nn(table[...], pick)
    for h in range(heads):
        band = pltpu.roll(jnp.broadcast_to(line[h : h + 1], (t, 4 * t)), 0, 1, stride=1, stride_axis=0)
        for r in range(3):
            bands[h, r] = band[:, r * t : (r + 1) * t].astype(bf16)
        bands[h, 3] = jnp.zeros((t, t), bf16)
    n1 = rms(x[...].astype(f32), gain[...].astype(f32)).astype(bf16)
    q[...] = nn(n1, wq[...]).astype(bf16)


def prepare(ids, lens, x, gain, table, wq, wk, wv):
    t, d = x.shape
    heads, w = table.shape[0], wq.shape[1]
    return call(
        prepare_kernel, "prepare", 4,
        [shape(t, w), shape(t, 128, dtype=f32), shape(heads, 4, t, t), shape(3 * w, d), shape(8, 4 * t, dtype=f32),
         shape(t, d), shape(d, w), shape(d, w), shape(d, w)],
        (ids, lens), (gain, table, x, jnp.concatenate([wq, wk, wv], axis=1)),
    )


def segment_bounds(lens):
    lane = iota((1, 128), 1)
    low = jnp.where(lane == 0, -1, 2**30)
    high = jnp.full((1, 128), -1, i32)
    total = 0
    for k in range(lens.shape[0]):
        total = total + lens[k]
        high = jnp.where(lane == k, total, high)
        low = jnp.where(lane == k + 1, total, low)
    return low, jnp.where(lane == lens.shape[0], 2**30, high)


def attend_kernel(n, first, count, pieces, ids, lens, *refs):
    x, refs = refs[:pieces], refs[pieces:]
    gain, wk, wv, q, ext, bands, line, n1, e, acc, stat = refs[:11]
    pairs = q.shape[1] // 128
    kv, p = refs[11 : 11 + pairs], refs[11 + pairs : -1]
    s = refs[-1]
    me = ids[0]
    t = q.shape[0]
    low, high = segment_bounds(lens)
    row = iota((t, 128), 0)
    lanes = iota((t, 128), 1)
    begin = 0
    for ref in x:
        n1[begin : begin + ref.shape[0]] = rms(ref[...].astype(f32), gain[...].astype(f32)).astype(bf16)
        begin += ref.shape[0]
    for i in range(count):
        at = slice(i * t, (i + 1) * t)
        block = me ^ (first + i)
        pos = row + block * t
        away = block - me
        flag = jnp.where(away <= -2, LEFT, jnp.where(away >= 2, RIGHT, ONES))
        here = ((pos >= low) & (pos < high)) | (lanes == flag) | (lanes == ONES)
        e[at] = here.astype(f32).astype(bf16)
    upper = iota((t, 128), 1) >= 64
    near = [i for i in range(count) if (first + i) & (first + i + 1) == 0]

    def project(g, i):
        rows, at = slice(i * t, (i + 1) * t), slice(g * 128, g * 128 + 128)
        both = nn(n1[rows], jnp.concatenate([wk[:, at], wv[:, at]], axis=1))
        keys, values = both[:, :128], turn(both[:, 128:])
        kv[g][0, rows] = jnp.where(upper, values, keys).astype(bf16)
        kv[g][1, rows] = jnp.where(upper, keys, values).astype(bf16)

    def query(h):
        lane_ext = jnp.where(lanes == LEFT, line[h : h + 1, 0:1],
                             jnp.where(lanes == RIGHT, line[h : h + 1, 3 * t - 1 : 3 * t], ext[...]))
        q2 = q[:, h // 2 * 128 : h // 2 * 128 + 128].astype(f32)
        return jnp.concatenate([jnp.where(upper == (h % 2 == 1), q2, 0.0), lane_ext], axis=1).astype(bf16)

    def keys_of(h, i):
        rows = slice(i * t, (i + 1) * t)
        return jnp.concatenate([kv[h // 2][h % 2, rows], e[rows]], axis=1)

    def score(h, i, qa, top):
        block = nt(qa, keys_of(h, i))
        if i in near:
            away = (me ^ (first + i)) - me
            block = block + bands[h, jnp.where(jnp.abs(away) <= 1, away + 1, 3)].astype(f32)
        s[h % 2, :, i * t : (i + 1) * t] = block
        here = block[:, :128]
        for c in range(1, t // 128):
            here = jnp.maximum(here, block[:, c * 128 : (c + 1) * 128])
        return here if top is None else jnp.maximum(top, here)

    def mix(h, i, top, out):
        raised = jnp.exp(s[h % 2, :, i * t : (i + 1) * t] - top).astype(bf16)
        p[h // 2][h % 2, :, i * t : (i + 1) * t] = raised
        more = nn(raised, keys_of(h, i))
        return more if out is None else out + more

    for g in range(pairs):
        for i in range(count):
            project(g, i)
    stats = jnp.zeros((t, 128), f32)
    last = None
    sums = []
    for h in range(2 * pairs + 1):
        qa = query(h) if h < 2 * pairs else None
        top = out = None
        for i in range(count):
            if h < 2 * pairs:
                top = score(h, i, qa, top)
            if h > 0:
                out = mix(h - 1, i, last, out)
        if h > 0:
            stats = jnp.where(lanes == h - 1, last, stats)
            stats = jnp.where(lanes == 7 + h, out[:, 128 + ONES : 129 + ONES], stats)
            sums.append(out[:, :128])
        if h < 2 * pairs:
            last = jnp.max(top, axis=1, keepdims=True)
    for g in range(pairs):
        acc[:, g * 128 : g * 128 + 128] = turn(jnp.where(upper, sums[2 * g], sums[2 * g + 1]))
    stat[...] = stats


def attend(n, first, ids, lens, blocks, gain, wk, wv, q, ext, bands, line):
    count = len(blocks)
    blocks = [piece for block in blocks for piece in block]
    t, d = q.shape[0], wk.shape[0]
    pairs = wk.shape[1] // 128
    c = count * t
    out = call(
        partial(attend_kernel, n, first, count, len(blocks)), "attend", 2 * count,
        [shape(c, d), shape(c, 128), shape(t, wk.shape[1], dtype=f32), shape(t, 128, dtype=f32)]
        + [shape(2, c, 128)] * pairs + [shape(2, t, c)] * pairs,
        (ids, lens), (*blocks, gain, wk, wv, q, ext, bands, line), scratch=[pltpu.VMEM((2, t, c), f32)], much=n > 8,
    )
    return dict(n1=out[0], e=out[1], acc=out[2], stat=out[3], kv=out[4 : 4 + pairs], p=out[4 + pairs :])


def feed_forward_kernel(phases, ids, lens, gain, x, wo, wg, wu, wd, cot, *refs):
    accs, stats = refs[:phases], refs[phases : 2 * phases]
    out, dh, do, scale, gwo, keep, send, gn, grads, mixed_all, n2_all, u_all, gb_all, dg_all, du_all, dh_all = refs[2 * phases :]
    t, d = x.shape
    pairs = wo.shape[0] // 128
    chunk = t // FFN_CHUNKS
    lanes = iota((chunk, 128), 1)
    g2 = gain[...].astype(f32)
    last = lens[0]
    for k in range(1, lens.shape[0]):
        last = last + lens[k]
    work = [dict(rows=slice(c * chunk, (c + 1) * chunk)) for c in range(FFN_CHUNKS)]

    def weigh(v):
        rows = v["rows"]
        tops = [ref[rows] for ref in stats]
        top = tops[0]
        for other in tops[1:]:
            top = jnp.maximum(top, other)
        weights = [jnp.exp(a - top) for a in tops]
        total = jnp.where(lanes < 2 * pairs, 0.0, 1.0)
        for w, ref in zip(weights, stats, strict=True):
            total = total + w * pltpu.roll(ref[rows], 120, 1)
        weights = [jnp.where(lanes < 2 * pairs, w / total, 0.0) for w in weights]
        v["scales"] = weights[0]
        for i, w in enumerate(weights[1:], 1):
            v["scales"] = v["scales"] + pltpu.roll(w, 8 * i, 1)
        v["o"] = []
        for g in range(pairs):
            at = slice(g * 128, g * 128 + 128)
            value = jnp.zeros((chunk, 128), f32)
            for i, w in enumerate(weights):
                value = value + accs[i][rows, at] * jnp.where(lanes < 64, w[:, 2 * g : 2 * g + 1], w[:, 2 * g + 1 : 2 * g + 2])
            v["o"].append(value)
            mixed_all[rows, at] = value.astype(bf16)
        pos = ids[0] * t + rows.start + iota((chunk, 1), 0)
        v["g"] = cot[rows].astype(f32) * (pos < last).astype(f32)
        gb_all[rows] = v["g"].astype(bf16)
        v["du"] = nt(gb_all[rows], wd[...]).astype(bf16).astype(f32)

    def norm(v):
        rows = v["rows"]
        v["h1"] = x[rows].astype(f32) + nn(mixed_all[rows], wo[...])
        v["s2"] = lax.rsqrt(jnp.mean(v["h1"] * v["h1"], axis=-1, keepdims=True) + EPS)
        v["hat"] = v["h1"] * v["s2"]
        n2_all[rows] = (v["hat"] * g2).astype(bf16)

    def project(v):
        rows = v["rows"]
        v["gate"], v["up"] = nn(n2_all[rows], wg[...]), nn(n2_all[rows], wu[...])

    def activate(v):
        rows, gate, up = v["rows"], v["gate"], v["up"]
        c0 = 0.7978845608028654
        square = gate * gate
        th = jnp.tanh(c0 * gate * (1.0 + 0.044715 * square))
        half = 0.5 * (1.0 + th)
        act = gate * half
        dact = half + 0.5 * gate * (1.0 - th * th) * (c0 * (1.0 + 3 * 0.044715 * square))
        u_all[rows] = (act * up).astype(bf16)
        dg_all[rows] = (v["du"] * up * dact).astype(bf16)
        du_all[rows] = (v["du"] * act).astype(bf16)

    def down(v):
        rows = v["rows"]
        v["dn2"] = nt(dg_all[rows], wg[...]) + nt(du_all[rows], wu[...])

    def norm_back(v):
        rows, dn2, hat, s2 = v["rows"], v["dn2"], v["hat"], v["s2"]
        out[rows] = (v["h1"] + nn(u_all[rows], wd[...])).astype(bf16)
        v["gn"] = jnp.sum(dn2 * hat, axis=0, keepdims=True)
        scaled = dn2 * g2
        dh1 = v["g"] + s2 * (scaled - hat * jnp.mean(hat * scaled, axis=-1, keepdims=True))
        dh[rows] = dh1
        dh_all[rows] = dh1.astype(bf16)

    def mix_back(v):
        rows = v["rows"]
        dmix = nt(dh_all[rows], wo[...]).astype(bf16)
        do[rows] = dmix
        scales = v["scales"]
        for h in range(2 * pairs):
            at = slice(h // 2 * 128, h // 2 * 128 + 128)
            product = dmix[:, at].astype(f32) * v["o"][h // 2]
            own = jnp.where((lanes < 64) == (h % 2 == 0), product, 0.0)
            scales = jnp.where(lanes == 64 + h, jnp.sum(own, axis=1, keepdims=True), scales)
        scale[rows] = scales

    def weights_kernel():
        low = tn(u_all[...], gb_all[...]).astype(bf16)
        for k, value in enumerate((tn(n2_all[...], dg_all[...]).astype(bf16), tn(n2_all[...], du_all[...]).astype(bf16))):
            for i in range(d // PIECE):
                grads[(3 * i + k) * PIECE : (3 * i + k + 1) * PIECE] = value[i * PIECE : (i + 1) * PIECE]
        for i in range(d // PIECE):
            at = slice((3 * i + 2) * PIECE, (3 * i + 3) * PIECE)
            grads[at, :d] = low[i * PIECE : (i + 1) * PIECE]
            grads[at, d:] = low[d + i * PIECE : d + (i + 1) * PIECE]

    stages = [weigh, norm, project, activate, down, norm_back, mix_back]
    for step in range(len(stages) + FFN_CHUNKS - 1):
        for c, v in enumerate(work):
            if 0 <= step - c < len(stages):
                stages[step - c](v)
        if step == len(stages) + FFN_CHUNKS - 2:
            weights_kernel()
    gn[...] = sum(v["gn"] for v in work)
    gwo[...] = tn(mixed_all[...], dh_all[...]).astype(bf16)
    rows = keep.shape[0]
    keep[...] = grads[pl.ds(pl.multiple_of(ids[1] * rows, 16), rows)]
    send[...] = grads[pl.ds(pl.multiple_of((1 - ids[1]) * rows, 16), rows)]


def feed_forward(ids, lens, gain, x, wo, wg, wu, wd, cot, parts):
    t, d = x.shape
    ff, w = wg.shape[1], wo.shape[0]
    half = 3 * d // 2
    return call(
        partial(feed_forward_kernel, len(parts)), "feed_forward", 8,
        [shape(t, d), shape(t, d, dtype=f32), shape(t, w), shape(t, 128, dtype=f32), shape(w, d),
         shape(half, ff), shape(half, ff), shape(1, d, dtype=f32)],
        (ids, lens), (gain, x, wo, wg, wu, wd, cot, *[v["acc"] for v in parts], *[v["stat"] for v in parts]),
        scratch=[pltpu.VMEM((3 * d, ff), bf16)]
        + [pltpu.VMEM((t, k), bf16) for k in (w, d, ff, d, ff, ff, d)],
    )


def attend_back_kernel(n, pairs, counts, ids, q, do, scale, *refs):
    phases, size = len(counts), len(pairs)
    p = [refs[i * size : (i + 1) * size] for i in range(phases)]
    refs = refs[phases * size :]
    kv = [refs[i * size : (i + 1) * size] for i in range(phases)]
    e, refs = refs[phases * size : phases * size + phases], refs[phases * size + phases :]
    dk, dv, refs = refs[:size], refs[size : 2 * size], refs[2 * size :]
    dq, line, ds = refs
    me = ids[0]
    t = q.shape[0]
    lower = low_half(t)
    back = (iota((t, t), 0) + iota((t, t), 1) == t - 1).astype(f32).astype(bf16)
    lane = iota((1, 128), 1)
    line[...] = jnp.zeros_like(line)
    slots = [(i, j) for i, count in enumerate(counts) for j in range(count)]

    def operands(k):
        h = 2 * pairs[k // 2] + k % 2
        at = slice(h // 2 * 128, h // 2 * 128 + 128)
        qt = jnp.where(lower == (k % 2 == 0), q[:, at].astype(f32), 0.0).T
        doh = jnp.where(lower == (k % 2 == 1), turn(do[:, at].astype(f32)), 0.0)
        out = []
        for i in range(phases):
            factor = scale[:, 8 * i + h : 8 * i + h + 1]
            scaled = doh * factor
            shift = scale[:, 64 + h : 65 + h] * factor
            out.append((scaled.astype(bf16), shift, jnp.concatenate([qt, scaled.T], axis=1).astype(bf16)))
        return out

    def start(k, s, ops):
        i, j = slots[s]
        return nt(ops[i][0], kv[i][k // 2][k % 2, j * t : (j + 1) * t])

    def finish(k, s, ops, d_prob, acc):
        i, j = slots[s]
        rows = slice(j * t, (j + 1) * t)
        probs = p[i][k // 2][k % 2, :, rows]
        d_score = (probs.astype(f32) * (d_prob - ops[i][1])).astype(bf16)
        ds[k % 2, :, s * t : (s + 1) * t] = d_score
        more = nn(d_score, jnp.concatenate([kv[i][k // 2][k % 2, rows], e[i][rows]], axis=1))
        both = nn(ops[i][2], jnp.concatenate([d_score, probs], axis=0)).astype(bf16)
        mine, other = (both[:64], both[64:]) if k % 2 == 0 else (both[64:], both[:64])
        dk[k // 2][k % 2 * 64 : k % 2 * 64 + 64, s * t : (s + 1) * t] = mine
        dv[k // 2][k % 2 * 64 : k % 2 * 64 + 64, s * t : (s + 1) * t] = other
        return more if acc is None else acc + more

    def bias(k, acc):
        parts = []
        for r in (-1, 0, 1):
            there = me + r
            inside = (there >= 0) & (there < n)
            slot = jnp.where(inside, me ^ there, 0)
            block = ds[k % 2, :, pl.ds(pl.multiple_of(slot * t, t), t)]
            parts.append(nn(back, block) * inside.astype(f32))
        parts.append(jnp.zeros((t, t), f32))
        band = pltpu.roll(jnp.concatenate(parts, axis=1), 0, 1, stride=1, stride_axis=0)
        line[k : k + 1, : 4 * t] = jnp.sum(band, axis=0, keepdims=True)
        ends = jnp.sum(acc[:, 128:], axis=0, keepdims=True)
        line[k : k + 1, 4 * t :] = jnp.where((lane == LEFT) | (lane == RIGHT), ends, 0.0)

    tasks = [(k, s) for k in range(2 * size) for s in range(len(slots))]
    ops = [operands(0)]
    d_prob = start(0, 0, ops[0])
    accs = [None] * (2 * size)
    for index, (k, s) in enumerate(tasks):
        if s == 0 and k + 1 < 2 * size:
            ops.append(operands(k + 1))
        later = None
        if index + 1 < len(tasks):
            k2, s2 = tasks[index + 1]
            later = start(k2, s2, ops[k2])
        accs[k] = finish(k, s, ops[k], d_prob, accs[k])
        d_prob = later
        if s == len(slots) - 1:
            bias(k, accs[k])
    for g in range(size):
        dq[:, g * 128 : g * 128 + 128] = jnp.where(lower, accs[2 * g][:, :128], accs[2 * g + 1][:, :128]).astype(bf16)


def attend_back(n, pairs, ids, q, do, scale, parts):
    t = q.shape[0]
    widths = [v["e"].shape[0] for v in parts]
    s = sum(widths)
    size = len(pairs)
    out = call(
        partial(attend_back_kernel, n, pairs, [w // t for w in widths]), "attend_back", 4 * size,
        [shape(128, s)] * (2 * size) + [shape(t, 128 * size), shape(8, 4 * t + 128, dtype=f32)],
        (ids,), (q, do, scale, *[v["p"][g] for v in parts for g in pairs],
                 *[v["kv"][g] for v in parts for g in pairs], *[v["e"] for v in parts]),
        scratch=[pltpu.VMEM((2, t, s), bf16)], much=n > 8,
    )
    return dict(dk=out[:size], dv=out[size : 2 * size], dq=out[-2], line=out[-1], pairs=size)


def gather_back_kernel(n, buckets, counts, pairs, ids, gain, gn, gwo, wq, wk, wv, wt, *refs):
    phases = len(counts)
    n1, refs = refs[:phases], refs[phases:]
    total_pairs = sum(pairs)
    dkv, refs = refs[: 2 * total_pairs], refs[2 * total_pairs :]
    dq, lines = refs[: len(pairs)], refs[len(pairs) : 2 * len(pairs)]
    even, odd, dn1q, keep, send, grads, sums, diagonal = refs[2 * len(pairs) :]
    d, w = wq.shape
    t = dn1q.shape[0]
    weights = jnp.concatenate([wk[...], wv[...]], axis=1)
    total = jnp.zeros((2 * w, d), f32)
    slot = 0
    for i, count in enumerate(counts):
        begin = sum(counts[:i]) * t
        both = jnp.concatenate([ref[:, begin : begin + count * t] for ref in dkv], axis=0)
        total = total + nn(both, n1[i][...])
        back = nn(weights, both).astype(bf16)
        for _ in range(count):
            ref = odd if slot % 2 else even
            ref[slot // 2] = back[:, slot * t - begin : slot * t - begin + t]
            slot += 1
    dq_all = jnp.concatenate([ref[...] for ref in dq], axis=1)
    from_q = tn(dq_all, n1[0][:t])
    dn1q[...] = nt(dq_all, wq[...])
    grads[:w] = from_q.astype(bf16)
    grads[w : 3 * w] = total.astype(bf16)
    grads[3 * w :] = gwo[...]
    gains = jnp.sum(from_q * wt[:w].astype(f32), axis=0, keepdims=True)
    gains = gains + jnp.sum(total * wt[w:].astype(f32), axis=0, keepdims=True)
    sums[...] = jnp.zeros_like(sums)
    sums[0:1] = gains / gain[...].astype(f32)
    sums[1:2] = gn[...]
    diagonal[...] = jnp.zeros_like(diagonal)
    begin = 0
    for ref, count in zip(lines, pairs, strict=True):
        diagonal[begin : begin + 2 * count] = ref[: 2 * count]
        begin += 2 * count
    width = diagonal.shape[1]
    u = iota((width, 128), 0)
    bucket = bucket_of(u - (2 * t - 1), buckets)
    bucket = jnp.where(u == 4 * t + LEFT, buckets // 2 - 1, jnp.where(u == 4 * t + RIGHT, buckets - 1, bucket))
    pick = (bucket == iota((width, 128), 1)).astype(f32)
    sums[8:16, :128] = lax.dot_general(diagonal[...], pick, (((1,), (0,)), ((), ())),
                                       precision=lax.Precision.HIGHEST, preferred_element_type=f32)
    small = sums[...].astype(bf16)
    rows = 2 * w
    keep[:rows] = grads[pl.ds(pl.multiple_of(ids[1] * rows, 16), rows)]
    send[:rows] = grads[pl.ds(pl.multiple_of((1 - ids[1]) * rows, 16), rows)]
    keep[rows:] = small
    send[rows:] = small


def gather_back(n, buckets, ids, gain, gn, gwo, wq, wk, wv, wt, parts, backs):
    d, w = wq.shape
    t = backs[0]["dq"].shape[0]
    pairs = [v["pairs"] for v in backs]
    counts = [v["e"].shape[0] // t for v in parts]
    pieces = [ref for v in backs for ref in v["dk"]] + [ref for v in backs for ref in v["dv"]]
    half = 2 * w + SMALL
    return call(
        partial(gather_back_kernel, n, buckets, counts, pairs), "gather_back", 6,
        [shape(n // 2, d, t), shape(n // 2, d, t), shape(t, d, dtype=f32), shape(half, d), shape(half, d)],
        (ids,), (gain, gn, gwo, wq, wk, wv, wt, *[v["n1"] for v in parts], *pieces, *[v["dq"] for v in backs],
                 *[v["line"] for v in backs]),
        scratch=[pltpu.VMEM((4 * w, d), bf16), pltpu.VMEM((SMALL, d), f32), pltpu.VMEM((8, 4 * t + 128), f32)], much=n > 8,
    )


def rest_back_kernel(n, buckets, pairs, counts, sizes, ids, *refs):
    first, second, outs, inner = (refs[a:b] for a, b in zip(sizes[:-1], sizes[1:], strict=True))
    size = len(pairs)
    dkv, (dq, line), ds = inner[: 2 * size], inner[2 * size : 2 * size + 2], inner[2 * size + 2]
    attend_back_kernel(n, pairs, counts, ids, *first, *dkv, dq, line, ds)
    head, (dk0, dv0, dq0, line0) = second[: 7 + len(counts)], second[7 + len(counts) :]
    gather_back_kernel(n, buckets, counts, [1, size], ids, *head, dk0, *dkv[:size], dv0, *dkv[size:], dq0, dq, line0, line,
                       *outs, *inner[2 * size + 3 :])


def rest_back(n, buckets, pairs, ids, q, do, scale, gain, gn, gwo, wq, wk, wv, wt, parts, back):
    d, w = wq.shape
    t = q.shape[0]
    widths = [v["e"].shape[0] for v in parts]
    s, size, half = sum(widths), len(pairs), 2 * w + SMALL
    first = (q, do, scale, *[v["p"][g] for v in parts for g in pairs], *[v["kv"][g] for v in parts for g in pairs],
             *[v["e"] for v in parts])
    second = (gain, gn, gwo, wq, wk, wv, wt, *[v["n1"] for v in parts], back["dk"][0], back["dv"][0], back["dq"], back["line"])
    cuts = [0, len(first), len(first) + len(second), len(first) + len(second) + 5]
    inner = [pltpu.VMEM((128, s), bf16)] * (2 * size) + [pltpu.VMEM((t, 128 * size), bf16), pltpu.VMEM((8, 4 * t + 128), f32),
             pltpu.VMEM((2, t, s), bf16), pltpu.VMEM((4 * w, d), bf16), pltpu.VMEM((SMALL, d), f32),
             pltpu.VMEM((8, 4 * t + 128), f32)]
    return call(
        partial(rest_back_kernel, n, buckets, pairs, [v // t for v in widths], [*cuts, cuts[-1] + len(inner)]), "rest_back", 10,
        [shape(n // 2, d, t), shape(n // 2, d, t), shape(t, d, dtype=f32), shape(half, d), shape(half, d)],
        (ids,), (*first, *second), scratch=inner,
    )


def split_kernel(which, count, extra, ids, *refs):
    inputs, outs = refs[:-count], refs[-count:]
    rows = (inputs[0].shape[0] - extra) // count
    own = ids[which]
    for j in range(count):
        at = pl.ds(pl.multiple_of((own ^ j) * rows, 16), rows)
        total = inputs[0][at].astype(f32)
        for ref in inputs[1:]:
            total = total + ref[at].astype(f32)
        outs[j][:rows] = total.astype(bf16)
    if extra:
        at = pl.ds(rows * count, extra)
        total = inputs[0][at].astype(f32)
        for ref in inputs[1:]:
            total = total + ref[at].astype(f32)
        for j in range(count):
            outs[j][rows:] = total.astype(bf16)


def add_and_split(which, count, extra, ids, *arrays):
    rows = (arrays[0].shape[0] - extra) // count + extra
    out = shape(rows, arrays[0].shape[1])
    return call(partial(split_kernel, which, count, extra), "add_parts", 1, [out] * count, (ids,), arrays)


def by_chip_kernel(ids, keep, recv, *outs):
    rows = keep.shape[0] // 4
    for half, own in ((0, ids[2] % 2), (1, ids[2] // 2)):
        for j in range(2):
            at = pl.ds(pl.multiple_of((2 * half + (own ^ j)) * rows, 16), rows)
            outs[2 * half + j][...] = (keep[at].astype(f32) + recv[at].astype(f32)).astype(bf16)


def by_next_chip_kernel(ids, keep_x, recv_x, keep_y, recv_y, *outs):
    rows = keep_x.shape[0] // 2
    for half, own, a, b in ((0, ids[2] // 2, keep_x, recv_x), (1, ids[2] % 2, keep_y, recv_y)):
        for j in range(2):
            at = pl.ds(pl.multiple_of((own ^ j) * rows, 16), rows)
            outs[2 * half + j][...] = (a[at].astype(f32) + b[at].astype(f32)).astype(bf16)


def by_row_kernel(ids, keep_x, recv_x, keep_y, recv_y, mine, other):
    first = keep_x[...].astype(f32) + recv_x[...].astype(f32)
    second = keep_y[...].astype(f32) + recv_y[...].astype(f32)
    even = ids[3] % 2 == 0
    mine[...] = jnp.where(even, first, second).astype(bf16)
    other[...] = jnp.where(even, second, first).astype(bf16)


def pick_kernel(ids, mine, other, first, second):
    even = ids[3] % 2 == 0
    a, b = mine[...].astype(f32), other[...].astype(f32)
    first[...] = jnp.where(even, a, b).astype(bf16)
    second[...] = jnp.where(even, b, a).astype(bf16)


def stack_kernel(ids, *refs):
    *parts, out = refs
    rows = parts[0].shape[0]
    for i, ref in enumerate(parts):
        out[i * rows : (i + 1) * rows] = ref[...]


def join_kernel(ids, a, b, c, d, first, second):
    rows = a.shape[0]
    first[:rows], first[rows:] = a[...], b[...]
    second[:rows], second[rows:] = c[...], d[...]


def swap(array, axis, j):
    size = lax.axis_size(axis)
    return lax.ppermute(array, axis, [(i, i ^ j) for i in range(size)])


def order(first, *values):
    first, values = lax.optimization_barrier((first, values))
    return values if len(values) > 1 else values[0]


def sum_all(ids, keep, recv, extra):
    both = add_and_split(0, 1, extra, ids * 0, keep, recv)[0].astype(f32)
    size = both.shape[0] - extra
    placed = jnp.zeros((2 * size, both.shape[1]), f32)
    placed = lax.dynamic_update_slice_in_dim(placed, both[:size], ids[1] * size, 0)
    full, tail = lax.psum((placed, both[size:] * 0.5), ("rows", "seq"))
    mine = lax.dynamic_slice_in_dim(full, ids[1] * size, size, 0)
    other = lax.dynamic_slice_in_dim(full, (1 - ids[1]) * size, size, 0)
    return [mine.astype(bf16)], [other.astype(bf16)], tail.astype(bf16)


def to_chips(parts):
    return [parts[0]] + [swap(parts[j], "seq", 2 * j) for j in range(1, len(parts))]


def place_halves(ids, mine, other, full):
    size = full.shape[0] // 2
    if len(mine) == 1:
        full[pl.ds(pl.multiple_of(ids[1] * size, 16), size)] = mine[0][...]
        full[pl.ds(pl.multiple_of((1 - ids[1]) * size, 16), size)] = other[0][...]
        return
    piece = size // len(mine)
    for c, refs in ((ids[1], mine), (1 - ids[1], other)):
        for a, ref in enumerate(refs):
            at = c * size + (ids[2] ^ a) * piece
            for b in range(2):
                where = at + ((ids[3] % 2) ^ b) * (piece // 2)
                full[pl.ds(pl.multiple_of(where, 16), piece // 2)] = ref[b * (piece // 2) : (b + 1) * (piece // 2)]


def send_out(copies, source, target, sem):
    copies.append(pltpu.make_async_copy(source, target, sem))
    copies[-1].start()


def write_ffn(far, ids, parts, gate, up, down, full, sems):
    d = gate.shape[0]
    x, y = ids[2] % 2, ids[2] // 2
    rows = 3 * PIECE
    copies = []
    for c, *pair in parts:
        for half, first, second in ((0, x, y), (1, y, x)):
            for b in range(2):
                k = len(copies) // 4
                piece = 8 * c + 4 * half + 2 * (first ^ far) + (second ^ b)
                full[k] = pair[half][b * rows : (b + 1) * rows].astype(f32)
                at = pl.multiple_of(piece * PIECE, PIECE)
                send_out(copies, full.at[k, :PIECE], gate.at[pl.ds(at, PIECE)], sems.at[4 * k])
                send_out(copies, full.at[k, PIECE : 2 * PIECE], up.at[pl.ds(at, PIECE)], sems.at[4 * k + 1])
                send_out(copies, full.at[k, 2 * PIECE :, :d], down.at[pl.ds(at, PIECE)], sems.at[4 * k + 2])
                send_out(copies, full.at[k, 2 * PIECE :, d:], down.at[pl.ds(d + at, PIECE)], sems.at[4 * k + 3])
    return copies


def unpack_near_kernel(ids, *refs):
    for copy in write_ffn(0, ids, ((ids[1], *refs[:2]), (1 - ids[1], *refs[2:4])), *refs[4:]):
        copy.wait()


def unpack_half_kernel(other, filled, chips, ids, *refs):
    (x, y, *stacks), refs = refs[:4], refs[4 + filled :]
    gate, up, down, gq, gk, gv, go, full, sems, both, wide, tall, sem2 = refs
    core = ids[1] ^ other
    copies = write_ffn(1, ids, ((core, x, y),), gate, up, down, full, sems)
    rows = stacks[0].shape[0] // chips
    for k, stack in enumerate(stacks):
        for a in range(chips):
            where = ((ids[2] ^ a) * 2 + ((ids[3] % 2) ^ k)) * rows
            both[pl.ds(pl.multiple_of(where, 16), rows)] = stack[a * rows : (a + 1) * rows]
    w = wide.shape[2]

    def finish(matrices):
        moves = []
        for i, (ref, turned) in enumerate(matrices):
            value = both[i * w : (i + 1) * w].astype(f32)
            source = wide.at[i] if turned else tall
            source[...] = value.T if turned else value
            send_out(moves, source, ref, sem2.at[i])
        for copy in moves:
            copy.wait()

    @pl.when(core == 0)
    def _():
        finish(((gq, True), (gk, True)))

    @pl.when(core == 1)
    def _():
        finish(((gv, True), (go, False)))

    for copy in copies:
        copy.wait()


def unpack(kernel, ids, vmem_args, filled, out_shape, scratch):
    vmem, hbm = pl.BlockSpec(memory_space=pltpu.VMEM), pl.BlockSpec(memory_space=pl.ANY)
    return pl.pallas_call(
        kernel,
        in_specs=[pl.BlockSpec(memory_space=pltpu.SMEM)] + [vmem] * len(vmem_args) + [hbm] * len(filled),
        out_specs=[hbm] * len(out_shape),
        out_shape=out_shape,
        scratch_shapes=scratch,
        input_output_aliases={1 + len(vmem_args) + i: i for i in range(len(filled))},
        compiler_params=pltpu.CompilerParams(vmem_limit_bytes=VMEM),
        cost_estimate=pl.CostEstimate(flops=1000, bytes_accessed=1000, transcendentals=0),
        name="unpack",
    )(ids, *vmem_args, *filled)


def unpack_ffn_halves(ids, mine, other, d, ff):
    full = jnp.where(ids[1] == 0, jnp.concatenate([mine, other]), jnp.concatenate([other, mine])).astype(f32)
    full = full.reshape(d // PIECE, 3, PIECE, ff)
    low = full[:, 2].reshape(d, ff)
    return full[:, 0].reshape(d, ff), full[:, 1].reshape(d, ff), jnp.concatenate([low[:, :d], low[:, d:]])


def unpack_attention_kernel(pieces, ids, *refs):
    gq, gk, gv, go, full = refs[2 * pieces :]
    place_halves(ids, refs[:pieces], refs[pieces : 2 * pieces], full)
    w = gq.shape[1]
    for k, ref in enumerate((gq, gk, gv)):
        ref[...] = full[k * w : (k + 1) * w].astype(f32).T
    go[...] = full[3 * w :].astype(f32)


def unpack_small_kernel(ids, tail, g1, g2, gb):
    small = tail[...].astype(f32)
    g1[...] = small[0:1]
    g2[...] = small[1:2]
    gb[...] = small[8 : 8 + gb.shape[0], : gb.shape[1]]


def input_grad_kernel(ids, *refs):
    *parts, dn1q, x, dh, gain, out = refs
    total = parts[0][...].astype(f32)
    for ref in parts[1:]:
        total = total + ref[...].astype(f32)
    dn1 = total.T + dn1q[...]
    value = x[...].astype(f32)
    s1 = lax.rsqrt(jnp.mean(value * value, axis=-1, keepdims=True) + EPS)
    hat = value * s1
    scaled = dn1 * gain[...].astype(f32)
    out[...] = dh[...] + s1 * (scaled - hat * jnp.mean(hat * scaled, axis=-1, keepdims=True))


def slots_kernel(count, ids, mine, other, *outs):
    for j in range(count):
        outs[j][...] = (mine[j].astype(f32) + other[j].astype(f32)).astype(bf16)


def shards(
    tokens, norm_attn, query_weight, key_weight, value_weight, out_weight, bucket_bias_table, norm_ffn,
    gate_weight, expansion_matrix, down_weight, lengths, cotangent,
):
    _, t, d = tokens.shape
    n = lax.axis_size("seq")
    buckets, heads = bucket_bias_table.shape
    width = query_weight.shape[1]
    ff = gate_weight.shape[1]
    seq = lax.axis_index("seq")
    ids = jnp.stack([seq, seq % 2, seq // 2, lax.axis_index("rows")]).astype(i32)
    x = tokens.reshape(t, d)
    cot = cotangent.reshape(t, d)
    lens = lengths.reshape(-1)
    gain1 = norm_attn.reshape(1, d)
    gain2 = norm_ffn.reshape(1, d)

    blocks = [[x], [swap(x, "seq", 1)]] + [None] * (n - 2)
    for j in range(2, n, 2):
        if n != 8 or j != 6:
            blocks[j] = [swap(x, "seq", j)]
    q, ext, bands, wt, line, x, wq, wk, wv = prepare(
        ids, lens, x, gain1, bucket_bias_table.T, query_weight, key_weight, value_weight
    )
    blocks[0] = [x]
    cuts = [0, 2, 6, *range(8, n, 8), n]

    def phase(a, b):
        return attend(n, a, ids, lens, blocks[a:b], gain1, wk, wv, q, ext, bands, line)

    parts = []
    for a, b in zip(cuts[:-1], cuts[1:], strict=True):
        for j in range(a, b, 2):
            if j:
                blocks[j] = [order(parts[-1]["acc"], v) for v in blocks[j]]
                blocks[j + 1] = [swap(v, "seq", 1) for v in blocks[j]]
        if n == 8 and a == 2:
            blocks[6] = [swap(blocks[4][0][: t // 2], "seq", 2), swap(blocks[2][0][t // 2 :], "seq", 4)]
        parts.append(phase(a, b))
    output, dh, do, scale, gwo, keep, send, gn = feed_forward(
        ids, lens, gain2, x, out_weight, gate_weight, expansion_matrix, down_weight, cot, parts
    )
    half = n // 2
    pairs = width // 128
    whole = n != 8 or lax.axis_size("rows") != 4
    zero, near = ids * 0, ids[3:4] % 2

    def unpack_attention(mine, other):
        return call(
            partial(unpack_attention_kernel, len(mine)), "unpack_attention", 3,
            [shape(d, width, dtype=f32)] * 3 + [shape(width, d, dtype=f32)],
            (ids,), (*mine, *other), scratch=[pltpu.VMEM((4 * width, d), bf16)],
        )

    def unpack_small(tail):
        return call(unpack_small_kernel, "unpack_small", 1,
                    [shape(1, d, dtype=f32)] * 2 + [shape(heads, buckets, dtype=f32)], (ids,), (tail,))

    def input_grad(slots):
        return call(input_grad_kernel, "input_grad", 2, shape(t, d, dtype=f32), (ids,), (*slots, dn1q, x, dh, gain1))

    def add_slots(recv):
        return call(partial(slots_kernel, half), "add_slots", 1, [shape(d, t)] * half, (ids,), (even, recv))

    f_core = swap(send, "seq", 1)
    back = attend_back(n, [0], ids, q, do, scale, parts)
    f_keep = keep
    if whole:
        backs = [back, attend_back(n, list(range(1, pairs)), ids, q, do, scale, parts)]
        even, odd, dn1q, keep, send = gather_back(n, buckets, ids, gain1, gn, gwo, wq, wk, wv, wt, parts, backs)
        a_core, d_core = swap(send, "seq", 1), swap(odd, "seq", 1)
        mine, other, _ = sum_all(ids, f_keep, f_core, 0)
        gate, up, down = unpack_ffn_halves(ids, mine[0], other[0], d, ff)
        grad_tokens = input_grad(to_chips(add_slots(d_core)))
        mine, other, tail = sum_all(ids, keep, a_core, SMALL)
        gq, gk, gv, go = unpack_attention(mine, other)
        g1, g2, gb = unpack_small(tail)
    else:
        part = lambda rows: shape(f_keep.shape[0] // rows, ff)
        f_core = order(back["dq"], f_core)
        f_x, f_x2, f_y, f_y2 = call(by_chip_kernel, "add_parts", 1, [part(4)] * 4, (ids,), (keep, f_core))
        do = order(f_x, do)
        f_x2, f_y2 = swap(f_x2, "seq", 2), swap(f_y2, "seq", 4)
        even, odd, dn1q, keep, send = rest_back(
            n, buckets, list(range(1, pairs)), ids, q, do, scale, gain1, gn, gwo, wq, wk, wv, wt, parts, back
        )
        send, odd = order((f_x2, f_y2), send, odd)
        live = dict(a=swap(send, "seq", 1), d=swap(odd, "seq", 1))
        f_x, f_x2, f_y, f_y2 = call(
            by_next_chip_kernel, "add_parts", 1, [part(8)] * 4, (ids,), (f_x, f_x2, f_y, f_y2)
        )
        live["f"] = [swap(f_x2, "seq", 4), swap(f_y2, "seq", 2)]
        size = (keep.shape[0] - SMALL) // 8
        ffn_out = [shape(d, ff, dtype=f32), shape(d, ff, dtype=f32), shape(ff, d, dtype=f32)]
        ffn_scratch = [pltpu.VMEM((8, 3 * PIECE, ff), f32), pltpu.SemaphoreType.DMA((32,))]
        kept = dict(f=(f_x, f_y))

        def f_rows():
            (f_x, f_y), (f_x2, f_y2) = kept["f"], live["f"]
            mine, other = call(by_row_kernel, "add_parts", 1, [part(8)] * 2, (ids,), (f_x, f_x2, f_y, f_y2))
            kept["f"], live["f"] = mine, swap(other, "rows", 1)
            return mine

        def f_add(j):
            mine = add_and_split(0, 1, 0, zero, kept["f"], live["f"])[0]
            kept["f"], live["f"] = mine, swap(mine, "rows", j)
            return mine

        def f_pick():
            x, y = call(pick_kernel, "pick", 1, [part(8)] * 2, (ids,), (kept["f"], live["f"]))
            kept["f"], live["f"] = (x, y), [swap(x, "seq", 4), swap(y, "seq", 2)]
            return x

        def f_join():
            (x, y), (x2, y2) = kept["f"], live["f"]
            x, y = call(join_kernel, "join", 1, [part(4)] * 2, (ids,), (x, x2, y, y2))
            kept["f"], live["f"] = (x, y), [swap(x, "seq", 2), swap(y, "seq", 4)]
            live["near"] = [swap(v, "seq", 1) for v in (x, y)]
            return x

        def f_near():
            kept["near"] = unpack(unpack_near_kernel, ids, (*kept["f"], *live["near"]), (), ffn_out, ffn_scratch)
            return kept["near"][0]

        def f_swap():
            live["far"] = [swap(v, "seq", 1) for v in live["f"]]
            return None

        def a_chips():
            kept["a"] = add_and_split(2, half, SMALL, ids, keep, live["a"])
            live["a"] = to_chips(kept["a"])
            return kept["a"][0]

        def a_rows():
            kept["a"], other = add_and_split(0, 2, SMALL, near, *live["a"])
            live["a"] = swap(other, "rows", 1)
            return kept["a"]

        def a_add(j):
            kept["a"] = add_and_split(0, 1, SMALL, zero, kept["a"], live["a"])[0]
            live["a"] = swap(kept["a"], "rows", 2) if j == 2 else to_chips([kept["a"][:size]] * half)
            return kept["a"]

        def a_stack():
            kept["stack"] = call(stack_kernel, "stack", 1, shape(half * size, d), (ids,), live["a"])
            live["a"] = swap(kept["stack"], "rows", 1)
            live["anear"] = swap(kept["stack"], "seq", 1)
            return kept["stack"]

        def a_swap():
            live["afar"] = swap(live["a"], "seq", 1)
            return None

        def unpack_half(other, x, y, first, second, filled):
            return unpack(
                partial(unpack_half_kernel, other, len(filled), half), ids, (x, y, first, second), filled,
                ffn_out + [shape(d, width, dtype=f32)] * 3 + [shape(width, d, dtype=f32)],
                [*ffn_scratch, pltpu.VMEM((2 * width, d), bf16), pltpu.VMEM((2, d, width), f32),
                 pltpu.VMEM((width, d), f32), pltpu.SemaphoreType.DMA((2,))],
            )

        def own():
            kept["near"] = unpack_half(0, *live["f"], kept["stack"], live["a"], kept["near"])
            return kept["near"][0]

        def last():
            kept["out"] = unpack_half(1, *live["far"], live["anear"], live["afar"], kept["near"])
            return kept["out"][0]

        def d_slots():
            kept["d"] = add_slots(live["d"])
            live["d"] = to_chips(kept["d"])
            return kept["d"][0]

        def d_out():
            kept["tokens"] = input_grad(live["d"])
            return kept["tokens"]

        def small():
            kept["small"] = unpack_small(kept["a"][size:])
            return kept["small"][0]

        steps = dict(
            f_rows=(f_rows, "f"), f_z0=(partial(f_add, 2), "f"), f_z1=(partial(f_add, 1), "f"), f_pick=(f_pick, "f"),
            f_join=(f_join, "f"), f_near=(f_near, "near"), f_swap=(f_swap, "f"), own=(own, "f"), last=(last, "far"),
            a_chips=(a_chips, "a"), a_rows=(a_rows, "a"), a_z0=(partial(a_add, 2), "a"), a_z1=(partial(a_add, 1), "a"),
            a_stack=(a_stack, "a"), a_swap=(a_swap, "a"),
            d_slots=(d_slots, "d"), d_out=(d_out, "d"), small=(small, None),
        )
        token = f_x
        for name in STEPS:
            if ":" in name:
                stream, j = name.split(":")
                live[stream][int(j)] = token = order(token, live[stream][int(j)])
                continue
            step, stream = steps[name]
            if stream is not None:
                live[stream] = order(token, live[stream])
            elif name == "small":
                kept["a"] = order(token, kept["a"])
            done = step()
            token = live[stream] if done is None else done
        gate, up, down, gq, gk, gv, go = kept["out"]
        g1, g2, gb = kept["small"]
        grad_tokens = kept["tokens"]
    return (
        output.reshape(tokens.shape), grad_tokens.reshape(tokens.shape), g1.reshape(d), gq, gk, gv, go, gb.T,
        g2.reshape(d), gate, up, down,
    )


def solution(mesh):
    split = P("rows", "seq", None)
    in_specs = (split,) + (P(),) * 10 + (P("rows", None), split)
    out_specs = (split, split) + (P(),) * 10
    return jax.shard_map(shards, mesh=mesh, in_specs=in_specs, out_specs=out_specs, check_vma=False)
```

```python
from functools import partial

import jax
import jax.numpy as jnp
from jax import lax
from jax.experimental import pallas as pl
from jax.experimental.pallas import tpu as pltpu
from jax.sharding import PartitionSpec as P

EPS = 1e-6
BIG = -(2.0**30)
LEFT, RIGHT, ONES = 17, 18, 19
PIECE = 32
FFN_CHUNKS = 1
STEPS = (
    "a_chips", "f_rows", "f_z0", "a_rows", "d_slots", "f_z1", "f_pick", "a_z0", "d:3", "d_out", "a_z1",
    "f_join", "a_stack", "small", "f_near", "f_swap", "a_swap", "own", "last",
)
SMALL = 16
VMEM = 24 * 1024 * 1024
MUCH = 56 * 1024 * 1024

f32, bf16, i32 = jnp.float32, jnp.bfloat16, jnp.int32


def thresholds(buckets, max_distance):
    half = buckets // 2
    exact = half // 2
    steps = half - exact
    out = list(range(1, exact))
    for j in range(steps):
        target = exact ** (steps - j) * max_distance**j
        m = exact
        while m**steps < target:
            m += 1
        out.append(m)
    return out


def bucket_of(offset, buckets):
    distance = jnp.abs(offset)
    bucket = (offset > 0).astype(i32) * (buckets // 2)
    for t in thresholds(buckets, 128):
        bucket = bucket + (distance >= t).astype(i32)
    return bucket


def nn(a, b):
    return lax.dot_general(a, b, (((1,), (0,)), ((), ())), preferred_element_type=f32)


def nt(a, b):
    return lax.dot_general(a, b, (((1,), (1,)), ((), ())), preferred_element_type=f32)


def tn(a, b):
    return lax.dot_general(a, b, (((0,), (0,)), ((), ())), preferred_element_type=f32)


def iota(shape, dim):
    return lax.broadcasted_iota(i32, shape, dim)


def rms(values, gain):
    scale = lax.rsqrt(jnp.mean(values * values, axis=-1, keepdims=True) + EPS)
    return values * scale * gain


def call(kernel, name, us, out_shape, smem_args, args, scratch=(), much=False, anywhere=0):
    smem = pl.BlockSpec(memory_space=pltpu.SMEM)
    vmem = pl.BlockSpec(memory_space=pltpu.VMEM)
    return pl.pallas_call(
        kernel,
        in_specs=[smem] * len(smem_args) + [vmem] * (len(args) - anywhere) + [pl.BlockSpec(memory_space=pltpu.HBM)] * anywhere,
        out_specs=jax.tree.map(lambda _: vmem, out_shape),
        out_shape=out_shape,
        scratch_shapes=list(scratch),
        compiler_params=pltpu.CompilerParams(vmem_limit_bytes=MUCH if much else VMEM),
        cost_estimate=pl.CostEstimate(flops=int(us * 1e6), bytes_accessed=int(us * 2e3), transcendentals=0),
        name=name,
    )(*smem_args, *args)


def shape(*dims, dtype=bf16):
    return jax.ShapeDtypeStruct(dims, dtype)


def low_half(t):
    return iota((t, 128), 1) < 64


def turn(pair):
    return pltpu.roll(pair, 64, 1)


def prepare_kernel(ids, lens, gain, table, x, w3, q, ext, bands, wt, line, x_here, wq, wk, wv):
    w = wq.shape[1]
    for k, ref in enumerate((wq, wk, wv)):
        ref[...] = w3[:, k * w : (k + 1) * w]
        wt[k * w : (k + 1) * w] = ref[...].astype(f32).T.astype(bf16)
    x_here[...] = x[...]
    t = x.shape[0]
    heads, buckets = table.shape
    low, high = segment_bounds(lens)
    lanes = iota((t, 128), 1)
    pos = iota((t, 128), 0) + ids[0] * t
    other = jnp.where((pos >= low) & (pos < high), 0.0, BIG)
    ext[...] = jnp.where(lanes < LEFT, other, 0.0)
    u = iota((buckets, 4 * t), 1)
    bucket = bucket_of(jnp.where(u < 3 * t, u - t, u - 5 * t), buckets)
    pick = (bucket == iota((buckets, 4 * t), 0)).astype(f32).astype(bf16)
    line[...] = jnp.zeros_like(line)
    line[:heads] = nn(table[...], pick)
    for h in range(heads):
        band = pltpu.roll(jnp.broadcast_to(line[h : h + 1], (t, 4 * t)), 0, 1, stride=1, stride_axis=0)
        for r in range(3):
            bands[h, r] = band[:, r * t : (r + 1) * t].astype(bf16)
        bands[h, 3] = jnp.zeros((t, t), bf16)
    n1 = rms(x[...].astype(f32), gain[...].astype(f32)).astype(bf16)
    q[...] = nn(n1, wq[...]).astype(bf16)


def prepare(ids, lens, x, gain, table, wq, wk, wv):
    t, d = x.shape
    heads, w = table.shape[0], wq.shape[1]
    return call(
        prepare_kernel, "prepare", 4,
        [shape(t, w), shape(t, 128, dtype=f32), shape(heads, 4, t, t), shape(3 * w, d), shape(8, 4 * t, dtype=f32),
         shape(t, d), shape(d, w), shape(d, w), shape(d, w)],
        (ids, lens), (gain, table, x, jnp.concatenate([wq, wk, wv], axis=1)),
    )


def segment_bounds(lens):
    lane = iota((1, 128), 1)
    low = jnp.where(lane == 0, -1, 2**30)
    high = jnp.full((1, 128), -1, i32)
    total = 0
    for k in range(lens.shape[0]):
        total = total + lens[k]
        high = jnp.where(lane == k, total, high)
        low = jnp.where(lane == k + 1, total, low)
    return low, jnp.where(lane == lens.shape[0], 2**30, high)


def attend_kernel(n, first, count, pieces, ids, lens, *refs):
    x, refs = refs[:pieces], refs[pieces:]
    gain, wk, wv, q, ext, bands, line, n1, e, acc, stat = refs[:11]
    pairs = q.shape[1] // 128
    kv, p = refs[11 : 11 + pairs], refs[11 + pairs : -1]
    s = refs[-1]
    me = ids[0]
    t = q.shape[0]
    low, high = segment_bounds(lens)
    row = iota((t, 128), 0)
    lanes = iota((t, 128), 1)
    begin = 0
    for ref in x:
        n1[begin : begin + ref.shape[0]] = rms(ref[...].astype(f32), gain[...].astype(f32)).astype(bf16)
        begin += ref.shape[0]
    for i in range(count):
        at = slice(i * t, (i + 1) * t)
        block = me ^ (first + i)
        pos = row + block * t
        away = block - me
        flag = jnp.where(away <= -2, LEFT, jnp.where(away >= 2, RIGHT, ONES))
        here = ((pos >= low) & (pos < high)) | (lanes == flag) | (lanes == ONES)
        e[at] = here.astype(f32).astype(bf16)
    upper = iota((t, 128), 1) >= 64
    near = [i for i in range(count) if (first + i) & (first + i + 1) == 0]

    def project(g, i):
        rows, at = slice(i * t, (i + 1) * t), slice(g * 128, g * 128 + 128)
        both = nn(n1[rows], jnp.concatenate([wk[:, at], wv[:, at]], axis=1))
        keys, values = both[:, :128], turn(both[:, 128:])
        kv[g][0, rows] = jnp.where(upper, values, keys).astype(bf16)
        kv[g][1, rows] = jnp.where(upper, keys, values).astype(bf16)

    def query(h):
        lane_ext = jnp.where(lanes == LEFT, line[h : h + 1, 0:1],
                             jnp.where(lanes == RIGHT, line[h : h + 1, 3 * t - 1 : 3 * t], ext[...]))
        q2 = q[:, h // 2 * 128 : h // 2 * 128 + 128].astype(f32)
        return jnp.concatenate([jnp.where(upper == (h % 2 == 1), q2, 0.0), lane_ext], axis=1).astype(bf16)

    def keys_of(h, i):
        rows = slice(i * t, (i + 1) * t)
        return jnp.concatenate([kv[h // 2][h % 2, rows], e[rows]], axis=1)

    def score(h, i, qa, top):
        block = nt(qa, keys_of(h, i))
        if i in near:
            away = (me ^ (first + i)) - me
            block = block + bands[h, jnp.where(jnp.abs(away) <= 1, away + 1, 3)].astype(f32)
        s[h % 2, :, i * t : (i + 1) * t] = block
        here = block[:, :128]
        for c in range(1, t // 128):
            here = jnp.maximum(here, block[:, c * 128 : (c + 1) * 128])
        return here if top is None else jnp.maximum(top, here)

    def mix(h, i, top, out):
        raised = jnp.exp(s[h % 2, :, i * t : (i + 1) * t] - top).astype(bf16)
        p[h // 2][h % 2, :, i * t : (i + 1) * t] = raised
        more = nn(raised, keys_of(h, i))
        return more if out is None else out + more

    for g in range(pairs):
        for i in range(count):
            project(g, i)
    stats = jnp.zeros((t, 128), f32)
    last = None
    sums = []
    for h in range(2 * pairs + 1):
        qa = query(h) if h < 2 * pairs else None
        top = out = None
        for i in range(count):
            if h < 2 * pairs:
                top = score(h, i, qa, top)
            if h > 0:
                out = mix(h - 1, i, last, out)
        if h > 0:
            stats = jnp.where(lanes == h - 1, last, stats)
            stats = jnp.where(lanes == 7 + h, out[:, 128 + ONES : 129 + ONES], stats)
            sums.append(out[:, :128])
        if h < 2 * pairs:
            last = jnp.max(top, axis=1, keepdims=True)
    for g in range(pairs):
        acc[:, g * 128 : g * 128 + 128] = turn(jnp.where(upper, sums[2 * g], sums[2 * g + 1]))
    stat[...] = stats


def attend(n, first, ids, lens, blocks, gain, wk, wv, q, ext, bands, line):
    count = len(blocks)
    blocks = [piece for block in blocks for piece in block]
    t, d = q.shape[0], wk.shape[0]
    pairs = wk.shape[1] // 128
    c = count * t
    out = call(
        partial(attend_kernel, n, first, count, len(blocks)), "attend", 2 * count,
        [shape(c, d), shape(c, 128), shape(t, wk.shape[1], dtype=f32), shape(t, 128, dtype=f32)]
        + [shape(2, c, 128)] * pairs + [shape(2, t, c)] * pairs,
        (ids, lens), (*blocks, gain, wk, wv, q, ext, bands, line), scratch=[pltpu.VMEM((2, t, c), f32)], much=n > 8,
    )
    return dict(n1=out[0], e=out[1], acc=out[2], stat=out[3], kv=out[4 : 4 + pairs], p=out[4 + pairs :])


def feed_forward_kernel(phases, ids, lens, gain, x, wo, wg, wu, wd, cot, *refs):
    accs, stats = refs[:phases], refs[phases : 2 * phases]
    out, dh, do, scale, gwo, keep, send, gn, grads, mixed_all, n2_all, u_all, gb_all, dg_all, du_all, dh_all = refs[2 * phases :]
    t, d = x.shape
    pairs = wo.shape[0] // 128
    chunk = t // FFN_CHUNKS
    lanes = iota((chunk, 128), 1)
    g2 = gain[...].astype(f32)
    last = lens[0]
    for k in range(1, lens.shape[0]):
        last = last + lens[k]
    work = [dict(rows=slice(c * chunk, (c + 1) * chunk)) for c in range(FFN_CHUNKS)]

    def weigh(v):
        rows = v["rows"]
        tops = [ref[rows] for ref in stats]
        top = tops[0]
        for other in tops[1:]:
            top = jnp.maximum(top, other)
        weights = [jnp.exp(a - top) for a in tops]
        total = jnp.where(lanes < 2 * pairs, 0.0, 1.0)
        for w, ref in zip(weights, stats, strict=True):
            total = total + w * pltpu.roll(ref[rows], 120, 1)
        weights = [jnp.where(lanes < 2 * pairs, w / total, 0.0) for w in weights]
        v["scales"] = weights[0]
        for i, w in enumerate(weights[1:], 1):
            v["scales"] = v["scales"] + pltpu.roll(w, 8 * i, 1)
        v["o"] = []
        for g in range(pairs):
            at = slice(g * 128, g * 128 + 128)
            value = jnp.zeros((chunk, 128), f32)
            for i, w in enumerate(weights):
                value = value + accs[i][rows, at] * jnp.where(lanes < 64, w[:, 2 * g : 2 * g + 1], w[:, 2 * g + 1 : 2 * g + 2])
            v["o"].append(value)
            mixed_all[rows, at] = value.astype(bf16)
        pos = ids[0] * t + rows.start + iota((chunk, 1), 0)
        v["g"] = cot[rows].astype(f32) * (pos < last).astype(f32)
        gb_all[rows] = v["g"].astype(bf16)
        v["du"] = nt(gb_all[rows], wd[...]).astype(bf16).astype(f32)

    def norm(v):
        rows = v["rows"]
        v["h1"] = x[rows].astype(f32) + nn(mixed_all[rows], wo[...])
        v["s2"] = lax.rsqrt(jnp.mean(v["h1"] * v["h1"], axis=-1, keepdims=True) + EPS)
        v["hat"] = v["h1"] * v["s2"]
        n2_all[rows] = (v["hat"] * g2).astype(bf16)

    def project(v):
        rows = v["rows"]
        v["gate"], v["up"] = nn(n2_all[rows], wg[...]), nn(n2_all[rows], wu[...])

    def activate(v):
        rows, gate, up = v["rows"], v["gate"], v["up"]
        c0 = 0.7978845608028654
        square = gate * gate
        th = jnp.tanh(c0 * gate * (1.0 + 0.044715 * square))
        half = 0.5 * (1.0 + th)
        act = gate * half
        dact = half + 0.5 * gate * (1.0 - th * th) * (c0 * (1.0 + 3 * 0.044715 * square))
        u_all[rows] = (act * up).astype(bf16)
        dg_all[rows] = (v["du"] * up * dact).astype(bf16)
        du_all[rows] = (v["du"] * act).astype(bf16)

    def down(v):
        rows = v["rows"]
        v["dn2"] = nt(dg_all[rows], wg[...]) + nt(du_all[rows], wu[...])

    def norm_back(v):
        rows, dn2, hat, s2 = v["rows"], v["dn2"], v["hat"], v["s2"]
        out[rows] = (v["h1"] + nn(u_all[rows], wd[...])).astype(bf16)
        v["gn"] = jnp.sum(dn2 * hat, axis=0, keepdims=True)
        scaled = dn2 * g2
        dh1 = v["g"] + s2 * (scaled - hat * jnp.mean(hat * scaled, axis=-1, keepdims=True))
        dh[rows] = dh1
        dh_all[rows] = dh1.astype(bf16)

    def mix_back(v):
        rows = v["rows"]
        dmix = nt(dh_all[rows], wo[...]).astype(bf16)
        do[rows] = dmix
        scales = v["scales"]
        for h in range(2 * pairs):
            at = slice(h // 2 * 128, h // 2 * 128 + 128)
            product = dmix[:, at].astype(f32) * v["o"][h // 2]
            own = jnp.where((lanes < 64) == (h % 2 == 0), product, 0.0)
            scales = jnp.where(lanes == 64 + h, jnp.sum(own, axis=1, keepdims=True), scales)
        scale[rows] = scales

    def weights_kernel():
        low = tn(u_all[...], gb_all[...]).astype(bf16)
        for k, value in enumerate((tn(n2_all[...], dg_all[...]).astype(bf16), tn(n2_all[...], du_all[...]).astype(bf16))):
            for i in range(d // PIECE):
                grads[(3 * i + k) * PIECE : (3 * i + k + 1) * PIECE] = value[i * PIECE : (i + 1) * PIECE]
        for i in range(d // PIECE):
            at = slice((3 * i + 2) * PIECE, (3 * i + 3) * PIECE)
            grads[at, :d] = low[i * PIECE : (i + 1) * PIECE]
            grads[at, d:] = low[d + i * PIECE : d + (i + 1) * PIECE]

    stages = [weigh, norm, project, activate, down, norm_back, mix_back]
    for step in range(len(stages) + FFN_CHUNKS - 1):
        for c, v in enumerate(work):
            if 0 <= step - c < len(stages):
                stages[step - c](v)
        if step == len(stages) + FFN_CHUNKS - 2:
            weights_kernel()
    gn[...] = sum(v["gn"] for v in work)
    gwo[...] = tn(mixed_all[...], dh_all[...]).astype(bf16)
    rows = keep.shape[0]
    keep[...] = grads[pl.ds(pl.multiple_of(ids[1] * rows, 16), rows)]
    send[...] = grads[pl.ds(pl.multiple_of((1 - ids[1]) * rows, 16), rows)]


def feed_forward(ids, lens, gain, x, wo, wg, wu, wd, cot, parts):
    t, d = x.shape
    ff, w = wg.shape[1], wo.shape[0]
    half = 3 * d // 2
    return call(
        partial(feed_forward_kernel, len(parts)), "feed_forward", 8,
        [shape(t, d), shape(t, d, dtype=f32), shape(t, w), shape(t, 128, dtype=f32), shape(w, d),
         shape(half, ff), shape(half, ff), shape(1, d, dtype=f32)],
        (ids, lens), (gain, x, wo, wg, wu, wd, cot, *[v["acc"] for v in parts], *[v["stat"] for v in parts]),
        scratch=[pltpu.VMEM((3 * d, ff), bf16)]
        + [pltpu.VMEM((t, k), bf16) for k in (w, d, ff, d, ff, ff, d)],
    )


def attend_back_kernel(n, pairs, counts, ids, q, do, scale, *refs):
    phases, size = len(counts), len(pairs)
    p = [refs[i * size : (i + 1) * size] for i in range(phases)]
    refs = refs[phases * size :]
    kv = [refs[i * size : (i + 1) * size] for i in range(phases)]
    e, refs = refs[phases * size : phases * size + phases], refs[phases * size + phases :]
    dk, dv, refs = refs[:size], refs[size : 2 * size], refs[2 * size :]
    dq, line, ds = refs
    me = ids[0]
    t = q.shape[0]
    lower = low_half(t)
    back = (iota((t, t), 0) + iota((t, t), 1) == t - 1).astype(f32).astype(bf16)
    lane = iota((1, 128), 1)
    line[...] = jnp.zeros_like(line)
    slots = [(i, j) for i, count in enumerate(counts) for j in range(count)]

    def operands(k):
        h = 2 * pairs[k // 2] + k % 2
        at = slice(h // 2 * 128, h // 2 * 128 + 128)
        qt = jnp.where(lower == (k % 2 == 0), q[:, at].astype(f32), 0.0).T
        doh = jnp.where(lower == (k % 2 == 1), turn(do[:, at].astype(f32)), 0.0)
        out = []
        for i in range(phases):
            factor = scale[:, 8 * i + h : 8 * i + h + 1]
            scaled = doh * factor
            shift = scale[:, 64 + h : 65 + h] * factor
            out.append((scaled.astype(bf16), shift, jnp.concatenate([qt, scaled.T], axis=1).astype(bf16)))
        return out

    def start(k, s, ops):
        i, j = slots[s]
        return nt(ops[i][0], kv[i][k // 2][k % 2, j * t : (j + 1) * t])

    def finish(k, s, ops, d_prob, acc):
        i, j = slots[s]
        rows = slice(j * t, (j + 1) * t)
        probs = p[i][k // 2][k % 2, :, rows]
        d_score = (probs.astype(f32) * (d_prob - ops[i][1])).astype(bf16)
        ds[k % 2, :, s * t : (s + 1) * t] = d_score
        more = nn(d_score, jnp.concatenate([kv[i][k // 2][k % 2, rows], e[i][rows]], axis=1))
        both = nn(ops[i][2], jnp.concatenate([d_score, probs], axis=0)).astype(bf16)
        mine, other = (both[:64], both[64:]) if k % 2 == 0 else (both[64:], both[:64])
        dk[k // 2][k % 2 * 64 : k % 2 * 64 + 64, s * t : (s + 1) * t] = mine
        dv[k // 2][k % 2 * 64 : k % 2 * 64 + 64, s * t : (s + 1) * t] = other
        return more if acc is None else acc + more

    def bias(k, acc):
        parts = []
        for r in (-1, 0, 1):
            there = me + r
            inside = (there >= 0) & (there < n)
            slot = jnp.where(inside, me ^ there, 0)
            block = ds[k % 2, :, pl.ds(pl.multiple_of(slot * t, t), t)]
            parts.append(nn(back, block) * inside.astype(f32))
        parts.append(jnp.zeros((t, t), f32))
        band = pltpu.roll(jnp.concatenate(parts, axis=1), 0, 1, stride=1, stride_axis=0)
        line[k : k + 1, : 4 * t] = jnp.sum(band, axis=0, keepdims=True)
        ends = jnp.sum(acc[:, 128:], axis=0, keepdims=True)
        line[k : k + 1, 4 * t :] = jnp.where((lane == LEFT) | (lane == RIGHT), ends, 0.0)

    tasks = [(k, s) for k in range(2 * size) for s in range(len(slots))]
    ops = [operands(0)]
    d_prob = start(0, 0, ops[0])
    accs = [None] * (2 * size)
    for index, (k, s) in enumerate(tasks):
        if s == 0 and k + 1 < 2 * size:
            ops.append(operands(k + 1))
        later = None
        if index + 1 < len(tasks):
            k2, s2 = tasks[index + 1]
            later = start(k2, s2, ops[k2])
        accs[k] = finish(k, s, ops[k], d_prob, accs[k])
        d_prob = later
        if s == len(slots) - 1:
            bias(k, accs[k])
    for g in range(size):
        dq[:, g * 128 : g * 128 + 128] = jnp.where(lower, accs[2 * g][:, :128], accs[2 * g + 1][:, :128]).astype(bf16)


def attend_back(n, pairs, ids, q, do, scale, parts):
    t = q.shape[0]
    widths = [v["e"].shape[0] for v in parts]
    s = sum(widths)
    size = len(pairs)
    out = call(
        partial(attend_back_kernel, n, pairs, [w // t for w in widths]), "attend_back", 4 * size,
        [shape(128, s)] * (2 * size) + [shape(t, 128 * size), shape(8, 4 * t + 128, dtype=f32)],
        (ids,), (q, do, scale, *[v["p"][g] for v in parts for g in pairs],
                 *[v["kv"][g] for v in parts for g in pairs], *[v["e"] for v in parts]),
        scratch=[pltpu.VMEM((2, t, s), bf16)], much=n > 8,
    )
    return dict(dk=out[:size], dv=out[size : 2 * size], dq=out[-2], line=out[-1], pairs=size)


def gather_back_kernel(n, buckets, counts, pairs, ids, gain, gn, gwo, wq, wk, wv, wt, *refs):
    phases = len(counts)
    n1, refs = refs[:phases], refs[phases:]
    total_pairs = sum(pairs)
    dkv, refs = refs[: 2 * total_pairs], refs[2 * total_pairs :]
    dq, lines = refs[: len(pairs)], refs[len(pairs) : 2 * len(pairs)]
    even, odd, dn1q, keep, send, grads, sums, diagonal = refs[2 * len(pairs) :]
    d, w = wq.shape
    t = dn1q.shape[0]
    weights = jnp.concatenate([wk[...], wv[...]], axis=1)
    total = jnp.zeros((2 * w, d), f32)
    slot = 0
    for i, count in enumerate(counts):
        begin = sum(counts[:i]) * t
        both = jnp.concatenate([ref[:, begin : begin + count * t] for ref in dkv], axis=0)
        total = total + nn(both, n1[i][...])
        back = nn(weights, both).astype(bf16)
        for _ in range(count):
            ref = odd if slot % 2 else even
            ref[slot // 2] = back[:, slot * t - begin : slot * t - begin + t]
            slot += 1
    dq_all = jnp.concatenate([ref[...] for ref in dq], axis=1)
    from_q = tn(dq_all, n1[0][:t])
    dn1q[...] = nt(dq_all, wq[...])
    grads[:w] = from_q.astype(bf16)
    grads[w : 3 * w] = total.astype(bf16)
    grads[3 * w :] = gwo[...]
    gains = jnp.sum(from_q * wt[:w].astype(f32), axis=0, keepdims=True)
    gains = gains + jnp.sum(total * wt[w:].astype(f32), axis=0, keepdims=True)
    sums[...] = jnp.zeros_like(sums)
    sums[0:1] = gains / gain[...].astype(f32)
    sums[1:2] = gn[...]
    diagonal[...] = jnp.zeros_like(diagonal)
    begin = 0
    for ref, count in zip(lines, pairs, strict=True):
        diagonal[begin : begin + 2 * count] = ref[: 2 * count]
        begin += 2 * count
    width = diagonal.shape[1]
    u = iota((width, 128), 0)
    bucket = bucket_of(u - (2 * t - 1), buckets)
    bucket = jnp.where(u == 4 * t + LEFT, buckets // 2 - 1, jnp.where(u == 4 * t + RIGHT, buckets - 1, bucket))
    pick = (bucket == iota((width, 128), 1)).astype(f32)
    sums[8:16, :128] = lax.dot_general(diagonal[...], pick, (((1,), (0,)), ((), ())),
                                       precision=lax.Precision.HIGHEST, preferred_element_type=f32)
    small = sums[...].astype(bf16)
    rows = 2 * w
    keep[:rows] = grads[pl.ds(pl.multiple_of(ids[1] * rows, 16), rows)]
    send[:rows] = grads[pl.ds(pl.multiple_of((1 - ids[1]) * rows, 16), rows)]
    keep[rows:] = small
    send[rows:] = small


def gather_back(n, buckets, ids, gain, gn, gwo, wq, wk, wv, wt, parts, backs):
    d, w = wq.shape
    t = backs[0]["dq"].shape[0]
    pairs = [v["pairs"] for v in backs]
    counts = [v["e"].shape[0] // t for v in parts]
    pieces = [ref for v in backs for ref in v["dk"]] + [ref for v in backs for ref in v["dv"]]
    half = 2 * w + SMALL
    return call(
        partial(gather_back_kernel, n, buckets, counts, pairs), "gather_back", 6,
        [shape(n // 2, d, t), shape(n // 2, d, t), shape(t, d, dtype=f32), shape(half, d), shape(half, d)],
        (ids,), (gain, gn, gwo, wq, wk, wv, wt, *[v["n1"] for v in parts], *pieces, *[v["dq"] for v in backs],
                 *[v["line"] for v in backs]),
        scratch=[pltpu.VMEM((4 * w, d), bf16), pltpu.VMEM((SMALL, d), f32), pltpu.VMEM((8, 4 * t + 128), f32)], much=n > 8,
    )


def rest_back_kernel(n, buckets, pairs, counts, sizes, ids, *refs):
    first, second, outs, inner = (refs[a:b] for a, b in zip(sizes[:-1], sizes[1:], strict=True))
    size = len(pairs)
    dkv, (dq, line), ds = inner[: 2 * size], inner[2 * size : 2 * size + 2], inner[2 * size + 2]
    attend_back_kernel(n, pairs, counts, ids, *first, *dkv, dq, line, ds)
    head, (dk0, dv0, dq0, line0) = second[: 7 + len(counts)], second[7 + len(counts) :]
    gather_back_kernel(n, buckets, counts, [1, size], ids, *head, dk0, *dkv[:size], dv0, *dkv[size:], dq0, dq, line0, line,
                       *outs, *inner[2 * size + 3 :])


def rest_back(n, buckets, pairs, ids, q, do, scale, gain, gn, gwo, wq, wk, wv, wt, parts, back):
    d, w = wq.shape
    t = q.shape[0]
    widths = [v["e"].shape[0] for v in parts]
    s, size, half = sum(widths), len(pairs), 2 * w + SMALL
    first = (q, do, scale, *[v["p"][g] for v in parts for g in pairs], *[v["kv"][g] for v in parts for g in pairs],
             *[v["e"] for v in parts])
    second = (gain, gn, gwo, wq, wk, wv, wt, *[v["n1"] for v in parts], back["dk"][0], back["dv"][0], back["dq"], back["line"])
    cuts = [0, len(first), len(first) + len(second), len(first) + len(second) + 5]
    inner = [pltpu.VMEM((128, s), bf16)] * (2 * size) + [pltpu.VMEM((t, 128 * size), bf16), pltpu.VMEM((8, 4 * t + 128), f32),
             pltpu.VMEM((2, t, s), bf16), pltpu.VMEM((4 * w, d), bf16), pltpu.VMEM((SMALL, d), f32),
             pltpu.VMEM((8, 4 * t + 128), f32)]
    return call(
        partial(rest_back_kernel, n, buckets, pairs, [v // t for v in widths], [*cuts, cuts[-1] + len(inner)]), "rest_back", 10,
        [shape(n // 2, d, t), shape(n // 2, d, t), shape(t, d, dtype=f32), shape(half, d), shape(half, d)],
        (ids,), (*first, *second), scratch=inner,
    )


def split_kernel(which, count, extra, ids, *refs):
    inputs, outs = refs[:-count], refs[-count:]
    rows = (inputs[0].shape[0] - extra) // count
    own = ids[which]
    for j in range(count):
        at = pl.ds(pl.multiple_of((own ^ j) * rows, 16), rows)
        total = inputs[0][at].astype(f32)
        for ref in inputs[1:]:
            total = total + ref[at].astype(f32)
        outs[j][:rows] = total.astype(bf16)
    if extra:
        at = pl.ds(rows * count, extra)
        total = inputs[0][at].astype(f32)
        for ref in inputs[1:]:
            total = total + ref[at].astype(f32)
        for j in range(count):
            outs[j][rows:] = total.astype(bf16)


def add_and_split(which, count, extra, ids, *arrays):
    rows = (arrays[0].shape[0] - extra) // count + extra
    out = shape(rows, arrays[0].shape[1])
    return call(partial(split_kernel, which, count, extra), "add_parts", 1, [out] * count, (ids,), arrays)


def by_chip_kernel(ids, keep, recv, *outs):
    rows = keep.shape[0] // 4
    for half, own in ((0, ids[2] % 2), (1, ids[2] // 2)):
        for j in range(2):
            at = pl.ds(pl.multiple_of((2 * half + (own ^ j)) * rows, 16), rows)
            outs[2 * half + j][...] = (keep[at].astype(f32) + recv[at].astype(f32)).astype(bf16)


def by_next_chip_kernel(ids, keep_x, recv_x, keep_y, recv_y, *outs):
    rows = keep_x.shape[0] // 2
    for half, own, a, b in ((0, ids[2] // 2, keep_x, recv_x), (1, ids[2] % 2, keep_y, recv_y)):
        for j in range(2):
            at = pl.ds(pl.multiple_of((own ^ j) * rows, 16), rows)
            outs[2 * half + j][...] = (a[at].astype(f32) + b[at].astype(f32)).astype(bf16)


def by_row_kernel(ids, keep_x, recv_x, keep_y, recv_y, mine, other):
    first = keep_x[...].astype(f32) + recv_x[...].astype(f32)
    second = keep_y[...].astype(f32) + recv_y[...].astype(f32)
    even = ids[3] % 2 == 0
    mine[...] = jnp.where(even, first, second).astype(bf16)
    other[...] = jnp.where(even, second, first).astype(bf16)


def pick_kernel(ids, mine, other, first, second):
    even = ids[3] % 2 == 0
    a, b = mine[...].astype(f32), other[...].astype(f32)
    first[...] = jnp.where(even, a, b).astype(bf16)
    second[...] = jnp.where(even, b, a).astype(bf16)


def stack_kernel(ids, *refs):
    *parts, out = refs
    rows = parts[0].shape[0]
    for i, ref in enumerate(parts):
        out[i * rows : (i + 1) * rows] = ref[...]


def join_kernel(ids, a, b, c, d, first, second):
    rows = a.shape[0]
    first[:rows], first[rows:] = a[...], b[...]
    second[:rows], second[rows:] = c[...], d[...]


def swap(array, axis, j):
    size = lax.axis_size(axis)
    return lax.ppermute(array, axis, [(i, i ^ j) for i in range(size)])


def order(first, *values):
    first, values = lax.optimization_barrier((first, values))
    return values if len(values) > 1 else values[0]


def sum_all(ids, keep, recv, extra):
    both = add_and_split(0, 1, extra, ids * 0, keep, recv)[0].astype(f32)
    size = both.shape[0] - extra
    placed = jnp.zeros((2 * size, both.shape[1]), f32)
    placed = lax.dynamic_update_slice_in_dim(placed, both[:size], ids[1] * size, 0)
    full, tail = lax.psum((placed, both[size:] * 0.5), ("rows", "seq"))
    mine = lax.dynamic_slice_in_dim(full, ids[1] * size, size, 0)
    other = lax.dynamic_slice_in_dim(full, (1 - ids[1]) * size, size, 0)
    return [mine.astype(bf16)], [other.astype(bf16)], tail.astype(bf16)


def to_chips(parts):
    return [parts[0]] + [swap(parts[j], "seq", 2 * j) for j in range(1, len(parts))]


def place_halves(ids, mine, other, full):
    size = full.shape[0] // 2
    if len(mine) == 1:
        full[pl.ds(pl.multiple_of(ids[1] * size, 16), size)] = mine[0][...]
        full[pl.ds(pl.multiple_of((1 - ids[1]) * size, 16), size)] = other[0][...]
        return
    piece = size // len(mine)
    for c, refs in ((ids[1], mine), (1 - ids[1], other)):
        for a, ref in enumerate(refs):
            at = c * size + (ids[2] ^ a) * piece
            for b in range(2):
                where = at + ((ids[3] % 2) ^ b) * (piece // 2)
                full[pl.ds(pl.multiple_of(where, 16), piece // 2)] = ref[b * (piece // 2) : (b + 1) * (piece // 2)]


def send_out(copies, source, target, sem):
    copies.append(pltpu.make_async_copy(source, target, sem))
    copies[-1].start()


def write_ffn(far, ids, parts, gate, up, down, full, sems):
    d = gate.shape[0]
    x, y = ids[2] % 2, ids[2] // 2
    rows = 3 * PIECE
    copies = []
    for c, *pair in parts:
        for half, first, second in ((0, x, y), (1, y, x)):
            for b in range(2):
                k = len(copies) // 4
                piece = 8 * c + 4 * half + 2 * (first ^ far) + (second ^ b)
                full[k] = pair[half][b * rows : (b + 1) * rows].astype(f32)
                at = pl.multiple_of(piece * PIECE, PIECE)
                send_out(copies, full.at[k, :PIECE], gate.at[pl.ds(at, PIECE)], sems.at[4 * k])
                send_out(copies, full.at[k, PIECE : 2 * PIECE], up.at[pl.ds(at, PIECE)], sems.at[4 * k + 1])
                send_out(copies, full.at[k, 2 * PIECE :, :d], down.at[pl.ds(at, PIECE)], sems.at[4 * k + 2])
                send_out(copies, full.at[k, 2 * PIECE :, d:], down.at[pl.ds(d + at, PIECE)], sems.at[4 * k + 3])
    return copies


def unpack_near_kernel(ids, *refs):
    for copy in write_ffn(0, ids, ((ids[1], *refs[:2]), (1 - ids[1], *refs[2:4])), *refs[4:]):
        copy.wait()


def unpack_half_kernel(other, filled, chips, ids, *refs):
    (x, y, *stacks), refs = refs[:4], refs[4 + filled :]
    gate, up, down, gq, gk, gv, go, full, sems, both, wide, tall, sem2 = refs
    core = ids[1] ^ other
    copies = write_ffn(1, ids, ((core, x, y),), gate, up, down, full, sems)
    rows = stacks[0].shape[0] // chips
    for k, stack in enumerate(stacks):
        for a in range(chips):
            where = ((ids[2] ^ a) * 2 + ((ids[3] % 2) ^ k)) * rows
            both[pl.ds(pl.multiple_of(where, 16), rows)] = stack[a * rows : (a + 1) * rows]
    w = wide.shape[2]

    def finish(matrices):
        moves = []
        for i, (ref, turned) in enumerate(matrices):
            value = both[i * w : (i + 1) * w].astype(f32)
            source = wide.at[i] if turned else tall
            source[...] = value.T if turned else value
            send_out(moves, source, ref, sem2.at[i])
        for copy in moves:
            copy.wait()

    @pl.when(core == 0)
    def _():
        finish(((gq, True), (gk, True)))

    @pl.when(core == 1)
    def _():
        finish(((gv, True), (go, False)))

    for copy in copies:
        copy.wait()


def unpack(kernel, ids, vmem_args, filled, out_shape, scratch):
    vmem, hbm = pl.BlockSpec(memory_space=pltpu.VMEM), pl.BlockSpec(memory_space=pl.ANY)
    return pl.pallas_call(
        kernel,
        in_specs=[pl.BlockSpec(memory_space=pltpu.SMEM)] + [vmem] * len(vmem_args) + [hbm] * len(filled),
        out_specs=[hbm] * len(out_shape),
        out_shape=out_shape,
        scratch_shapes=scratch,
        input_output_aliases={1 + len(vmem_args) + i: i for i in range(len(filled))},
        compiler_params=pltpu.CompilerParams(vmem_limit_bytes=VMEM),
        cost_estimate=pl.CostEstimate(flops=1000, bytes_accessed=1000, transcendentals=0),
        name="unpack",
    )(ids, *vmem_args, *filled)


def unpack_ffn_halves(ids, mine, other, d, ff):
    full = jnp.where(ids[1] == 0, jnp.concatenate([mine, other]), jnp.concatenate([other, mine])).astype(f32)
    full = full.reshape(d // PIECE, 3, PIECE, ff)
    low = full[:, 2].reshape(d, ff)
    return full[:, 0].reshape(d, ff), full[:, 1].reshape(d, ff), jnp.concatenate([low[:, :d], low[:, d:]])


def unpack_attention_kernel(pieces, ids, *refs):
    gq, gk, gv, go, full = refs[2 * pieces :]
    place_halves(ids, refs[:pieces], refs[pieces : 2 * pieces], full)
    w = gq.shape[1]
    for k, ref in enumerate((gq, gk, gv)):
        ref[...] = full[k * w : (k + 1) * w].astype(f32).T
    go[...] = full[3 * w :].astype(f32)


def unpack_small_kernel(ids, tail, g1, g2, gb):
    small = tail[...].astype(f32)
    g1[...] = small[0:1]
    g2[...] = small[1:2]
    gb[...] = small[8 : 8 + gb.shape[0], : gb.shape[1]]


def input_grad_kernel(ids, *refs):
    *parts, dn1q, x, dh, gain, out = refs
    total = parts[0][...].astype(f32)
    for ref in parts[1:]:
        total = total + ref[...].astype(f32)
    dn1 = total.T + dn1q[...]
    value = x[...].astype(f32)
    s1 = lax.rsqrt(jnp.mean(value * value, axis=-1, keepdims=True) + EPS)
    hat = value * s1
    scaled = dn1 * gain[...].astype(f32)
    out[...] = dh[...] + s1 * (scaled - hat * jnp.mean(hat * scaled, axis=-1, keepdims=True))


def slots_kernel(count, ids, mine, other, *outs):
    for j in range(count):
        outs[j][...] = (mine[j].astype(f32) + other[j].astype(f32)).astype(bf16)


def shards(
    tokens, norm_attn, query_weight, key_weight, value_weight, out_weight, bucket_bias_table, norm_ffn,
    gate_weight, expansion_matrix, down_weight, lengths, cotangent,
):
    _, t, d = tokens.shape
    n = lax.axis_size("seq")
    buckets, heads = bucket_bias_table.shape
    width = query_weight.shape[1]
    ff = gate_weight.shape[1]
    seq = lax.axis_index("seq")
    ids = jnp.stack([seq, seq % 2, seq // 2, lax.axis_index("rows")]).astype(i32)
    x = tokens.reshape(t, d)
    cot = cotangent.reshape(t, d)
    lens = lengths.reshape(-1)
    gain1 = norm_attn.reshape(1, d)
    gain2 = norm_ffn.reshape(1, d)

    blocks = [[x], [swap(x, "seq", 1)]] + [None] * (n - 2)
    for j in range(2, n, 2):
        if n != 8 or j != 6:
            blocks[j] = [swap(x, "seq", j)]
    q, ext, bands, wt, line, x, wq, wk, wv = prepare(
        ids, lens, x, gain1, bucket_bias_table.T, query_weight, key_weight, value_weight
    )
    blocks[0] = [x]
    cuts = [0, 2, 6, *range(8, n, 8), n]

    def phase(a, b):
        return attend(n, a, ids, lens, blocks[a:b], gain1, wk, wv, q, ext, bands, line)

    parts = []
    for a, b in zip(cuts[:-1], cuts[1:], strict=True):
        for j in range(a, b, 2):
            if j:
                blocks[j] = [order(parts[-1]["acc"], v) for v in blocks[j]]
                blocks[j + 1] = [swap(v, "seq", 1) for v in blocks[j]]
        if n == 8 and a == 2:
            blocks[6] = [swap(blocks[4][0][: t // 2], "seq", 2), swap(blocks[2][0][t // 2 :], "seq", 4)]
        parts.append(phase(a, b))
    output, dh, do, scale, gwo, keep, send, gn = feed_forward(
        ids, lens, gain2, x, out_weight, gate_weight, expansion_matrix, down_weight, cot, parts
    )
    half = n // 2
    pairs = width // 128
    whole = n != 8 or lax.axis_size("rows") != 4
    zero, near = ids * 0, ids[3:4] % 2

    def unpack_attention(mine, other):
        return call(
            partial(unpack_attention_kernel, len(mine)), "unpack_attention", 3,
            [shape(d, width, dtype=f32)] * 3 + [shape(width, d, dtype=f32)],
            (ids,), (*mine, *other), scratch=[pltpu.VMEM((4 * width, d), bf16)],
        )

    def unpack_small(tail):
        return call(unpack_small_kernel, "unpack_small", 1,
                    [shape(1, d, dtype=f32)] * 2 + [shape(heads, buckets, dtype=f32)], (ids,), (tail,))

    def input_grad(slots):
        return call(input_grad_kernel, "input_grad", 2, shape(t, d, dtype=f32), (ids,), (*slots, dn1q, x, dh, gain1))

    def add_slots(recv):
        return call(partial(slots_kernel, half), "add_slots", 1, [shape(d, t)] * half, (ids,), (even, recv))

    f_core = swap(send, "seq", 1)
    back = attend_back(n, [0], ids, q, do, scale, parts)
    f_keep = keep
    if whole:
        backs = [back, attend_back(n, list(range(1, pairs)), ids, q, do, scale, parts)]
        even, odd, dn1q, keep, send = gather_back(n, buckets, ids, gain1, gn, gwo, wq, wk, wv, wt, parts, backs)
        a_core, d_core = swap(send, "seq", 1), swap(odd, "seq", 1)
        mine, other, _ = sum_all(ids, f_keep, f_core, 0)
        gate, up, down = unpack_ffn_halves(ids, mine[0], other[0], d, ff)
        grad_tokens = input_grad(to_chips(add_slots(d_core)))
        mine, other, tail = sum_all(ids, keep, a_core, SMALL)
        gq, gk, gv, go = unpack_attention(mine, other)
        g1, g2, gb = unpack_small(tail)
    else:
        part = lambda rows: shape(f_keep.shape[0] // rows, ff)
        f_core = order(back["dq"], f_core)
        f_x, f_x2, f_y, f_y2 = call(by_chip_kernel, "add_parts", 1, [part(4)] * 4, (ids,), (keep, f_core))
        do = order(f_x, do)
        f_x2, f_y2 = swap(f_x2, "seq", 2), swap(f_y2, "seq", 4)
        even, odd, dn1q, keep, send = rest_back(
            n, buckets, list(range(1, pairs)), ids, q, do, scale, gain1, gn, gwo, wq, wk, wv, wt, parts, back
        )
        send, odd = order((f_x2, f_y2), send, odd)
        live = dict(a=swap(send, "seq", 1), d=swap(odd, "seq", 1))
        f_x, f_x2, f_y, f_y2 = call(
            by_next_chip_kernel, "add_parts", 1, [part(8)] * 4, (ids,), (f_x, f_x2, f_y, f_y2)
        )
        live["f"] = [swap(f_x2, "seq", 4), swap(f_y2, "seq", 2)]
        size = (keep.shape[0] - SMALL) // 8
        ffn_out = [shape(d, ff, dtype=f32), shape(d, ff, dtype=f32), shape(ff, d, dtype=f32)]
        ffn_scratch = [pltpu.VMEM((8, 3 * PIECE, ff), f32), pltpu.SemaphoreType.DMA((32,))]
        kept = dict(f=(f_x, f_y))

        def f_rows():
            (f_x, f_y), (f_x2, f_y2) = kept["f"], live["f"]
            mine, other = call(by_row_kernel, "add_parts", 1, [part(8)] * 2, (ids,), (f_x, f_x2, f_y, f_y2))
            kept["f"], live["f"] = mine, swap(other, "rows", 1)
            return mine

        def f_add(j):
            mine = add_and_split(0, 1, 0, zero, kept["f"], live["f"])[0]
            kept["f"], live["f"] = mine, swap(mine, "rows", j)
            return mine

        def f_pick():
            x, y = call(pick_kernel, "pick", 1, [part(8)] * 2, (ids,), (kept["f"], live["f"]))
            kept["f"], live["f"] = (x, y), [swap(x, "seq", 4), swap(y, "seq", 2)]
            return x

        def f_join():
            (x, y), (x2, y2) = kept["f"], live["f"]
            x, y = call(join_kernel, "join", 1, [part(4)] * 2, (ids,), (x, x2, y, y2))
            kept["f"], live["f"] = (x, y), [swap(x, "seq", 2), swap(y, "seq", 4)]
            live["near"] = [swap(v, "seq", 1) for v in (x, y)]
            return x

        def f_near():
            kept["near"] = unpack(unpack_near_kernel, ids, (*kept["f"], *live["near"]), (), ffn_out, ffn_scratch)
            return kept["near"][0]

        def f_swap():
            live["far"] = [swap(v, "seq", 1) for v in live["f"]]
            return None

        def a_chips():
            kept["a"] = add_and_split(2, half, SMALL, ids, keep, live["a"])
            live["a"] = to_chips(kept["a"])
            return kept["a"][0]

        def a_rows():
            kept["a"], other = add_and_split(0, 2, SMALL, near, *live["a"])
            live["a"] = swap(other, "rows", 1)
            return kept["a"]

        def a_add(j):
            kept["a"] = add_and_split(0, 1, SMALL, zero, kept["a"], live["a"])[0]
            live["a"] = swap(kept["a"], "rows", 2) if j == 2 else to_chips([kept["a"][:size]] * half)
            return kept["a"]

        def a_stack():
            kept["stack"] = call(stack_kernel, "stack", 1, shape(half * size, d), (ids,), live["a"])
            live["a"] = swap(kept["stack"], "rows", 1)
            live["anear"] = swap(kept["stack"], "seq", 1)
            return kept["stack"]

        def a_swap():
            live["afar"] = swap(live["a"], "seq", 1)
            return None

        def unpack_half(other, x, y, first, second, filled):
            return unpack(
                partial(unpack_half_kernel, other, len(filled), half), ids, (x, y, first, second), filled,
                ffn_out + [shape(d, width, dtype=f32)] * 3 + [shape(width, d, dtype=f32)],
                [*ffn_scratch, pltpu.VMEM((2 * width, d), bf16), pltpu.VMEM((2, d, width), f32),
                 pltpu.VMEM((width, d), f32), pltpu.SemaphoreType.DMA((2,))],
            )

        def own():
            kept["near"] = unpack_half(0, *live["f"], kept["stack"], live["a"], kept["near"])
            return kept["near"][0]

        def last():
            kept["out"] = unpack_half(1, *live["far"], live["anear"], live["afar"], kept["near"])
            return kept["out"][0]

        def d_slots():
            kept["d"] = add_slots(live["d"])
            live["d"] = to_chips(kept["d"])
            return kept["d"][0]

        def d_out():
            kept["tokens"] = input_grad(live["d"])
            return kept["tokens"]

        def small():
            kept["small"] = unpack_small(kept["a"][size:])
            return kept["small"][0]

        steps = dict(
            f_rows=(f_rows, "f"), f_z0=(partial(f_add, 2), "f"), f_z1=(partial(f_add, 1), "f"), f_pick=(f_pick, "f"),
            f_join=(f_join, "f"), f_near=(f_near, "near"), f_swap=(f_swap, "f"), own=(own, "f"), last=(last, "far"),
            a_chips=(a_chips, "a"), a_rows=(a_rows, "a"), a_z0=(partial(a_add, 2), "a"), a_z1=(partial(a_add, 1), "a"),
            a_stack=(a_stack, "a"), a_swap=(a_swap, "a"),
            d_slots=(d_slots, "d"), d_out=(d_out, "d"), small=(small, None),
        )
        token = f_x
        for name in STEPS:
            if ":" in name:
                stream, j = name.split(":")
                live[stream][int(j)] = token = order(token, live[stream][int(j)])
                continue
            step, stream = steps[name]
            if stream is not None:
                live[stream] = order(token, live[stream])
            elif name == "small":
                kept["a"] = order(token, kept["a"])
            done = step()
            token = live[stream] if done is None else done
        gate, up, down, gq, gk, gv, go = kept["out"]
        g1, g2, gb = kept["small"]
        grad_tokens = kept["tokens"]
    return (
        output.reshape(tokens.shape), grad_tokens.reshape(tokens.shape), g1.reshape(d), gq, gk, gv, go, gb.T,
        g2.reshape(d), gate, up, down,
    )


def solution(mesh):
    split = P("rows", "seq", None)
    in_specs = (split,) + (P(),) * 10 + (P("rows", None), split)
    out_specs = (split, split) + (P(),) * 10
    return jax.shard_map(shards, mesh=mesh, in_specs=in_specs, out_specs=out_specs, check_vma=False)
```

```python
from functools import partial

import jax
import jax.numpy as jnp
from jax import lax
from jax.experimental import pallas as pl
from jax.experimental.pallas import tpu as pltpu
from jax.sharding import PartitionSpec as P

EPS = 1e-6
BIG = -(2.0**30)
LEFT, RIGHT, ONES = 17, 18, 19
PIECE = 32
FFN_CHUNKS = 1
STEPS = (
    "a_chips", "f_rows", "f_z0", "a_rows", "d_slots", "f_z1", "f_pick", "a_z0", "d:3", "d_out", "a_z1",
    "f_join", "a_stack", "small", "f_near", "f_swap", "a_swap", "own", "last",
)
SMALL = 16
VMEM = 24 * 1024 * 1024
MUCH = 56 * 1024 * 1024

f32, bf16, i32 = jnp.float32, jnp.bfloat16, jnp.int32


def thresholds(buckets, max_distance):
    half = buckets // 2
    exact = half // 2
    steps = half - exact
    out = list(range(1, exact))
    for j in range(steps):
        target = exact ** (steps - j) * max_distance**j
        m = exact
        while m**steps < target:
            m += 1
        out.append(m)
    return out


def bucket_of(offset, buckets):
    distance = jnp.abs(offset)
    bucket = (offset > 0).astype(i32) * (buckets // 2)
    for t in thresholds(buckets, 128):
        bucket = bucket + (distance >= t).astype(i32)
    return bucket


def nn(a, b):
    return lax.dot_general(a, b, (((1,), (0,)), ((), ())), preferred_element_type=f32)


def nt(a, b):
    return lax.dot_general(a, b, (((1,), (1,)), ((), ())), preferred_element_type=f32)


def tn(a, b):
    return lax.dot_general(a, b, (((0,), (0,)), ((), ())), preferred_element_type=f32)


def iota(shape, dim):
    return lax.broadcasted_iota(i32, shape, dim)


def rms(values, gain):
    scale = lax.rsqrt(jnp.mean(values * values, axis=-1, keepdims=True) + EPS)
    return values * scale * gain


def call(kernel, name, us, out_shape, smem_args, args, scratch=(), much=False, anywhere=0):
    smem = pl.BlockSpec(memory_space=pltpu.SMEM)
    vmem = pl.BlockSpec(memory_space=pltpu.VMEM)
    return pl.pallas_call(
        kernel,
        in_specs=[smem] * len(smem_args) + [vmem] * (len(args) - anywhere) + [pl.BlockSpec(memory_space=pltpu.HBM)] * anywhere,
        out_specs=jax.tree.map(lambda _: vmem, out_shape),
        out_shape=out_shape,
        scratch_shapes=list(scratch),
        compiler_params=pltpu.CompilerParams(vmem_limit_bytes=MUCH if much else VMEM),
        cost_estimate=pl.CostEstimate(flops=int(us * 1e6), bytes_accessed=int(us * 2e3), transcendentals=0),
        name=name,
    )(*smem_args, *args)


def shape(*dims, dtype=bf16):
    return jax.ShapeDtypeStruct(dims, dtype)


def low_half(t):
    return iota((t, 128), 1) < 64


def turn(pair):
    return pltpu.roll(pair, 64, 1)


def prepare_kernel(ids, lens, gain, table, x, w3, q, ext, bands, wt, line, x_here, wq, wk, wv):
    w = wq.shape[1]
    for k, ref in enumerate((wq, wk, wv)):
        ref[...] = w3[:, k * w : (k + 1) * w]
        wt[k * w : (k + 1) * w] = ref[...].astype(f32).T.astype(bf16)
    x_here[...] = x[...]
    t = x.shape[0]
    heads, buckets = table.shape
    low, high = segment_bounds(lens)
    lanes = iota((t, 128), 1)
    pos = iota((t, 128), 0) + ids[0] * t
    other = jnp.where((pos >= low) & (pos < high), 0.0, BIG)
    ext[...] = jnp.where(lanes < LEFT, other, 0.0)
    u = iota((buckets, 4 * t), 1)
    bucket = bucket_of(jnp.where(u < 3 * t, u - t, u - 5 * t), buckets)
    pick = (bucket == iota((buckets, 4 * t), 0)).astype(f32).astype(bf16)
    line[...] = jnp.zeros_like(line)
    line[:heads] = nn(table[...], pick)
    for h in range(heads):
        band = pltpu.roll(jnp.broadcast_to(line[h : h + 1], (t, 4 * t)), 0, 1, stride=1, stride_axis=0)
        for r in range(3):
            bands[h, r] = band[:, r * t : (r + 1) * t].astype(bf16)
        bands[h, 3] = jnp.zeros((t, t), bf16)
    n1 = rms(x[...].astype(f32), gain[...].astype(f32)).astype(bf16)
    q[...] = nn(n1, wq[...]).astype(bf16)


def prepare(ids, lens, x, gain, table, wq, wk, wv):
    t, d = x.shape
    heads, w = table.shape[0], wq.shape[1]
    return call(
        prepare_kernel, "prepare", 4,
        [shape(t, w), shape(t, 128, dtype=f32), shape(heads, 4, t, t), shape(3 * w, d), shape(8, 4 * t, dtype=f32),
         shape(t, d), shape(d, w), shape(d, w), shape(d, w)],
        (ids, lens), (gain, table, x, jnp.concatenate([wq, wk, wv], axis=1)),
    )


def segment_bounds(lens):
    lane = iota((1, 128), 1)
    low = jnp.where(lane == 0, -1, 2**30)
    high = jnp.full((1, 128), -1, i32)
    total = 0
    for k in range(lens.shape[0]):
        total = total + lens[k]
        high = jnp.where(lane == k, total, high)
        low = jnp.where(lane == k + 1, total, low)
    return low, jnp.where(lane == lens.shape[0], 2**30, high)


def attend_kernel(n, first, count, pieces, ids, lens, *refs):
    x, refs = refs[:pieces], refs[pieces:]
    gain, wk, wv, q, ext, bands, line, n1, e, acc, stat = refs[:11]
    pairs = q.shape[1] // 128
    kv, p = refs[11 : 11 + pairs], refs[11 + pairs : -1]
    s = refs[-1]
    me = ids[0]
    t = q.shape[0]
    low, high = segment_bounds(lens)
    row = iota((t, 128), 0)
    lanes = iota((t, 128), 1)
    begin = 0
    for ref in x:
        n1[begin : begin + ref.shape[0]] = rms(ref[...].astype(f32), gain[...].astype(f32)).astype(bf16)
        begin += ref.shape[0]
    for i in range(count):
        at = slice(i * t, (i + 1) * t)
        block = me ^ (first + i)
        pos = row + block * t
        away = block - me
        flag = jnp.where(away <= -2, LEFT, jnp.where(away >= 2, RIGHT, ONES))
        here = ((pos >= low) & (pos < high)) | (lanes == flag) | (lanes == ONES)
        e[at] = here.astype(f32).astype(bf16)
    upper = iota((t, 128), 1) >= 64
    near = [i for i in range(count) if (first + i) & (first + i + 1) == 0]

    def project(g, i):
        rows, at = slice(i * t, (i + 1) * t), slice(g * 128, g * 128 + 128)
        both = nn(n1[rows], jnp.concatenate([wk[:, at], wv[:, at]], axis=1))
        keys, values = both[:, :128], turn(both[:, 128:])
        kv[g][0, rows] = jnp.where(upper, values, keys).astype(bf16)
        kv[g][1, rows] = jnp.where(upper, keys, values).astype(bf16)

    def query(h):
        lane_ext = jnp.where(lanes == LEFT, line[h : h + 1, 0:1],
                             jnp.where(lanes == RIGHT, line[h : h + 1, 3 * t - 1 : 3 * t], ext[...]))
        q2 = q[:, h // 2 * 128 : h // 2 * 128 + 128].astype(f32)
        return jnp.concatenate([jnp.where(upper == (h % 2 == 1), q2, 0.0), lane_ext], axis=1).astype(bf16)

    def keys_of(h, i):
        rows = slice(i * t, (i + 1) * t)
        return jnp.concatenate([kv[h // 2][h % 2, rows], e[rows]], axis=1)

    def score(h, i, qa, top):
        block = nt(qa, keys_of(h, i))
        if i in near:
            away = (me ^ (first + i)) - me
            block = block + bands[h, jnp.where(jnp.abs(away) <= 1, away + 1, 3)].astype(f32)
        s[h % 2, :, i * t : (i + 1) * t] = block
        here = block[:, :128]
        for c in range(1, t // 128):
            here = jnp.maximum(here, block[:, c * 128 : (c + 1) * 128])
        return here if top is None else jnp.maximum(top, here)

    def mix(h, i, top, out):
        raised = jnp.exp(s[h % 2, :, i * t : (i + 1) * t] - top).astype(bf16)
        p[h // 2][h % 2, :, i * t : (i + 1) * t] = raised
        more = nn(raised, keys_of(h, i))
        return more if out is None else out + more

    for g in range(pairs):
        for i in range(count):
            project(g, i)
    stats = jnp.zeros((t, 128), f32)
    last = None
    sums = []
    for h in range(2 * pairs + 1):
        qa = query(h) if h < 2 * pairs else None
        top = out = None
        for i in range(count):
            if h < 2 * pairs:
                top = score(h, i, qa, top)
            if h > 0:
                out = mix(h - 1, i, last, out)
        if h > 0:
            stats = jnp.where(lanes == h - 1, last, stats)
            stats = jnp.where(lanes == 7 + h, out[:, 128 + ONES : 129 + ONES], stats)
            sums.append(out[:, :128])
        if h < 2 * pairs:
            last = jnp.max(top, axis=1, keepdims=True)
    for g in range(pairs):
        acc[:, g * 128 : g * 128 + 128] = turn(jnp.where(upper, sums[2 * g], sums[2 * g + 1]))
    stat[...] = stats


def attend(n, first, ids, lens, blocks, gain, wk, wv, q, ext, bands, line):
    count = len(blocks)
    blocks = [piece for block in blocks for piece in block]
    t, d = q.shape[0], wk.shape[0]
    pairs = wk.shape[1] // 128
    c = count * t
    out = call(
        partial(attend_kernel, n, first, count, len(blocks)), "attend", 2 * count,
        [shape(c, d), shape(c, 128), shape(t, wk.shape[1], dtype=f32), shape(t, 128, dtype=f32)]
        + [shape(2, c, 128)] * pairs + [shape(2, t, c)] * pairs,
        (ids, lens), (*blocks, gain, wk, wv, q, ext, bands, line), scratch=[pltpu.VMEM((2, t, c), f32)], much=n > 8,
    )
    return dict(n1=out[0], e=out[1], acc=out[2], stat=out[3], kv=out[4 : 4 + pairs], p=out[4 + pairs :])


def feed_forward_kernel(phases, ids, lens, gain, x, wo, wg, wu, wd, cot, *refs):
    accs, stats = refs[:phases], refs[phases : 2 * phases]
    out, dh, do, scale, gwo, keep, send, gn, grads, mixed_all, n2_all, u_all, gb_all, dg_all, du_all, dh_all = refs[2 * phases :]
    t, d = x.shape
    pairs = wo.shape[0] // 128
    chunk = t // FFN_CHUNKS
    lanes = iota((chunk, 128), 1)
    g2 = gain[...].astype(f32)
    last = lens[0]
    for k in range(1, lens.shape[0]):
        last = last + lens[k]
    work = [dict(rows=slice(c * chunk, (c + 1) * chunk)) for c in range(FFN_CHUNKS)]

    def weigh(v):
        rows = v["rows"]
        tops = [ref[rows] for ref in stats]
        top = tops[0]
        for other in tops[1:]:
            top = jnp.maximum(top, other)
        weights = [jnp.exp(a - top) for a in tops]
        total = jnp.where(lanes < 2 * pairs, 0.0, 1.0)
        for w, ref in zip(weights, stats, strict=True):
            total = total + w * pltpu.roll(ref[rows], 120, 1)
        weights = [jnp.where(lanes < 2 * pairs, w / total, 0.0) for w in weights]
        v["scales"] = weights[0]
        for i, w in enumerate(weights[1:], 1):
            v["scales"] = v["scales"] + pltpu.roll(w, 8 * i, 1)
        v["o"] = []
        for g in range(pairs):
            at = slice(g * 128, g * 128 + 128)
            value = jnp.zeros((chunk, 128), f32)
            for i, w in enumerate(weights):
                value = value + accs[i][rows, at] * jnp.where(lanes < 64, w[:, 2 * g : 2 * g + 1], w[:, 2 * g + 1 : 2 * g + 2])
            v["o"].append(value)
            mixed_all[rows, at] = value.astype(bf16)
        pos = ids[0] * t + rows.start + iota((chunk, 1), 0)
        v["g"] = cot[rows].astype(f32) * (pos < last).astype(f32)
        gb_all[rows] = v["g"].astype(bf16)
        v["du"] = nt(gb_all[rows], wd[...]).astype(bf16).astype(f32)

    def norm(v):
        rows = v["rows"]
        v["h1"] = x[rows].astype(f32) + nn(mixed_all[rows], wo[...])
        v["s2"] = lax.rsqrt(jnp.mean(v["h1"] * v["h1"], axis=-1, keepdims=True) + EPS)
        v["hat"] = v["h1"] * v["s2"]
        n2_all[rows] = (v["hat"] * g2).astype(bf16)

    def project(v):
        rows = v["rows"]
        v["gate"], v["up"] = nn(n2_all[rows], wg[...]), nn(n2_all[rows], wu[...])

    def activate(v):
        rows, gate, up = v["rows"], v["gate"], v["up"]
        c0 = 0.7978845608028654
        square = gate * gate
        th = jnp.tanh(c0 * gate * (1.0 + 0.044715 * square))
        half = 0.5 * (1.0 + th)
        act = gate * half
        dact = half + 0.5 * gate * (1.0 - th * th) * (c0 * (1.0 + 3 * 0.044715 * square))
        u_all[rows] = (act * up).astype(bf16)
        dg_all[rows] = (v["du"] * up * dact).astype(bf16)
        du_all[rows] = (v["du"] * act).astype(bf16)

    def down(v):
        rows = v["rows"]
        v["dn2"] = nt(dg_all[rows], wg[...]) + nt(du_all[rows], wu[...])

    def norm_back(v):
        rows, dn2, hat, s2 = v["rows"], v["dn2"], v["hat"], v["s2"]
        out[rows] = (v["h1"] + nn(u_all[rows], wd[...])).astype(bf16)
        v["gn"] = jnp.sum(dn2 * hat, axis=0, keepdims=True)
        scaled = dn2 * g2
        dh1 = v["g"] + s2 * (scaled - hat * jnp.mean(hat * scaled, axis=-1, keepdims=True))
        dh[rows] = dh1
        dh_all[rows] = dh1.astype(bf16)

    def mix_back(v):
        rows = v["rows"]
        dmix = nt(dh_all[rows], wo[...]).astype(bf16)
        do[rows] = dmix
        scales = v["scales"]
        for h in range(2 * pairs):
            at = slice(h // 2 * 128, h // 2 * 128 + 128)
            product = dmix[:, at].astype(f32) * v["o"][h // 2]
            own = jnp.where((lanes < 64) == (h % 2 == 0), product, 0.0)
            scales = jnp.where(lanes == 64 + h, jnp.sum(own, axis=1, keepdims=True), scales)
        scale[rows] = scales

    def weights_kernel():
        low = tn(u_all[...], gb_all[...]).astype(bf16)
        for k, value in enumerate((tn(n2_all[...], dg_all[...]).astype(bf16), tn(n2_all[...], du_all[...]).astype(bf16))):
            for i in range(d // PIECE):
                grads[(3 * i + k) * PIECE : (3 * i + k + 1) * PIECE] = value[i * PIECE : (i + 1) * PIECE]
        for i in range(d // PIECE):
            at = slice((3 * i + 2) * PIECE, (3 * i + 3) * PIECE)
            grads[at, :d] = low[i * PIECE : (i + 1) * PIECE]
            grads[at, d:] = low[d + i * PIECE : d + (i + 1) * PIECE]

    stages = [weigh, norm, project, activate, down, norm_back, mix_back]
    for step in range(len(stages) + FFN_CHUNKS - 1):
        for c, v in enumerate(work):
            if 0 <= step - c < len(stages):
                stages[step - c](v)
        if step == len(stages) + FFN_CHUNKS - 2:
            weights_kernel()
    gn[...] = sum(v["gn"] for v in work)
    gwo[...] = tn(mixed_all[...], dh_all[...]).astype(bf16)
    rows = keep.shape[0]
    keep[...] = grads[pl.ds(pl.multiple_of(ids[1] * rows, 16), rows)]
    send[...] = grads[pl.ds(pl.multiple_of((1 - ids[1]) * rows, 16), rows)]


def feed_forward(ids, lens, gain, x, wo, wg, wu, wd, cot, parts):
    t, d = x.shape
    ff, w = wg.shape[1], wo.shape[0]
    half = 3 * d // 2
    return call(
        partial(feed_forward_kernel, len(parts)), "feed_forward", 8,
        [shape(t, d), shape(t, d, dtype=f32), shape(t, w), shape(t, 128, dtype=f32), shape(w, d),
         shape(half, ff), shape(half, ff), shape(1, d, dtype=f32)],
        (ids, lens), (gain, x, wo, wg, wu, wd, cot, *[v["acc"] for v in parts], *[v["stat"] for v in parts]),
        scratch=[pltpu.VMEM((3 * d, ff), bf16)]
        + [pltpu.VMEM((t, k), bf16) for k in (w, d, ff, d, ff, ff, d)],
    )


def attend_back_kernel(n, pairs, counts, ids, q, do, scale, *refs):
    phases, size = len(counts), len(pairs)
    p = [refs[i * size : (i + 1) * size] for i in range(phases)]
    refs = refs[phases * size :]
    kv = [refs[i * size : (i + 1) * size] for i in range(phases)]
    e, refs = refs[phases * size : phases * size + phases], refs[phases * size + phases :]
    dk, dv, refs = refs[:size], refs[size : 2 * size], refs[2 * size :]
    dq, line, ds = refs
    me = ids[0]
    t = q.shape[0]
    lower = low_half(t)
    back = (iota((t, t), 0) + iota((t, t), 1) == t - 1).astype(f32).astype(bf16)
    lane = iota((1, 128), 1)
    line[...] = jnp.zeros_like(line)
    slots = [(i, j) for i, count in enumerate(counts) for j in range(count)]

    def operands(k):
        h = 2 * pairs[k // 2] + k % 2
        at = slice(h // 2 * 128, h // 2 * 128 + 128)
        qt = jnp.where(lower == (k % 2 == 0), q[:, at].astype(f32), 0.0).T
        doh = jnp.where(lower == (k % 2 == 1), turn(do[:, at].astype(f32)), 0.0)
        out = []
        for i in range(phases):
            factor = scale[:, 8 * i + h : 8 * i + h + 1]
            scaled = doh * factor
            shift = scale[:, 64 + h : 65 + h] * factor
            out.append((scaled.astype(bf16), shift, jnp.concatenate([qt, scaled.T], axis=1).astype(bf16)))
        return out

    def start(k, s, ops):
        i, j = slots[s]
        return nt(ops[i][0], kv[i][k // 2][k % 2, j * t : (j + 1) * t])

    def finish(k, s, ops, d_prob, acc):
        i, j = slots[s]
        rows = slice(j * t, (j + 1) * t)
        probs = p[i][k // 2][k % 2, :, rows]
        d_score = (probs.astype(f32) * (d_prob - ops[i][1])).astype(bf16)
        ds[k % 2, :, s * t : (s + 1) * t] = d_score
        more = nn(d_score, jnp.concatenate([kv[i][k // 2][k % 2, rows], e[i][rows]], axis=1))
        both = nn(ops[i][2], jnp.concatenate([d_score, probs], axis=0)).astype(bf16)
        mine, other = (both[:64], both[64:]) if k % 2 == 0 else (both[64:], both[:64])
        dk[k // 2][k % 2 * 64 : k % 2 * 64 + 64, s * t : (s + 1) * t] = mine
        dv[k // 2][k % 2 * 64 : k % 2 * 64 + 64, s * t : (s + 1) * t] = other
        return more if acc is None else acc + more

    def bias(k, acc):
        parts = []
        for r in (-1, 0, 1):
            there = me + r
            inside = (there >= 0) & (there < n)
            slot = jnp.where(inside, me ^ there, 0)
            block = ds[k % 2, :, pl.ds(pl.multiple_of(slot * t, t), t)]
            parts.append(nn(back, block) * inside.astype(f32))
        parts.append(jnp.zeros((t, t), f32))
        band = pltpu.roll(jnp.concatenate(parts, axis=1), 0, 1, stride=1, stride_axis=0)
        line[k : k + 1, : 4 * t] = jnp.sum(band, axis=0, keepdims=True)
        ends = jnp.sum(acc[:, 128:], axis=0, keepdims=True)
        line[k : k + 1, 4 * t :] = jnp.where((lane == LEFT) | (lane == RIGHT), ends, 0.0)

    tasks = [(k, s) for k in range(2 * size) for s in range(len(slots))]
    ops = [operands(0)]
    d_prob = start(0, 0, ops[0])
    accs = [None] * (2 * size)
    for index, (k, s) in enumerate(tasks):
        if s == 0 and k + 1 < 2 * size:
            ops.append(operands(k + 1))
        later = None
        if index + 1 < len(tasks):
            k2, s2 = tasks[index + 1]
            later = start(k2, s2, ops[k2])
        accs[k] = finish(k, s, ops[k], d_prob, accs[k])
        d_prob = later
        if s == 3 and k > 0:
            bias(k - 1, accs[k - 1])
    bias(2 * size - 1, accs[2 * size - 1])
    for g in range(size):
        dq[:, g * 128 : g * 128 + 128] = jnp.where(lower, accs[2 * g][:, :128], accs[2 * g + 1][:, :128]).astype(bf16)


def attend_back(n, pairs, ids, q, do, scale, parts):
    t = q.shape[0]
    widths = [v["e"].shape[0] for v in parts]
    s = sum(widths)
    size = len(pairs)
    out = call(
        partial(attend_back_kernel, n, pairs, [w // t for w in widths]), "attend_back", 4 * size,
        [shape(128, s)] * (2 * size) + [shape(t, 128 * size), shape(8, 4 * t + 128, dtype=f32)],
        (ids,), (q, do, scale, *[v["p"][g] for v in parts for g in pairs],
                 *[v["kv"][g] for v in parts for g in pairs], *[v["e"] for v in parts]),
        scratch=[pltpu.VMEM((2, t, s), bf16)], much=n > 8,
    )
    return dict(dk=out[:size], dv=out[size : 2 * size], dq=out[-2], line=out[-1], pairs=size)


def gather_back_kernel(n, buckets, counts, pairs, ids, gain, gn, gwo, wq, wk, wv, wt, *refs):
    phases = len(counts)
    n1, refs = refs[:phases], refs[phases:]
    total_pairs = sum(pairs)
    dkv, refs = refs[: 2 * total_pairs], refs[2 * total_pairs :]
    dq, lines = refs[: len(pairs)], refs[len(pairs) : 2 * len(pairs)]
    even, odd, dn1q, keep, send, grads, sums, diagonal = refs[2 * len(pairs) :]
    d, w = wq.shape
    t = dn1q.shape[0]
    weights = jnp.concatenate([wk[...], wv[...]], axis=1)
    total = jnp.zeros((2 * w, d), f32)
    slot = 0
    for i, count in enumerate(counts):
        begin = sum(counts[:i]) * t
        both = jnp.concatenate([ref[:, begin : begin + count * t] for ref in dkv], axis=0)
        total = total + nn(both, n1[i][...])
        back = nn(weights, both).astype(bf16)
        for _ in range(count):
            ref = odd if slot % 2 else even
            ref[slot // 2] = back[:, slot * t - begin : slot * t - begin + t]
            slot += 1
    dq_all = jnp.concatenate([ref[...] for ref in dq], axis=1)
    from_q = tn(dq_all, n1[0][:t])
    dn1q[...] = nt(dq_all, wq[...])
    grads[:w] = from_q.astype(bf16)
    grads[w : 3 * w] = total.astype(bf16)
    grads[3 * w :] = gwo[...]
    gains = jnp.sum(from_q * wt[:w].astype(f32), axis=0, keepdims=True)
    gains = gains + jnp.sum(total * wt[w:].astype(f32), axis=0, keepdims=True)
    sums[...] = jnp.zeros_like(sums)
    sums[0:1] = gains / gain[...].astype(f32)
    sums[1:2] = gn[...]
    diagonal[...] = jnp.zeros_like(diagonal)
    begin = 0
    for ref, count in zip(lines, pairs, strict=True):
        diagonal[begin : begin + 2 * count] = ref[: 2 * count]
        begin += 2 * count
    width = diagonal.shape[1]
    u = iota((width, 128), 0)
    bucket = bucket_of(u - (2 * t - 1), buckets)
    bucket = jnp.where(u == 4 * t + LEFT, buckets // 2 - 1, jnp.where(u == 4 * t + RIGHT, buckets - 1, bucket))
    pick = (bucket == iota((width, 128), 1)).astype(f32)
    sums[8:16, :128] = lax.dot_general(diagonal[...], pick, (((1,), (0,)), ((), ())),
                                       precision=lax.Precision.HIGHEST, preferred_element_type=f32)
    small = sums[...].astype(bf16)
    rows = 2 * w
    keep[:rows] = grads[pl.ds(pl.multiple_of(ids[1] * rows, 16), rows)]
    send[:rows] = grads[pl.ds(pl.multiple_of((1 - ids[1]) * rows, 16), rows)]
    keep[rows:] = small
    send[rows:] = small


def gather_back(n, buckets, ids, gain, gn, gwo, wq, wk, wv, wt, parts, backs):
    d, w = wq.shape
    t = backs[0]["dq"].shape[0]
    pairs = [v["pairs"] for v in backs]
    counts = [v["e"].shape[0] // t for v in parts]
    pieces = [ref for v in backs for ref in v["dk"]] + [ref for v in backs for ref in v["dv"]]
    half = 2 * w + SMALL
    return call(
        partial(gather_back_kernel, n, buckets, counts, pairs), "gather_back", 6,
        [shape(n // 2, d, t), shape(n // 2, d, t), shape(t, d, dtype=f32), shape(half, d), shape(half, d)],
        (ids,), (gain, gn, gwo, wq, wk, wv, wt, *[v["n1"] for v in parts], *pieces, *[v["dq"] for v in backs],
                 *[v["line"] for v in backs]),
        scratch=[pltpu.VMEM((4 * w, d), bf16), pltpu.VMEM((SMALL, d), f32), pltpu.VMEM((8, 4 * t + 128), f32)], much=n > 8,
    )


def rest_back_kernel(n, buckets, pairs, counts, sizes, ids, *refs):
    first, second, outs, inner = (refs[a:b] for a, b in zip(sizes[:-1], sizes[1:], strict=True))
    size = len(pairs)
    dkv, (dq, line), ds = inner[: 2 * size], inner[2 * size : 2 * size + 2], inner[2 * size + 2]
    attend_back_kernel(n, pairs, counts, ids, *first, *dkv, dq, line, ds)
    head, (dk0, dv0, dq0, line0) = second[: 7 + len(counts)], second[7 + len(counts) :]
    gather_back_kernel(n, buckets, counts, [1, size], ids, *head, dk0, *dkv[:size], dv0, *dkv[size:], dq0, dq, line0, line,
                       *outs, *inner[2 * size + 3 :])


def rest_back(n, buckets, pairs, ids, q, do, scale, gain, gn, gwo, wq, wk, wv, wt, parts, back):
    d, w = wq.shape
    t = q.shape[0]
    widths = [v["e"].shape[0] for v in parts]
    s, size, half = sum(widths), len(pairs), 2 * w + SMALL
    first = (q, do, scale, *[v["p"][g] for v in parts for g in pairs], *[v["kv"][g] for v in parts for g in pairs],
             *[v["e"] for v in parts])
    second = (gain, gn, gwo, wq, wk, wv, wt, *[v["n1"] for v in parts], back["dk"][0], back["dv"][0], back["dq"], back["line"])
    cuts = [0, len(first), len(first) + len(second), len(first) + len(second) + 5]
    inner = [pltpu.VMEM((128, s), bf16)] * (2 * size) + [pltpu.VMEM((t, 128 * size), bf16), pltpu.VMEM((8, 4 * t + 128), f32),
             pltpu.VMEM((2, t, s), bf16), pltpu.VMEM((4 * w, d), bf16), pltpu.VMEM((SMALL, d), f32),
             pltpu.VMEM((8, 4 * t + 128), f32)]
    return call(
        partial(rest_back_kernel, n, buckets, pairs, [v // t for v in widths], [*cuts, cuts[-1] + len(inner)]), "rest_back", 10,
        [shape(n // 2, d, t), shape(n // 2, d, t), shape(t, d, dtype=f32), shape(half, d), shape(half, d)],
        (ids,), (*first, *second), scratch=inner,
    )


def add_all(refs, at):
    if len(refs) == 2:
        return refs[0][at] + refs[1][at]
    return sum(ref[at].astype(f32) for ref in refs).astype(bf16)


def split_kernel(which, count, extra, ids, *refs):
    inputs, outs = refs[:-count], refs[-count:]
    rows = (inputs[0].shape[0] - extra) // count
    own = ids[which]
    for j in range(count):
        at = pl.ds(pl.multiple_of((own ^ j) * rows, 16), rows)
        total = add_all(inputs, at)
        outs[j][:rows] = total
    if extra:
        at = pl.ds(rows * count, extra)
        total = add_all(inputs, at)
        for j in range(count):
            outs[j][rows:] = total


def add_and_split(which, count, extra, ids, *arrays):
    rows = (arrays[0].shape[0] - extra) // count + extra
    out = shape(rows, arrays[0].shape[1])
    return call(partial(split_kernel, which, count, extra), "add_parts", 1, [out] * count, (ids,), arrays)


def by_chip_kernel(ids, keep, recv, *outs):
    rows = keep.shape[0] // 4
    for half, own in ((0, ids[2] % 2), (1, ids[2] // 2)):
        for j in range(2):
            at = pl.ds(pl.multiple_of((2 * half + (own ^ j)) * rows, 16), rows)
            outs[2 * half + j][...] = keep[at] + recv[at]


def by_next_chip_kernel(ids, keep_x, recv_x, keep_y, recv_y, *outs):
    rows = keep_x.shape[0] // 2
    for half, own, a, b in ((0, ids[2] // 2, keep_x, recv_x), (1, ids[2] % 2, keep_y, recv_y)):
        for j in range(2):
            at = pl.ds(pl.multiple_of((own ^ j) * rows, 16), rows)
            outs[2 * half + j][...] = a[at] + b[at]


def by_row_kernel(ids, keep_x, recv_x, keep_y, recv_y, mine, other):
    first = keep_x[...].astype(f32) + recv_x[...].astype(f32)
    second = keep_y[...].astype(f32) + recv_y[...].astype(f32)
    even = ids[3] % 2 == 0
    mine[...] = jnp.where(even, first, second).astype(bf16)
    other[...] = jnp.where(even, second, first).astype(bf16)


def pick_kernel(ids, mine, other, first, second):
    even = ids[3] % 2 == 0
    a, b = mine[...].astype(f32), other[...].astype(f32)
    first[...] = jnp.where(even, a, b).astype(bf16)
    second[...] = jnp.where(even, b, a).astype(bf16)


def stack_kernel(ids, *refs):
    *parts, out = refs
    rows = parts[0].shape[0]
    for i, ref in enumerate(parts):
        out[i * rows : (i + 1) * rows] = ref[...]


def join_kernel(ids, a, b, c, d, first, second):
    rows = a.shape[0]
    first[:rows], first[rows:] = a[...], b[...]
    second[:rows], second[rows:] = c[...], d[...]


def swap(array, axis, j):
    size = lax.axis_size(axis)
    return lax.ppermute(array, axis, [(i, i ^ j) for i in range(size)])


def order(first, *values):
    first, values = lax.optimization_barrier((first, values))
    return values if len(values) > 1 else values[0]


def sum_all(ids, keep, recv, extra):
    both = add_and_split(0, 1, extra, ids * 0, keep, recv)[0].astype(f32)
    size = both.shape[0] - extra
    placed = jnp.zeros((2 * size, both.shape[1]), f32)
    placed = lax.dynamic_update_slice_in_dim(placed, both[:size], ids[1] * size, 0)
    full, tail = lax.psum((placed, both[size:] * 0.5), ("rows", "seq"))
    mine = lax.dynamic_slice_in_dim(full, ids[1] * size, size, 0)
    other = lax.dynamic_slice_in_dim(full, (1 - ids[1]) * size, size, 0)
    return [mine.astype(bf16)], [other.astype(bf16)], tail.astype(bf16)


def to_chips(parts):
    return [parts[0]] + [swap(parts[j], "seq", 2 * j) for j in range(1, len(parts))]


def place_halves(ids, mine, other, full):
    size = full.shape[0] // 2
    if len(mine) == 1:
        full[pl.ds(pl.multiple_of(ids[1] * size, 16), size)] = mine[0][...]
        full[pl.ds(pl.multiple_of((1 - ids[1]) * size, 16), size)] = other[0][...]
        return
    piece = size // len(mine)
    for c, refs in ((ids[1], mine), (1 - ids[1], other)):
        for a, ref in enumerate(refs):
            at = c * size + (ids[2] ^ a) * piece
            for b in range(2):
                where = at + ((ids[3] % 2) ^ b) * (piece // 2)
                full[pl.ds(pl.multiple_of(where, 16), piece // 2)] = ref[b * (piece // 2) : (b + 1) * (piece // 2)]


def send_out(copies, source, target, sem):
    copies.append(pltpu.make_async_copy(source, target, sem))
    copies[-1].start()


def write_ffn(far, ids, parts, gate, up, down, full, sems):
    d = gate.shape[0]
    x, y = ids[2] % 2, ids[2] // 2
    rows = 3 * PIECE
    copies = []
    for c, *pair in parts:
        for half, first, second in ((0, x, y), (1, y, x)):
            for b in range(2):
                k = len(copies) // 4
                piece = 8 * c + 4 * half + 2 * (first ^ far) + (second ^ b)
                full[k] = pair[half][b * rows : (b + 1) * rows].astype(f32)
                at = pl.multiple_of(piece * PIECE, PIECE)
                send_out(copies, full.at[k, :PIECE], gate.at[pl.ds(at, PIECE)], sems.at[4 * k])
                send_out(copies, full.at[k, PIECE : 2 * PIECE], up.at[pl.ds(at, PIECE)], sems.at[4 * k + 1])
                send_out(copies, full.at[k, 2 * PIECE :, :d], down.at[pl.ds(at, PIECE)], sems.at[4 * k + 2])
                send_out(copies, full.at[k, 2 * PIECE :, d:], down.at[pl.ds(d + at, PIECE)], sems.at[4 * k + 3])
    return copies


def unpack_near_kernel(ids, *refs):
    for copy in write_ffn(0, ids, ((ids[1], *refs[:2]), (1 - ids[1], *refs[2:4])), *refs[4:]):
        copy.wait()


def unpack_half_kernel(other, filled, chips, ids, *refs):
    (x, y, *stacks), refs = refs[:4], refs[4 + filled :]
    gate, up, down, gq, gk, gv, go, full, sems, both, wide, tall, sem2 = refs
    core = ids[1] ^ other
    copies = write_ffn(1, ids, ((core, x, y),), gate, up, down, full, sems)
    rows = stacks[0].shape[0] // chips
    for k, stack in enumerate(stacks):
        for a in range(chips):
            where = ((ids[2] ^ a) * 2 + ((ids[3] % 2) ^ k)) * rows
            both[pl.ds(pl.multiple_of(where, 16), rows)] = stack[a * rows : (a + 1) * rows]
    w = wide.shape[2]

    def finish(matrices):
        moves = []
        for i, (ref, turned) in enumerate(matrices):
            value = both[i * w : (i + 1) * w].astype(f32)
            source = wide.at[i] if turned else tall
            source[...] = value.T if turned else value
            send_out(moves, source, ref, sem2.at[i])
        for copy in moves:
            copy.wait()

    @pl.when(core == 0)
    def _():
        finish(((gq, True), (gk, True)))

    @pl.when(core == 1)
    def _():
        finish(((gv, True), (go, False)))

    for copy in copies:
        copy.wait()


def unpack(kernel, ids, vmem_args, filled, out_shape, scratch):
    vmem, hbm = pl.BlockSpec(memory_space=pltpu.VMEM), pl.BlockSpec(memory_space=pl.ANY)
    return pl.pallas_call(
        kernel,
        in_specs=[pl.BlockSpec(memory_space=pltpu.SMEM)] + [vmem] * len(vmem_args) + [hbm] * len(filled),
        out_specs=[hbm] * len(out_shape),
        out_shape=out_shape,
        scratch_shapes=scratch,
        input_output_aliases={1 + len(vmem_args) + i: i for i in range(len(filled))},
        compiler_params=pltpu.CompilerParams(vmem_limit_bytes=VMEM),
        cost_estimate=pl.CostEstimate(flops=1000, bytes_accessed=1000, transcendentals=0),
        name="unpack",
    )(ids, *vmem_args, *filled)


def unpack_ffn_halves(ids, mine, other, d, ff):
    full = jnp.where(ids[1] == 0, jnp.concatenate([mine, other]), jnp.concatenate([other, mine])).astype(f32)
    full = full.reshape(d // PIECE, 3, PIECE, ff)
    low = full[:, 2].reshape(d, ff)
    return full[:, 0].reshape(d, ff), full[:, 1].reshape(d, ff), jnp.concatenate([low[:, :d], low[:, d:]])


def unpack_attention_kernel(pieces, ids, *refs):
    gq, gk, gv, go, full = refs[2 * pieces :]
    place_halves(ids, refs[:pieces], refs[pieces : 2 * pieces], full)
    w = gq.shape[1]
    for k, ref in enumerate((gq, gk, gv)):
        ref[...] = full[k * w : (k + 1) * w].astype(f32).T
    go[...] = full[3 * w :].astype(f32)


def unpack_small_kernel(ids, tail, g1, g2, gb):
    small = tail[...].astype(f32)
    g1[...] = small[0:1]
    g2[...] = small[1:2]
    gb[...] = small[8 : 8 + gb.shape[0], : gb.shape[1]]


def input_grad_kernel(ids, *refs):
    *parts, dn1q, x, dh, gain, out = refs
    total = parts[0][...].astype(f32)
    for ref in parts[1:]:
        total = total + ref[...].astype(f32)
    dn1 = total.T + dn1q[...]
    value = x[...].astype(f32)
    s1 = lax.rsqrt(jnp.mean(value * value, axis=-1, keepdims=True) + EPS)
    hat = value * s1
    scaled = dn1 * gain[...].astype(f32)
    out[...] = dh[...] + s1 * (scaled - hat * jnp.mean(hat * scaled, axis=-1, keepdims=True))


def slots_kernel(count, ids, mine, other, *outs):
    for j in range(count):
        outs[j][...] = (mine[j].astype(f32) + other[j].astype(f32)).astype(bf16)


def shards(
    tokens, norm_attn, query_weight, key_weight, value_weight, out_weight, bucket_bias_table, norm_ffn,
    gate_weight, expansion_matrix, down_weight, lengths, cotangent,
):
    _, t, d = tokens.shape
    n = lax.axis_size("seq")
    buckets, heads = bucket_bias_table.shape
    width = query_weight.shape[1]
    ff = gate_weight.shape[1]
    seq = lax.axis_index("seq")
    ids = jnp.stack([seq, seq % 2, seq // 2, lax.axis_index("rows")]).astype(i32)
    x = tokens.reshape(t, d)
    cot = cotangent.reshape(t, d)
    lens = lengths.reshape(-1)
    gain1 = norm_attn.reshape(1, d)
    gain2 = norm_ffn.reshape(1, d)

    blocks = [[x], [swap(x, "seq", 1)]] + [None] * (n - 2)
    for j in range(2, n, 2):
        if n != 8 or j != 6:
            blocks[j] = [swap(x, "seq", j)]
    q, ext, bands, wt, line, x, wq, wk, wv = prepare(
        ids, lens, x, gain1, bucket_bias_table.T, query_weight, key_weight, value_weight
    )
    blocks[0] = [x]
    cuts = [0, 2, 6, *range(8, n, 8), n]

    def phase(a, b):
        return attend(n, a, ids, lens, blocks[a:b], gain1, wk, wv, q, ext, bands, line)

    parts = []
    for a, b in zip(cuts[:-1], cuts[1:], strict=True):
        for j in range(a, b, 2):
            if j:
                blocks[j] = [order(parts[-1]["acc"], v) for v in blocks[j]]
                blocks[j + 1] = [swap(v, "seq", 1) for v in blocks[j]]
        if n == 8 and a == 2:
            blocks[6] = [swap(blocks[4][0][: t // 2], "seq", 2), swap(blocks[2][0][t // 2 :], "seq", 4)]
        parts.append(phase(a, b))
    output, dh, do, scale, gwo, keep, send, gn = feed_forward(
        ids, lens, gain2, x, out_weight, gate_weight, expansion_matrix, down_weight, cot, parts
    )
    half = n // 2
    pairs = width // 128
    whole = n != 8 or lax.axis_size("rows") != 4
    zero, near = ids * 0, ids[3:4] % 2

    def unpack_attention(mine, other):
        return call(
            partial(unpack_attention_kernel, len(mine)), "unpack_attention", 3,
            [shape(d, width, dtype=f32)] * 3 + [shape(width, d, dtype=f32)],
            (ids,), (*mine, *other), scratch=[pltpu.VMEM((4 * width, d), bf16)],
        )

    def unpack_small(tail):
        return call(unpack_small_kernel, "unpack_small", 1,
                    [shape(1, d, dtype=f32)] * 2 + [shape(heads, buckets, dtype=f32)], (ids,), (tail,))

    def input_grad(slots):
        return call(input_grad_kernel, "input_grad", 2, shape(t, d, dtype=f32), (ids,), (*slots, dn1q, x, dh, gain1))

    def add_slots(recv):
        return call(partial(slots_kernel, half), "add_slots", 1, [shape(d, t)] * half, (ids,), (even, recv))

    f_core = swap(send, "seq", 1)
    back = attend_back(n, [0], ids, q, do, scale, parts)
    f_keep = keep
    if whole:
        backs = [back, attend_back(n, list(range(1, pairs)), ids, q, do, scale, parts)]
        even, odd, dn1q, keep, send = gather_back(n, buckets, ids, gain1, gn, gwo, wq, wk, wv, wt, parts, backs)
        a_core, d_core = swap(send, "seq", 1), swap(odd, "seq", 1)
        mine, other, _ = sum_all(ids, f_keep, f_core, 0)
        gate, up, down = unpack_ffn_halves(ids, mine[0], other[0], d, ff)
        grad_tokens = input_grad(to_chips(add_slots(d_core)))
        mine, other, tail = sum_all(ids, keep, a_core, SMALL)
        gq, gk, gv, go = unpack_attention(mine, other)
        g1, g2, gb = unpack_small(tail)
    else:
        part = lambda rows: shape(f_keep.shape[0] // rows, ff)
        f_core = order(back["dq"], f_core)
        f_x, f_x2, f_y, f_y2 = call(by_chip_kernel, "add_parts", 1, [part(4)] * 4, (ids,), (keep, f_core))
        do = order(f_x, do)
        f_x2, f_y2 = swap(f_x2, "seq", 2), swap(f_y2, "seq", 4)
        even, odd, dn1q, keep, send = rest_back(
            n, buckets, list(range(1, pairs)), ids, q, do, scale, gain1, gn, gwo, wq, wk, wv, wt, parts, back
        )
        send, odd = order((f_x2, f_y2), send, odd)
        live = dict(a=swap(send, "seq", 1), d=swap(odd, "seq", 1))
        f_x, f_x2, f_y, f_y2 = call(
            by_next_chip_kernel, "add_parts", 1, [part(8)] * 4, (ids,), (f_x, f_x2, f_y, f_y2)
        )
        live["f"] = [swap(f_x2, "seq", 4), swap(f_y2, "seq", 2)]
        size = (keep.shape[0] - SMALL) // 8
        ffn_out = [shape(d, ff, dtype=f32), shape(d, ff, dtype=f32), shape(ff, d, dtype=f32)]
        ffn_scratch = [pltpu.VMEM((8, 3 * PIECE, ff), f32), pltpu.SemaphoreType.DMA((32,))]
        kept = dict(f=(f_x, f_y))

        def f_rows():
            (f_x, f_y), (f_x2, f_y2) = kept["f"], live["f"]
            mine, other = call(by_row_kernel, "add_parts", 1, [part(8)] * 2, (ids,), (f_x, f_x2, f_y, f_y2))
            kept["f"], live["f"] = mine, swap(other, "rows", 1)
            return mine

        def f_add(j):
            mine = add_and_split(0, 1, 0, zero, kept["f"], live["f"])[0]
            kept["f"], live["f"] = mine, swap(mine, "rows", j)
            return mine

        def f_pick():
            x, y = call(pick_kernel, "pick", 1, [part(8)] * 2, (ids,), (kept["f"], live["f"]))
            kept["f"], live["f"] = (x, y), [swap(x, "seq", 4), swap(y, "seq", 2)]
            return x

        def f_join():
            (x, y), (x2, y2) = kept["f"], live["f"]
            x, y = call(join_kernel, "join", 1, [part(4)] * 2, (ids,), (x, x2, y, y2))
            kept["f"], live["f"] = (x, y), [swap(x, "seq", 2), swap(y, "seq", 4)]
            live["near"] = [swap(v, "seq", 1) for v in (x, y)]
            return x

        def f_near():
            kept["near"] = unpack(unpack_near_kernel, ids, (*kept["f"], *live["near"]), (), ffn_out, ffn_scratch)
            return kept["near"][0]

        def f_swap():
            live["far"] = [swap(v, "seq", 1) for v in live["f"]]
            return None

        def a_chips():
            kept["a"] = add_and_split(2, half, SMALL, ids, keep, live["a"])
            live["a"] = to_chips(kept["a"])
            return kept["a"][0]

        def a_rows():
            kept["a"], other = add_and_split(0, 2, SMALL, near, *live["a"])
            live["a"] = swap(other, "rows", 1)
            return kept["a"]

        def a_add(j):
            kept["a"] = add_and_split(0, 1, SMALL, zero, kept["a"], live["a"])[0]
            live["a"] = swap(kept["a"], "rows", 2) if j == 2 else to_chips([kept["a"][:size]] * half)
            return kept["a"]

        def a_stack():
            kept["stack"] = call(stack_kernel, "stack", 1, shape(half * size, d), (ids,), live["a"])
            live["a"] = swap(kept["stack"], "rows", 1)
            live["anear"] = swap(kept["stack"], "seq", 1)
            return kept["stack"]

        def a_swap():
            live["afar"] = swap(live["a"], "seq", 1)
            return None

        def unpack_half(other, x, y, first, second, filled):
            return unpack(
                partial(unpack_half_kernel, other, len(filled), half), ids, (x, y, first, second), filled,
                ffn_out + [shape(d, width, dtype=f32)] * 3 + [shape(width, d, dtype=f32)],
                [*ffn_scratch, pltpu.VMEM((2 * width, d), bf16), pltpu.VMEM((2, d, width), f32),
                 pltpu.VMEM((width, d), f32), pltpu.SemaphoreType.DMA((2,))],
            )

        def own():
            kept["near"] = unpack_half(0, *live["f"], kept["stack"], live["a"], kept["near"])
            return kept["near"][0]

        def last():
            kept["out"] = unpack_half(1, *live["far"], live["anear"], live["afar"], kept["near"])
            return kept["out"][0]

        def d_slots():
            kept["d"] = add_slots(live["d"])
            live["d"] = to_chips(kept["d"])
            return kept["d"][0]

        def d_out():
            kept["tokens"] = input_grad(live["d"])
            return kept["tokens"]

        def small():
            kept["small"] = unpack_small(kept["a"][size:])
            return kept["small"][0]

        steps = dict(
            f_rows=(f_rows, "f"), f_z0=(partial(f_add, 2), "f"), f_z1=(partial(f_add, 1), "f"), f_pick=(f_pick, "f"),
            f_join=(f_join, "f"), f_near=(f_near, "near"), f_swap=(f_swap, "f"), own=(own, "f"), last=(last, "far"),
            a_chips=(a_chips, "a"), a_rows=(a_rows, "a"), a_z0=(partial(a_add, 2), "a"), a_z1=(partial(a_add, 1), "a"),
            a_stack=(a_stack, "a"), a_swap=(a_swap, "a"),
            d_slots=(d_slots, "d"), d_out=(d_out, "d"), small=(small, None),
        )
        token = f_x
        for name in STEPS:
            if ":" in name:
                stream, j = name.split(":")
                live[stream][int(j)] = token = order(token, live[stream][int(j)])
                continue
            step, stream = steps[name]
            if stream is not None:
                live[stream] = order(token, live[stream])
            elif name == "small":
                kept["a"] = order(token, kept["a"])
            done = step()
            token = live[stream] if done is None else done
        gate, up, down, gq, gk, gv, go = kept["out"]
        g1, g2, gb = kept["small"]
        grad_tokens = kept["tokens"]
    return (
        output.reshape(tokens.shape), grad_tokens.reshape(tokens.shape), g1.reshape(d), gq, gk, gv, go, gb.T,
        g2.reshape(d), gate, up, down,
    )


def solution(mesh):
    split = P("rows", "seq", None)
    in_specs = (split,) + (P(),) * 10 + (P("rows", None), split)
    out_specs = (split, split) + (P(),) * 10
    return jax.shard_map(shards, mesh=mesh, in_specs=in_specs, out_specs=out_specs, check_vma=False)
```

```python
from functools import partial

import jax
import jax.numpy as jnp
from jax import lax
from jax.experimental import pallas as pl
from jax.experimental.pallas import tpu as pltpu
from jax.sharding import PartitionSpec as P

EPS = 1e-6
BIG = -(2.0**30)
LEFT, RIGHT, ONES = 17, 18, 19
PIECE = 32
FFN_CHUNKS = 1
STEPS = (
    "a_chips", "f_rows", "f_z0", "a_rows", "d_slots", "f_z1", "f_pick", "a_z0", "d:3", "d_out", "a_z1",
    "f_join", "a_stack", "small", "f_near", "f_swap", "a_swap", "own", "last",
)
SMALL = 16
VMEM = 24 * 1024 * 1024
MUCH = 56 * 1024 * 1024

f32, bf16, i32 = jnp.float32, jnp.bfloat16, jnp.int32


def thresholds(buckets, max_distance):
    half = buckets // 2
    exact = half // 2
    steps = half - exact
    out = list(range(1, exact))
    for j in range(steps):
        target = exact ** (steps - j) * max_distance**j
        m = exact
        while m**steps < target:
            m += 1
        out.append(m)
    return out


def bucket_of(offset, buckets):
    distance = jnp.abs(offset)
    bucket = (offset > 0).astype(i32) * (buckets // 2)
    for t in thresholds(buckets, 128):
        bucket = bucket + (distance >= t).astype(i32)
    return bucket


def nn(a, b):
    return lax.dot_general(a, b, (((1,), (0,)), ((), ())), preferred_element_type=f32)


def nt(a, b):
    return lax.dot_general(a, b, (((1,), (1,)), ((), ())), preferred_element_type=f32)


def tn(a, b):
    return lax.dot_general(a, b, (((0,), (0,)), ((), ())), preferred_element_type=f32)


def iota(shape, dim):
    return lax.broadcasted_iota(i32, shape, dim)


def rms(values, gain):
    scale = lax.rsqrt(jnp.mean(values * values, axis=-1, keepdims=True) + EPS)
    return values * scale * gain


def call(kernel, name, us, out_shape, smem_args, args, scratch=(), much=False, anywhere=0):
    smem = pl.BlockSpec(memory_space=pltpu.SMEM)
    vmem = pl.BlockSpec(memory_space=pltpu.VMEM)
    return pl.pallas_call(
        kernel,
        in_specs=[smem] * len(smem_args) + [vmem] * (len(args) - anywhere) + [pl.BlockSpec(memory_space=pltpu.HBM)] * anywhere,
        out_specs=jax.tree.map(lambda _: vmem, out_shape),
        out_shape=out_shape,
        scratch_shapes=list(scratch),
        compiler_params=pltpu.CompilerParams(vmem_limit_bytes=MUCH if much else VMEM),
        cost_estimate=pl.CostEstimate(flops=int(us * 1e6), bytes_accessed=int(us * 2e3), transcendentals=0),
        name=name,
    )(*smem_args, *args)


def shape(*dims, dtype=bf16):
    return jax.ShapeDtypeStruct(dims, dtype)


def low_half(t):
    return iota((t, 128), 1) < 64


def turn(pair):
    return pltpu.roll(pair, 64, 1)


def prepare_kernel(ids, lens, gain, table, x, w3, q, ext, bands, wt, line, x_here, wq, wk, wv):
    w = wq.shape[1]
    for k, ref in enumerate((wq, wk, wv)):
        ref[...] = w3[:, k * w : (k + 1) * w]
        wt[k * w : (k + 1) * w] = ref[...].astype(f32).T.astype(bf16)
    x_here[...] = x[...]
    t = x.shape[0]
    heads, buckets = table.shape
    low, high = segment_bounds(lens)
    lanes = iota((t, 128), 1)
    pos = iota((t, 128), 0) + ids[0] * t
    other = jnp.where((pos >= low) & (pos < high), 0.0, BIG)
    ext[...] = jnp.where(lanes < LEFT, other, 0.0)
    u = iota((buckets, 4 * t), 1)
    bucket = bucket_of(jnp.where(u < 3 * t, u - t, u - 5 * t), buckets)
    pick = (bucket == iota((buckets, 4 * t), 0)).astype(f32).astype(bf16)
    line[...] = jnp.zeros_like(line)
    line[:heads] = nn(table[...], pick)
    for h in range(heads):
        band = pltpu.roll(jnp.broadcast_to(line[h : h + 1], (t, 4 * t)), 0, 1, stride=1, stride_axis=0)
        for r in range(3):
            bands[h, r] = band[:, r * t : (r + 1) * t].astype(bf16)
        bands[h, 3] = jnp.zeros((t, t), bf16)
    n1 = rms(x[...].astype(f32), gain[...].astype(f32)).astype(bf16)
    q[...] = nn(n1, wq[...]).astype(bf16)


def prepare(ids, lens, x, gain, table, wq, wk, wv):
    t, d = x.shape
    heads, w = table.shape[0], wq.shape[1]
    return call(
        prepare_kernel, "prepare", 4,
        [shape(t, w), shape(t, 128, dtype=f32), shape(heads, 4, t, t), shape(3 * w, d), shape(8, 4 * t, dtype=f32),
         shape(t, d), shape(d, w), shape(d, w), shape(d, w)],
        (ids, lens), (gain, table, x, jnp.concatenate([wq, wk, wv], axis=1)),
    )


def segment_bounds(lens):
    lane = iota((1, 128), 1)
    low = jnp.where(lane == 0, -1, 2**30)
    high = jnp.full((1, 128), -1, i32)
    total = 0
    for k in range(lens.shape[0]):
        total = total + lens[k]
        high = jnp.where(lane == k, total, high)
        low = jnp.where(lane == k + 1, total, low)
    return low, jnp.where(lane == lens.shape[0], 2**30, high)


def attend_kernel(n, first, count, pieces, ids, lens, *refs):
    x, refs = refs[:pieces], refs[pieces:]
    gain, wk, wv, q, ext, bands, line, n1, e, acc, stat = refs[:11]
    pairs = q.shape[1] // 128
    kv, p = refs[11 : 11 + pairs], refs[11 + pairs : -1]
    s = refs[-1]
    me = ids[0]
    t = q.shape[0]
    low, high = segment_bounds(lens)
    row = iota((t, 128), 0)
    lanes = iota((t, 128), 1)
    begin = 0
    for ref in x:
        n1[begin : begin + ref.shape[0]] = rms(ref[...].astype(f32), gain[...].astype(f32)).astype(bf16)
        begin += ref.shape[0]
    for i in range(count):
        at = slice(i * t, (i + 1) * t)
        block = me ^ (first + i)
        pos = row + block * t
        away = block - me
        flag = jnp.where(away <= -2, LEFT, jnp.where(away >= 2, RIGHT, ONES))
        here = ((pos >= low) & (pos < high)) | (lanes == flag) | (lanes == ONES)
        e[at] = here.astype(f32).astype(bf16)
    upper = iota((t, 128), 1) >= 64
    near = [i for i in range(count) if (first + i) & (first + i + 1) == 0]

    def project(g, i):
        rows, at = slice(i * t, (i + 1) * t), slice(g * 128, g * 128 + 128)
        both = nn(n1[rows], jnp.concatenate([wk[:, at], wv[:, at]], axis=1))
        keys, values = both[:, :128], turn(both[:, 128:])
        kv[g][0, rows] = jnp.where(upper, values, keys).astype(bf16)
        kv[g][1, rows] = jnp.where(upper, keys, values).astype(bf16)

    def query(h):
        lane_ext = jnp.where(lanes == LEFT, line[h : h + 1, 0:1],
                             jnp.where(lanes == RIGHT, line[h : h + 1, 3 * t - 1 : 3 * t], ext[...]))
        q2 = q[:, h // 2 * 128 : h // 2 * 128 + 128].astype(f32)
        return jnp.concatenate([jnp.where(upper == (h % 2 == 1), q2, 0.0), lane_ext], axis=1).astype(bf16)

    def keys_of(h, i):
        rows = slice(i * t, (i + 1) * t)
        return jnp.concatenate([kv[h // 2][h % 2, rows], e[rows]], axis=1)

    def score(h, i, qa, top):
        block = nt(qa, keys_of(h, i))
        if i in near:
            away = (me ^ (first + i)) - me
            block = block + bands[h, jnp.where(jnp.abs(away) <= 1, away + 1, 3)].astype(f32)
        s[h % 2, :, i * t : (i + 1) * t] = block
        here = block[:, :128]
        for c in range(1, t // 128):
            here = jnp.maximum(here, block[:, c * 128 : (c + 1) * 128])
        return here if top is None else jnp.maximum(top, here)

    def mix(h, i, top, out):
        raised = jnp.exp(s[h % 2, :, i * t : (i + 1) * t] - top).astype(bf16)
        p[h // 2][h % 2, :, i * t : (i + 1) * t] = raised
        more = nn(raised, keys_of(h, i))
        return more if out is None else out + more

    for g in range(pairs):
        for i in range(count):
            project(g, i)
    stats = jnp.zeros((t, 128), f32)
    last = None
    sums = []
    for h in range(2 * pairs + 1):
        qa = query(h) if h < 2 * pairs else None
        top = out = None
        for i in range(count):
            if h < 2 * pairs:
                top = score(h, i, qa, top)
            if h > 0:
                out = mix(h - 1, i, last, out)
        if h > 0:
            stats = jnp.where(lanes == h - 1, last, stats)
            stats = jnp.where(lanes == 7 + h, out[:, 128 + ONES : 129 + ONES], stats)
            sums.append(out[:, :128])
        if h < 2 * pairs:
            last = jnp.max(top, axis=1, keepdims=True)
    for g in range(pairs):
        acc[:, g * 128 : g * 128 + 128] = turn(jnp.where(upper, sums[2 * g], sums[2 * g + 1]))
    stat[...] = stats


def attend(n, first, ids, lens, blocks, gain, wk, wv, q, ext, bands, line):
    count = len(blocks)
    blocks = [piece for block in blocks for piece in block]
    t, d = q.shape[0], wk.shape[0]
    pairs = wk.shape[1] // 128
    c = count * t
    out = call(
        partial(attend_kernel, n, first, count, len(blocks)), "attend", 2 * count,
        [shape(c, d), shape(c, 128), shape(t, wk.shape[1], dtype=f32), shape(t, 128, dtype=f32)]
        + [shape(2, c, 128)] * pairs + [shape(2, t, c)] * pairs,
        (ids, lens), (*blocks, gain, wk, wv, q, ext, bands, line), scratch=[pltpu.VMEM((2, t, c), f32)], much=n > 8,
    )
    return dict(n1=out[0], e=out[1], acc=out[2], stat=out[3], kv=out[4 : 4 + pairs], p=out[4 + pairs :])


def feed_forward_kernel(phases, ids, lens, gain, x, wo, wg, wu, wd, cot, *refs):
    accs, stats = refs[:phases], refs[phases : 2 * phases]
    out, dh, do, scale, gwo, keep, send, gn, grads, mixed_all, n2_all, u_all, gb_all, dg_all, du_all, dh_all = refs[2 * phases :]
    t, d = x.shape
    pairs = wo.shape[0] // 128
    chunk = t // FFN_CHUNKS
    lanes = iota((chunk, 128), 1)
    g2 = gain[...].astype(f32)
    last = lens[0]
    for k in range(1, lens.shape[0]):
        last = last + lens[k]
    work = [dict(rows=slice(c * chunk, (c + 1) * chunk)) for c in range(FFN_CHUNKS)]

    def weigh(v):
        rows = v["rows"]
        tops = [ref[rows] for ref in stats]
        top = tops[0]
        for other in tops[1:]:
            top = jnp.maximum(top, other)
        weights = [jnp.exp(a - top) for a in tops]
        total = jnp.where(lanes < 2 * pairs, 0.0, 1.0)
        for w, ref in zip(weights, stats, strict=True):
            total = total + w * pltpu.roll(ref[rows], 120, 1)
        weights = [jnp.where(lanes < 2 * pairs, w / total, 0.0) for w in weights]
        v["scales"] = weights[0]
        for i, w in enumerate(weights[1:], 1):
            v["scales"] = v["scales"] + pltpu.roll(w, 8 * i, 1)
        v["o"] = []
        for g in range(pairs):
            at = slice(g * 128, g * 128 + 128)
            value = jnp.zeros((chunk, 128), f32)
            for i, w in enumerate(weights):
                value = value + accs[i][rows, at] * jnp.where(lanes < 64, w[:, 2 * g : 2 * g + 1], w[:, 2 * g + 1 : 2 * g + 2])
            v["o"].append(value)
            mixed_all[rows, at] = value.astype(bf16)
        pos = ids[0] * t + rows.start + iota((chunk, 1), 0)
        v["g"] = cot[rows].astype(f32) * (pos < last).astype(f32)
        gb_all[rows] = v["g"].astype(bf16)
        v["du"] = nt(gb_all[rows], wd[...]).astype(bf16).astype(f32)

    def norm(v):
        rows = v["rows"]
        v["h1"] = x[rows].astype(f32) + nn(mixed_all[rows], wo[...])
        v["s2"] = lax.rsqrt(jnp.mean(v["h1"] * v["h1"], axis=-1, keepdims=True) + EPS)
        v["hat"] = v["h1"] * v["s2"]
        n2_all[rows] = (v["hat"] * g2).astype(bf16)

    def project(v):
        rows = v["rows"]
        v["gate"], v["up"] = nn(n2_all[rows], wg[...]), nn(n2_all[rows], wu[...])

    def activate(v):
        rows, gate, up = v["rows"], v["gate"], v["up"]
        c0 = 0.7978845608028654
        square = gate * gate
        th = jnp.tanh(c0 * gate * (1.0 + 0.044715 * square))
        half = 0.5 * (1.0 + th)
        act = gate * half
        dact = half + 0.5 * gate * (1.0 - th * th) * (c0 * (1.0 + 3 * 0.044715 * square))
        u_all[rows] = (act * up).astype(bf16)
        dg_all[rows] = (v["du"] * up * dact).astype(bf16)
        du_all[rows] = (v["du"] * act).astype(bf16)

    def down(v):
        rows = v["rows"]
        v["dn2"] = nt(dg_all[rows], wg[...]) + nt(du_all[rows], wu[...])

    def norm_back(v):
        rows, dn2, hat, s2 = v["rows"], v["dn2"], v["hat"], v["s2"]
        out[rows] = (v["h1"] + nn(u_all[rows], wd[...])).astype(bf16)
        v["gn"] = jnp.sum(dn2 * hat, axis=0, keepdims=True)
        scaled = dn2 * g2
        dh1 = v["g"] + s2 * (scaled - hat * jnp.mean(hat * scaled, axis=-1, keepdims=True))
        dh[rows] = dh1
        dh_all[rows] = dh1.astype(bf16)

    def mix_back(v):
        rows = v["rows"]
        dmix = nt(dh_all[rows], wo[...]).astype(bf16)
        do[rows] = dmix
        scales = v["scales"]
        for h in range(2 * pairs):
            at = slice(h // 2 * 128, h // 2 * 128 + 128)
            product = dmix[:, at].astype(f32) * v["o"][h // 2]
            own = jnp.where((lanes < 64) == (h % 2 == 0), product, 0.0)
            scales = jnp.where(lanes == 64 + h, jnp.sum(own, axis=1, keepdims=True), scales)
        scale[rows] = scales

    def weights_kernel():
        low = tn(u_all[...], gb_all[...]).astype(bf16)
        for k, value in enumerate((tn(n2_all[...], dg_all[...]).astype(bf16), tn(n2_all[...], du_all[...]).astype(bf16))):
            for i in range(d // PIECE):
                grads[(3 * i + k) * PIECE : (3 * i + k + 1) * PIECE] = value[i * PIECE : (i + 1) * PIECE]
        for i in range(d // PIECE):
            at = slice((3 * i + 2) * PIECE, (3 * i + 3) * PIECE)
            grads[at, :d] = low[i * PIECE : (i + 1) * PIECE]
            grads[at, d:] = low[d + i * PIECE : d + (i + 1) * PIECE]

    stages = [weigh, norm, project, activate, down, norm_back, mix_back]
    for step in range(len(stages) + FFN_CHUNKS - 1):
        for c, v in enumerate(work):
            if 0 <= step - c < len(stages):
                stages[step - c](v)
        if step == len(stages) + FFN_CHUNKS - 2:
            weights_kernel()
    gn[...] = sum(v["gn"] for v in work)
    gwo[...] = tn(mixed_all[...], dh_all[...]).astype(bf16)
    rows = keep.shape[0]
    keep[...] = grads[pl.ds(pl.multiple_of(ids[1] * rows, 16), rows)]
    send[...] = grads[pl.ds(pl.multiple_of((1 - ids[1]) * rows, 16), rows)]


def feed_forward(ids, lens, gain, x, wo, wg, wu, wd, cot, parts):
    t, d = x.shape
    ff, w = wg.shape[1], wo.shape[0]
    half = 3 * d // 2
    return call(
        partial(feed_forward_kernel, len(parts)), "feed_forward", 8,
        [shape(t, d), shape(t, d, dtype=f32), shape(t, w), shape(t, 128, dtype=f32), shape(w, d),
         shape(half, ff), shape(half, ff), shape(1, d, dtype=f32)],
        (ids, lens), (gain, x, wo, wg, wu, wd, cot, *[v["acc"] for v in parts], *[v["stat"] for v in parts]),
        scratch=[pltpu.VMEM((3 * d, ff), bf16)]
        + [pltpu.VMEM((t, k), bf16) for k in (w, d, ff, d, ff, ff, d)],
    )


def attend_back_kernel(n, pairs, counts, ids, q, do, scale, *refs):
    phases, size = len(counts), len(pairs)
    p = [refs[i * size : (i + 1) * size] for i in range(phases)]
    refs = refs[phases * size :]
    kv = [refs[i * size : (i + 1) * size] for i in range(phases)]
    e, refs = refs[phases * size : phases * size + phases], refs[phases * size + phases :]
    dk, dv, refs = refs[:size], refs[size : 2 * size], refs[2 * size :]
    dq, line, ds = refs
    me = ids[0]
    t = q.shape[0]
    lower = low_half(t)
    back = (iota((t, t), 0) + iota((t, t), 1) == t - 1).astype(f32).astype(bf16)
    lane = iota((1, 128), 1)
    line[...] = jnp.zeros_like(line)
    slots = [(i, j) for i, count in enumerate(counts) for j in range(count)]

    def operands(k):
        h = 2 * pairs[k // 2] + k % 2
        at = slice(h // 2 * 128, h // 2 * 128 + 128)
        qt = jnp.where(lower == (k % 2 == 0), q[:, at].astype(f32), 0.0).T
        doh = jnp.where(lower == (k % 2 == 1), turn(do[:, at].astype(f32)), 0.0)
        out = []
        for i in range(phases):
            factor = scale[:, 8 * i + h : 8 * i + h + 1]
            scaled = doh * factor
            shift = scale[:, 64 + h : 65 + h] * factor
            out.append((scaled.astype(bf16), shift, jnp.concatenate([qt, scaled.T], axis=1).astype(bf16)))
        return out

    def start(k, s, ops):
        i, j = slots[s]
        return nt(ops[i][0], kv[i][k // 2][k % 2, j * t : (j + 1) * t])

    def finish(k, s, ops, d_prob, acc):
        i, j = slots[s]
        rows = slice(j * t, (j + 1) * t)
        probs = p[i][k // 2][k % 2, :, rows]
        d_score = (probs.astype(f32) * (d_prob - ops[i][1])).astype(bf16)
        ds[k % 2, :, s * t : (s + 1) * t] = d_score
        more = nn(d_score, jnp.concatenate([kv[i][k // 2][k % 2, rows], e[i][rows]], axis=1))
        both = nn(ops[i][2], jnp.concatenate([d_score, probs], axis=0)).astype(bf16)
        mine, other = (both[:64], both[64:]) if k % 2 == 0 else (both[64:], both[:64])
        dk[k // 2][k % 2 * 64 : k % 2 * 64 + 64, s * t : (s + 1) * t] = mine
        dv[k // 2][k % 2 * 64 : k % 2 * 64 + 64, s * t : (s + 1) * t] = other
        return more if acc is None else acc + more

    def bias(k, acc):
        parts = []
        for r in (-1, 0, 1):
            there = me + r
            inside = (there >= 0) & (there < n)
            slot = jnp.where(inside, me ^ there, 0)
            block = ds[k % 2, :, pl.ds(pl.multiple_of(slot * t, t), t)]
            parts.append(nn(back, block) * inside.astype(f32))
        parts.append(jnp.zeros((t, t), f32))
        band = pltpu.roll(jnp.concatenate(parts, axis=1), 0, 1, stride=1, stride_axis=0)
        line[k : k + 1, : 4 * t] = jnp.sum(band, axis=0, keepdims=True)
        ends = jnp.sum(acc[:, 128:], axis=0, keepdims=True)
        line[k : k + 1, 4 * t :] = jnp.where((lane == LEFT) | (lane == RIGHT), ends, 0.0)

    tasks = [(k, s) for k in range(2 * size) for s in range(len(slots))]
    ops = [operands(0)]
    d_prob = start(0, 0, ops[0])
    accs = [None] * (2 * size)
    for index, (k, s) in enumerate(tasks):
        if s == 0 and k + 1 < 2 * size:
            ops.append(operands(k + 1))
        later = None
        if index + 1 < len(tasks):
            k2, s2 = tasks[index + 1]
            later = start(k2, s2, ops[k2])
        accs[k] = finish(k, s, ops[k], d_prob, accs[k])
        d_prob = later
        if s == 3 and k > 0:
            bias(k - 1, accs[k - 1])
    bias(2 * size - 1, accs[2 * size - 1])
    for g in range(size):
        dq[:, g * 128 : g * 128 + 128] = jnp.where(lower, accs[2 * g][:, :128], accs[2 * g + 1][:, :128]).astype(bf16)


def attend_back(n, pairs, ids, q, do, scale, parts):
    t = q.shape[0]
    widths = [v["e"].shape[0] for v in parts]
    s = sum(widths)
    size = len(pairs)
    out = call(
        partial(attend_back_kernel, n, pairs, [w // t for w in widths]), "attend_back", 4 * size,
        [shape(128, s)] * (2 * size) + [shape(t, 128 * size), shape(8, 4 * t + 128, dtype=f32)],
        (ids,), (q, do, scale, *[v["p"][g] for v in parts for g in pairs],
                 *[v["kv"][g] for v in parts for g in pairs], *[v["e"] for v in parts]),
        scratch=[pltpu.VMEM((2, t, s), bf16)], much=n > 8,
    )
    return dict(dk=out[:size], dv=out[size : 2 * size], dq=out[-2], line=out[-1], pairs=size)


def gather_back_kernel(n, buckets, counts, pairs, ids, gain, gn, gwo, wq, wk, wv, wt, *refs):
    phases = len(counts)
    n1, refs = refs[:phases], refs[phases:]
    total_pairs = sum(pairs)
    dkv, refs = refs[: 2 * total_pairs], refs[2 * total_pairs :]
    dq, lines = refs[: len(pairs)], refs[len(pairs) : 2 * len(pairs)]
    even, odd, dn1q, keep, send, grads, sums, diagonal = refs[2 * len(pairs) :]
    d, w = wq.shape
    t = dn1q.shape[0]
    weights = jnp.concatenate([wk[...], wv[...]], axis=1)
    total = jnp.zeros((2 * w, d), f32)
    slot = 0
    for i, count in enumerate(counts):
        begin = sum(counts[:i]) * t
        both = jnp.concatenate([ref[:, begin : begin + count * t] for ref in dkv], axis=0)
        total = total + nn(both, n1[i][...])
        back = nn(weights, both).astype(bf16)
        for _ in range(count):
            ref = odd if slot % 2 else even
            ref[slot // 2] = back[:, slot * t - begin : slot * t - begin + t]
            slot += 1
    dq_all = jnp.concatenate([ref[...] for ref in dq], axis=1)
    from_q = tn(dq_all, n1[0][:t])
    dn1q[...] = nt(dq_all, wq[...])
    grads[:w] = from_q.astype(bf16)
    grads[w : 3 * w] = total.astype(bf16)
    grads[3 * w :] = gwo[...]
    gains = jnp.sum(from_q * wt[:w].astype(f32), axis=0, keepdims=True)
    gains = gains + jnp.sum(total * wt[w:].astype(f32), axis=0, keepdims=True)
    sums[...] = jnp.zeros_like(sums)
    sums[0:1] = gains / gain[...].astype(f32)
    sums[1:2] = gn[...]
    diagonal[...] = jnp.zeros_like(diagonal)
    begin = 0
    for ref, count in zip(lines, pairs, strict=True):
        diagonal[begin : begin + 2 * count] = ref[: 2 * count]
        begin += 2 * count
    width = diagonal.shape[1]
    u = iota((width, 128), 0)
    bucket = bucket_of(u - (2 * t - 1), buckets)
    bucket = jnp.where(u == 4 * t + LEFT, buckets // 2 - 1, jnp.where(u == 4 * t + RIGHT, buckets - 1, bucket))
    pick = (bucket == iota((width, 128), 1)).astype(f32)
    sums[8:16, :128] = lax.dot_general(diagonal[...], pick, (((1,), (0,)), ((), ())),
                                       precision=lax.Precision.HIGHEST, preferred_element_type=f32)
    small = sums[...].astype(bf16)
    rows = 2 * w
    keep[:rows] = grads[pl.ds(pl.multiple_of(ids[1] * rows, 16), rows)]
    send[:rows] = grads[pl.ds(pl.multiple_of((1 - ids[1]) * rows, 16), rows)]
    keep[rows:] = small
    send[rows:] = small


def gather_back(n, buckets, ids, gain, gn, gwo, wq, wk, wv, wt, parts, backs):
    d, w = wq.shape
    t = backs[0]["dq"].shape[0]
    pairs = [v["pairs"] for v in backs]
    counts = [v["e"].shape[0] // t for v in parts]
    pieces = [ref for v in backs for ref in v["dk"]] + [ref for v in backs for ref in v["dv"]]
    half = 2 * w + SMALL
    return call(
        partial(gather_back_kernel, n, buckets, counts, pairs), "gather_back", 6,
        [shape(n // 2, d, t), shape(n // 2, d, t), shape(t, d, dtype=f32), shape(half, d), shape(half, d)],
        (ids,), (gain, gn, gwo, wq, wk, wv, wt, *[v["n1"] for v in parts], *pieces, *[v["dq"] for v in backs],
                 *[v["line"] for v in backs]),
        scratch=[pltpu.VMEM((4 * w, d), bf16), pltpu.VMEM((SMALL, d), f32), pltpu.VMEM((8, 4 * t + 128), f32)], much=n > 8,
    )


def rest_back_kernel(n, buckets, pairs, counts, sizes, ids, *refs):
    first, second, outs, inner = (refs[a:b] for a, b in zip(sizes[:-1], sizes[1:], strict=True))
    size = len(pairs)
    dkv, (dq, line), ds = inner[: 2 * size], inner[2 * size : 2 * size + 2], inner[2 * size + 2]
    attend_back_kernel(n, pairs, counts, ids, *first, *dkv, dq, line, ds)
    head, (dk0, dv0, dq0, line0) = second[: 7 + len(counts)], second[7 + len(counts) :]
    gather_back_kernel(n, buckets, counts, [1, size], ids, *head, dk0, *dkv[:size], dv0, *dkv[size:], dq0, dq, line0, line,
                       *outs, *inner[2 * size + 3 :])


def rest_back(n, buckets, pairs, ids, q, do, scale, gain, gn, gwo, wq, wk, wv, wt, parts, back):
    d, w = wq.shape
    t = q.shape[0]
    widths = [v["e"].shape[0] for v in parts]
    s, size, half = sum(widths), len(pairs), 2 * w + SMALL
    first = (q, do, scale, *[v["p"][g] for v in parts for g in pairs], *[v["kv"][g] for v in parts for g in pairs],
             *[v["e"] for v in parts])
    second = (gain, gn, gwo, wq, wk, wv, wt, *[v["n1"] for v in parts], back["dk"][0], back["dv"][0], back["dq"], back["line"])
    cuts = [0, len(first), len(first) + len(second), len(first) + len(second) + 5]
    inner = [pltpu.VMEM((128, s), bf16)] * (2 * size) + [pltpu.VMEM((t, 128 * size), bf16), pltpu.VMEM((8, 4 * t + 128), f32),
             pltpu.VMEM((2, t, s), bf16), pltpu.VMEM((4 * w, d), bf16), pltpu.VMEM((SMALL, d), f32),
             pltpu.VMEM((8, 4 * t + 128), f32)]
    return call(
        partial(rest_back_kernel, n, buckets, pairs, [v // t for v in widths], [*cuts, cuts[-1] + len(inner)]), "rest_back", 10,
        [shape(n // 2, d, t), shape(n // 2, d, t), shape(t, d, dtype=f32), shape(half, d), shape(half, d)],
        (ids,), (*first, *second), scratch=inner,
    )


def add_all(refs, at):
    if len(refs) == 2:
        return refs[0][at] + refs[1][at]
    return sum(ref[at].astype(f32) for ref in refs).astype(bf16)


def split_kernel(which, count, extra, ids, *refs):
    inputs, outs = refs[:-count], refs[-count:]
    rows = (inputs[0].shape[0] - extra) // count
    own = ids[which]
    for j in range(count):
        at = pl.ds(pl.multiple_of((own ^ j) * rows, 16), rows)
        total = add_all(inputs, at)
        outs[j][:rows] = total
    if extra:
        at = pl.ds(rows * count, extra)
        total = add_all(inputs, at)
        for j in range(count):
            outs[j][rows:] = total


def add_and_split(which, count, extra, ids, *arrays):
    rows = (arrays[0].shape[0] - extra) // count + extra
    out = shape(rows, arrays[0].shape[1])
    return call(partial(split_kernel, which, count, extra), "add_parts", 1, [out] * count, (ids,), arrays)


def by_chip_kernel(ids, keep, recv, *outs):
    rows = keep.shape[0] // 4
    for half, own in ((0, ids[2] % 2), (1, ids[2] // 2)):
        for j in range(2):
            at = pl.ds(pl.multiple_of((2 * half + (own ^ j)) * rows, 16), rows)
            outs[2 * half + j][...] = keep[at] + recv[at]


def by_next_chip_kernel(ids, keep_x, recv_x, keep_y, recv_y, *outs):
    rows = keep_x.shape[0] // 2
    for half, own, a, b in ((0, ids[2] // 2, keep_x, recv_x), (1, ids[2] % 2, keep_y, recv_y)):
        for j in range(2):
            at = pl.ds(pl.multiple_of((own ^ j) * rows, 16), rows)
            outs[2 * half + j][...] = a[at] + b[at]


def by_row_kernel(ids, keep_x, recv_x, keep_y, recv_y, mine, other):
    for parity, first, second in ((0, mine, other), (1, other, mine)):

        @pl.when(ids[3] % 2 == parity)
        def _(first=first, second=second):
            first[...] = keep_x[...] + recv_x[...]
            second[...] = keep_y[...] + recv_y[...]


def pick_kernel(ids, mine, other, first, second):
    for parity, a, b in ((0, mine, other), (1, other, mine)):

        @pl.when(ids[3] % 2 == parity)
        def _(a=a, b=b):
            first[...] = a[...]
            second[...] = b[...]


def stack_kernel(ids, *refs):
    *parts, out = refs
    rows = parts[0].shape[0]
    for i, ref in enumerate(parts):
        out[i * rows : (i + 1) * rows] = ref[...]


def join_kernel(ids, a, b, c, d, first, second):
    rows = a.shape[0]
    first[:rows], first[rows:] = a[...], b[...]
    second[:rows], second[rows:] = c[...], d[...]


def swap(array, axis, j):
    size = lax.axis_size(axis)
    return lax.ppermute(array, axis, [(i, i ^ j) for i in range(size)])


def order(first, *values):
    first, values = lax.optimization_barrier((first, values))
    return values if len(values) > 1 else values[0]


def sum_all(ids, keep, recv, extra):
    both = add_and_split(0, 1, extra, ids * 0, keep, recv)[0].astype(f32)
    size = both.shape[0] - extra
    placed = jnp.zeros((2 * size, both.shape[1]), f32)
    placed = lax.dynamic_update_slice_in_dim(placed, both[:size], ids[1] * size, 0)
    full, tail = lax.psum((placed, both[size:] * 0.5), ("rows", "seq"))
    mine = lax.dynamic_slice_in_dim(full, ids[1] * size, size, 0)
    other = lax.dynamic_slice_in_dim(full, (1 - ids[1]) * size, size, 0)
    return [mine.astype(bf16)], [other.astype(bf16)], tail.astype(bf16)


def to_chips(parts):
    return [parts[0]] + [swap(parts[j], "seq", 2 * j) for j in range(1, len(parts))]


def place_halves(ids, mine, other, full):
    size = full.shape[0] // 2
    if len(mine) == 1:
        full[pl.ds(pl.multiple_of(ids[1] * size, 16), size)] = mine[0][...]
        full[pl.ds(pl.multiple_of((1 - ids[1]) * size, 16), size)] = other[0][...]
        return
    piece = size // len(mine)
    for c, refs in ((ids[1], mine), (1 - ids[1], other)):
        for a, ref in enumerate(refs):
            at = c * size + (ids[2] ^ a) * piece
            for b in range(2):
                where = at + ((ids[3] % 2) ^ b) * (piece // 2)
                full[pl.ds(pl.multiple_of(where, 16), piece // 2)] = ref[b * (piece // 2) : (b + 1) * (piece // 2)]


def send_out(copies, source, target, sem):
    copies.append(pltpu.make_async_copy(source, target, sem))
    copies[-1].start()


def write_ffn(far, ids, parts, gate, up, down, full, sems):
    d = gate.shape[0]
    x, y = ids[2] % 2, ids[2] // 2
    rows = 3 * PIECE
    copies = []
    for c, *pair in parts:
        for half, first, second in ((0, x, y), (1, y, x)):
            for b in range(2):
                k = len(copies) // 4
                piece = 8 * c + 4 * half + 2 * (first ^ far) + (second ^ b)
                full[k] = pair[half][b * rows : (b + 1) * rows].astype(f32)
                at = pl.multiple_of(piece * PIECE, PIECE)
                send_out(copies, full.at[k, :PIECE], gate.at[pl.ds(at, PIECE)], sems.at[4 * k])
                send_out(copies, full.at[k, PIECE : 2 * PIECE], up.at[pl.ds(at, PIECE)], sems.at[4 * k + 1])
                send_out(copies, full.at[k, 2 * PIECE :, :d], down.at[pl.ds(at, PIECE)], sems.at[4 * k + 2])
                send_out(copies, full.at[k, 2 * PIECE :, d:], down.at[pl.ds(d + at, PIECE)], sems.at[4 * k + 3])
    return copies


def unpack_near_kernel(ids, *refs):
    for copy in write_ffn(0, ids, ((ids[1], *refs[:2]), (1 - ids[1], *refs[2:4])), *refs[4:]):
        copy.wait()


def unpack_half_kernel(other, filled, chips, ids, *refs):
    (x, y, *stacks), refs = refs[:4], refs[4 + filled :]
    gate, up, down, gq, gk, gv, go, full, sems, both, wide, tall, sem2 = refs
    core = ids[1] ^ other
    copies = write_ffn(1, ids, ((core, x, y),), gate, up, down, full, sems)
    rows = stacks[0].shape[0] // chips
    for k, stack in enumerate(stacks):
        for a in range(chips):
            where = ((ids[2] ^ a) * 2 + ((ids[3] % 2) ^ k)) * rows
            both[pl.ds(pl.multiple_of(where, 16), rows)] = stack[a * rows : (a + 1) * rows]
    w = wide.shape[2]

    def finish(matrices):
        moves = []
        for i, (ref, turned) in enumerate(matrices):
            value = both[i * w : (i + 1) * w].astype(f32)
            source = wide.at[i] if turned else tall
            source[...] = value.T if turned else value
            send_out(moves, source, ref, sem2.at[i])
        for copy in moves:
            copy.wait()

    @pl.when(core == 0)
    def _():
        finish(((gq, True), (gk, True)))

    @pl.when(core == 1)
    def _():
        finish(((gv, True), (go, False)))

    for copy in copies:
        copy.wait()


def unpack(kernel, ids, vmem_args, filled, out_shape, scratch):
    vmem, hbm = pl.BlockSpec(memory_space=pltpu.VMEM), pl.BlockSpec(memory_space=pl.ANY)
    return pl.pallas_call(
        kernel,
        in_specs=[pl.BlockSpec(memory_space=pltpu.SMEM)] + [vmem] * len(vmem_args) + [hbm] * len(filled),
        out_specs=[hbm] * len(out_shape),
        out_shape=out_shape,
        scratch_shapes=scratch,
        input_output_aliases={1 + len(vmem_args) + i: i for i in range(len(filled))},
        compiler_params=pltpu.CompilerParams(vmem_limit_bytes=VMEM),
        cost_estimate=pl.CostEstimate(flops=1000, bytes_accessed=1000, transcendentals=0),
        name="unpack",
    )(ids, *vmem_args, *filled)


def unpack_ffn_halves(ids, mine, other, d, ff):
    full = jnp.where(ids[1] == 0, jnp.concatenate([mine, other]), jnp.concatenate([other, mine])).astype(f32)
    full = full.reshape(d // PIECE, 3, PIECE, ff)
    low = full[:, 2].reshape(d, ff)
    return full[:, 0].reshape(d, ff), full[:, 1].reshape(d, ff), jnp.concatenate([low[:, :d], low[:, d:]])


def unpack_attention_kernel(pieces, ids, *refs):
    gq, gk, gv, go, full = refs[2 * pieces :]
    place_halves(ids, refs[:pieces], refs[pieces : 2 * pieces], full)
    w = gq.shape[1]
    for k, ref in enumerate((gq, gk, gv)):
        ref[...] = full[k * w : (k + 1) * w].astype(f32).T
    go[...] = full[3 * w :].astype(f32)


def unpack_small_kernel(ids, tail, g1, g2, gb):
    small = tail[...].astype(f32)
    g1[...] = small[0:1]
    g2[...] = small[1:2]
    gb[...] = small[8 : 8 + gb.shape[0], : gb.shape[1]]


def input_grad_kernel(ids, *refs):
    *parts, dn1q, x, dh, gain, out = refs
    total = parts[0][...].astype(f32)
    for ref in parts[1:]:
        total = total + ref[...].astype(f32)
    dn1 = total.T + dn1q[...]
    value = x[...].astype(f32)
    s1 = lax.rsqrt(jnp.mean(value * value, axis=-1, keepdims=True) + EPS)
    hat = value * s1
    scaled = dn1 * gain[...].astype(f32)
    out[...] = dh[...] + s1 * (scaled - hat * jnp.mean(hat * scaled, axis=-1, keepdims=True))


def slots_kernel(count, ids, mine, other, *outs):
    for j in range(count):
        outs[j][...] = (mine[j].astype(f32) + other[j].astype(f32)).astype(bf16)


def shards(
    tokens, norm_attn, query_weight, key_weight, value_weight, out_weight, bucket_bias_table, norm_ffn,
    gate_weight, expansion_matrix, down_weight, lengths, cotangent,
):
    _, t, d = tokens.shape
    n = lax.axis_size("seq")
    buckets, heads = bucket_bias_table.shape
    width = query_weight.shape[1]
    ff = gate_weight.shape[1]
    seq = lax.axis_index("seq")
    ids = jnp.stack([seq, seq % 2, seq // 2, lax.axis_index("rows")]).astype(i32)
    x = tokens.reshape(t, d)
    cot = cotangent.reshape(t, d)
    lens = lengths.reshape(-1)
    gain1 = norm_attn.reshape(1, d)
    gain2 = norm_ffn.reshape(1, d)

    blocks = [[x], [swap(x, "seq", 1)]] + [None] * (n - 2)
    for j in range(2, n, 2):
        if n != 8 or j != 6:
            blocks[j] = [swap(x, "seq", j)]
    q, ext, bands, wt, line, x, wq, wk, wv = prepare(
        ids, lens, x, gain1, bucket_bias_table.T, query_weight, key_weight, value_weight
    )
    blocks[0] = [x]
    cuts = [0, 2, 6, *range(8, n, 8), n]

    def phase(a, b):
        return attend(n, a, ids, lens, blocks[a:b], gain1, wk, wv, q, ext, bands, line)

    parts = []
    for a, b in zip(cuts[:-1], cuts[1:], strict=True):
        for j in range(a, b, 2):
            if j:
                blocks[j] = [order(parts[-1]["acc"], v) for v in blocks[j]]
                blocks[j + 1] = [swap(v, "seq", 1) for v in blocks[j]]
        if n == 8 and a == 2:
            blocks[6] = [swap(blocks[4][0][: t // 2], "seq", 2), swap(blocks[2][0][t // 2 :], "seq", 4)]
        parts.append(phase(a, b))
    output, dh, do, scale, gwo, keep, send, gn = feed_forward(
        ids, lens, gain2, x, out_weight, gate_weight, expansion_matrix, down_weight, cot, parts
    )
    half = n // 2
    pairs = width // 128
    whole = n != 8 or lax.axis_size("rows") != 4
    zero, near = ids * 0, ids[3:4] % 2

    def unpack_attention(mine, other):
        return call(
            partial(unpack_attention_kernel, len(mine)), "unpack_attention", 3,
            [shape(d, width, dtype=f32)] * 3 + [shape(width, d, dtype=f32)],
            (ids,), (*mine, *other), scratch=[pltpu.VMEM((4 * width, d), bf16)],
        )

    def unpack_small(tail):
        return call(unpack_small_kernel, "unpack_small", 1,
                    [shape(1, d, dtype=f32)] * 2 + [shape(heads, buckets, dtype=f32)], (ids,), (tail,))

    def input_grad(slots):
        return call(input_grad_kernel, "input_grad", 2, shape(t, d, dtype=f32), (ids,), (*slots, dn1q, x, dh, gain1))

    def add_slots(recv):
        return call(partial(slots_kernel, half), "add_slots", 1, [shape(d, t)] * half, (ids,), (even, recv))

    f_core = swap(send, "seq", 1)
    back = attend_back(n, [0], ids, q, do, scale, parts)
    f_keep = keep
    if whole:
        backs = [back, attend_back(n, list(range(1, pairs)), ids, q, do, scale, parts)]
        even, odd, dn1q, keep, send = gather_back(n, buckets, ids, gain1, gn, gwo, wq, wk, wv, wt, parts, backs)
        a_core, d_core = swap(send, "seq", 1), swap(odd, "seq", 1)
        mine, other, _ = sum_all(ids, f_keep, f_core, 0)
        gate, up, down = unpack_ffn_halves(ids, mine[0], other[0], d, ff)
        grad_tokens = input_grad(to_chips(add_slots(d_core)))
        mine, other, tail = sum_all(ids, keep, a_core, SMALL)
        gq, gk, gv, go = unpack_attention(mine, other)
        g1, g2, gb = unpack_small(tail)
    else:
        part = lambda rows: shape(f_keep.shape[0] // rows, ff)
        f_core = order(back["dq"], f_core)
        f_x, f_x2, f_y, f_y2 = call(by_chip_kernel, "add_parts", 1, [part(4)] * 4, (ids,), (keep, f_core))
        do = order(f_x, do)
        f_x2, f_y2 = swap(f_x2, "seq", 2), swap(f_y2, "seq", 4)
        even, odd, dn1q, keep, send = rest_back(
            n, buckets, list(range(1, pairs)), ids, q, do, scale, gain1, gn, gwo, wq, wk, wv, wt, parts, back
        )
        send, odd = order((f_x2, f_y2), send, odd)
        live = dict(a=swap(send, "seq", 1), d=swap(odd, "seq", 1))
        f_x, f_x2, f_y, f_y2 = call(
            by_next_chip_kernel, "add_parts", 1, [part(8)] * 4, (ids,), (f_x, f_x2, f_y, f_y2)
        )
        live["f"] = [swap(f_x2, "seq", 4), swap(f_y2, "seq", 2)]
        size = (keep.shape[0] - SMALL) // 8
        ffn_out = [shape(d, ff, dtype=f32), shape(d, ff, dtype=f32), shape(ff, d, dtype=f32)]
        ffn_scratch = [pltpu.VMEM((8, 3 * PIECE, ff), f32), pltpu.SemaphoreType.DMA((32,))]
        kept = dict(f=(f_x, f_y))

        def f_rows():
            (f_x, f_y), (f_x2, f_y2) = kept["f"], live["f"]
            mine, other = call(by_row_kernel, "add_parts", 1, [part(8)] * 2, (ids,), (f_x, f_x2, f_y, f_y2))
            kept["f"], live["f"] = mine, swap(other, "rows", 1)
            return mine

        def f_add(j):
            mine = add_and_split(0, 1, 0, zero, kept["f"], live["f"])[0]
            kept["f"], live["f"] = mine, swap(mine, "rows", j)
            return mine

        def f_pick():
            x, y = call(pick_kernel, "pick", 1, [part(8)] * 2, (ids,), (kept["f"], live["f"]))
            kept["f"], live["f"] = (x, y), [swap(x, "seq", 4), swap(y, "seq", 2)]
            return x

        def f_join():
            (x, y), (x2, y2) = kept["f"], live["f"]
            x, y = call(join_kernel, "join", 1, [part(4)] * 2, (ids,), (x, x2, y, y2))
            kept["f"], live["f"] = (x, y), [swap(x, "seq", 2), swap(y, "seq", 4)]
            live["near"] = [swap(v, "seq", 1) for v in (x, y)]
            return x

        def f_near():
            kept["near"] = unpack(unpack_near_kernel, ids, (*kept["f"], *live["near"]), (), ffn_out, ffn_scratch)
            return kept["near"][0]

        def f_swap():
            live["far"] = [swap(v, "seq", 1) for v in live["f"]]
            return None

        def a_chips():
            kept["a"] = add_and_split(2, half, SMALL, ids, keep, live["a"])
            live["a"] = to_chips(kept["a"])
            return kept["a"][0]

        def a_rows():
            kept["a"], other = add_and_split(0, 2, SMALL, near, *live["a"])
            live["a"] = swap(other, "rows", 1)
            return kept["a"]

        def a_add(j):
            kept["a"] = add_and_split(0, 1, SMALL, zero, kept["a"], live["a"])[0]
            live["a"] = swap(kept["a"], "rows", 2) if j == 2 else to_chips([kept["a"][:size]] * half)
            return kept["a"]

        def a_stack():
            kept["stack"] = call(stack_kernel, "stack", 1, shape(half * size, d), (ids,), live["a"])
            live["a"] = swap(kept["stack"], "rows", 1)
            live["anear"] = swap(kept["stack"], "seq", 1)
            return kept["stack"]

        def a_swap():
            live["afar"] = swap(live["a"], "seq", 1)
            return None

        def unpack_half(other, x, y, first, second, filled):
            return unpack(
                partial(unpack_half_kernel, other, len(filled), half), ids, (x, y, first, second), filled,
                ffn_out + [shape(d, width, dtype=f32)] * 3 + [shape(width, d, dtype=f32)],
                [*ffn_scratch, pltpu.VMEM((2 * width, d), bf16), pltpu.VMEM((2, d, width), f32),
                 pltpu.VMEM((width, d), f32), pltpu.SemaphoreType.DMA((2,))],
            )

        def own():
            kept["near"] = unpack_half(0, *live["f"], kept["stack"], live["a"], kept["near"])
            return kept["near"][0]

        def last():
            kept["out"] = unpack_half(1, *live["far"], live["anear"], live["afar"], kept["near"])
            return kept["out"][0]

        def d_slots():
            kept["d"] = add_slots(live["d"])
            live["d"] = to_chips(kept["d"])
            return kept["d"][0]

        def d_out():
            kept["tokens"] = input_grad(live["d"])
            return kept["tokens"]

        def small():
            kept["small"] = unpack_small(kept["a"][size:])
            return kept["small"][0]

        steps = dict(
            f_rows=(f_rows, "f"), f_z0=(partial(f_add, 2), "f"), f_z1=(partial(f_add, 1), "f"), f_pick=(f_pick, "f"),
            f_join=(f_join, "f"), f_near=(f_near, "near"), f_swap=(f_swap, "f"), own=(own, "f"), last=(last, "far"),
            a_chips=(a_chips, "a"), a_rows=(a_rows, "a"), a_z0=(partial(a_add, 2), "a"), a_z1=(partial(a_add, 1), "a"),
            a_stack=(a_stack, "a"), a_swap=(a_swap, "a"),
            d_slots=(d_slots, "d"), d_out=(d_out, "d"), small=(small, None),
        )
        token = f_x
        for name in STEPS:
            if ":" in name:
                stream, j = name.split(":")
                live[stream][int(j)] = token = order(token, live[stream][int(j)])
                continue
            step, stream = steps[name]
            if stream is not None:
                live[stream] = order(token, live[stream])
            elif name == "small":
                kept["a"] = order(token, kept["a"])
            done = step()
            token = live[stream] if done is None else done
        gate, up, down, gq, gk, gv, go = kept["out"]
        g1, g2, gb = kept["small"]
        grad_tokens = kept["tokens"]
    return (
        output.reshape(tokens.shape), grad_tokens.reshape(tokens.shape), g1.reshape(d), gq, gk, gv, go, gb.T,
        g2.reshape(d), gate, up, down,
    )


def solution(mesh):
    split = P("rows", "seq", None)
    in_specs = (split,) + (P(),) * 10 + (P("rows", None), split)
    out_specs = (split, split) + (P(),) * 10
    return jax.shard_map(shards, mesh=mesh, in_specs=in_specs, out_specs=out_specs, check_vma=False)
```
